128 devices in a mesh: fsdp: 16 (over x, y), emb: 8 (over z, core).
Axes of the slice: x: 4, y: 4, z: 4, core: 2. Of those that a mesh axis runs over, the one named last changes fastest.
Arguments:
- pooled: bfloat16 [16384, 49152], P(('fsdp', 'emb')), may hold values from -6 to 6
- projection: bfloat16 [256, 96], replicated, may hold values from -0.375 to 0.375
- out_weight: bfloat16 [24576, 128], P('fsdp'), may hold values from -0.0390625 to 0.0390625
- cotangent: bfloat16 [16384, 128], P(('fsdp', 'emb')), may hold values from -6 to 6
- segments: int32 [16384, 256], P(None, ('fsdp', 'emb')), may hold values from 0 to 1023, as said below
Outputs:
- weight_grad: float32 [24576, 128], P(('fsdp', 'emb'))
- proj_grad: float32 [256, 96], replicated
- row_grad: float32 [131072, 192], P(('fsdp', 'emb'))
The draws below stay inside these ranges and needn't reach their ends.
Inputs may be any that keep to these rules, and one draw needn't show every extreme that they name: `segments`: all features of one owner share that owner's count of distinct rows; every value of the owner lies below it, and the owner's largest value is that count minus one. Counts lie between 256 and 1024, and some owner's count is 1024.
All inputs are finite; a program needn't handle non-finite values.
Results may differ from the reference program's by a relative error of at most 0.008.
Values may be sent and summed in bfloat16 or wider, within the bound.
A program may use at most 192 MiB of HBM per device.

```python
import math
import jax
import jax.numpy as jnp
from jax import lax

F = 256
E = 192
K = 96
H = 128
UNIQUE_CAP = 1024
B_ALL = 16384
FPO = 2
DEVICES = 128


def draw_segments(key, part):
    key = jax.random.fold_in(key, 7)
    key_count, key_full, key_first, key_second = jax.random.split(key, 4)
    owners = F // FPO
    counts = jax.random.randint(key_count, (owners,), UNIQUE_CAP // 4, UNIQUE_CAP + 1)
    fullest = jax.random.randint(key_full, (), 0, owners)
    counts = jnp.where(jnp.arange(owners) == fullest, UNIQUE_CAP, counts)
    column_count = jnp.repeat(counts, FPO)
    first = jax.random.randint(key_first, (B_ALL, F), 0, column_count[None, :])
    second = jax.random.randint(key_second, (B_ALL, F), 0, column_count[None, :])
    chosen = jnp.minimum(first, second)
    chosen = chosen.at[0].set(column_count - 1)
    return chosen.astype(jnp.int32)


def block_scale(key, shape, cuts, least, top_value):
    factor_of = 1.0
    for position, parts in cuts:
        heights = jax.random.uniform(jax.random.fold_in(jax.random.fold_in(key, 6), position), (parts,), jnp.float32, least / len(cuts), top_value / len(cuts))
        factor_of = factor_of * jnp.repeat(jnp.exp(heights), shape[position] // parts).reshape((-1,) + (1,) * (len(shape) - 1 - position))
    return factor_of


def normal_values(stream_key, shape, deviation, reach, cuts=(), dtype=jnp.bfloat16):
    drawn = deviation * jax.random.normal(stream_key, shape, jnp.float32)
    if cuts:
        drawn = drawn * block_scale(stream_key, shape, cuts, -0.22, 0.18)
    return jnp.clip(drawn, -reach, reach).astype(dtype)


def setup_inputs(seed: int = 0) -> dict:
    seeds = jax.random.split(jax.random.key(seed), 6)
    return {
        "pooled": normal_values(seeds[0], (B_ALL, F * E), 1.0, 6.0, ((0, 128),)),
        "projection": normal_values(seeds[1], (F, K), F ** -0.5, 0.375),
        "out_weight": normal_values(seeds[2], (F * K, H), (F * K) ** -0.5, 0.0390625, ((0, 16),)),
        "cotangent": normal_values(seeds[3], (B_ALL, H), 1.0, 6.0, ((0, 128),)),
        "segments": draw_segments(jax.random.fold_in(seeds[5], 71), 0),
    }


def reference(pooled, projection, out_weight, cotangent, segments):
    scale = E ** -0.5
    total = pooled.shape[0]
    block = math.gcd(total, 512)
    count_blocks = total // block
    owner_base = ((jnp.arange(F) // FPO) * UNIQUE_CAP).astype(jnp.int32)
    proj32 = projection.astype(jnp.float32)

    def advance(carry, inputs):
        grad_weight, grad_projection, grad_rows = carry
        feats_flat, cot_block, seg_block = inputs
        feats = feats_flat.reshape(block, F, E).astype(jnp.float32)
        mixed = jnp.einsum('bfe,fk->bke', feats, proj32).astype(jnp.bfloat16)
        gram = (jnp.einsum('bfe,bke->bfk', feats, mixed.astype(jnp.float32)) * scale).astype(jnp.bfloat16)
        gram_flat = gram.reshape(block, F * K)
        preact = jnp.dot(gram_flat, out_weight, preferred_element_type=jnp.float32)
        sig = jax.nn.sigmoid(preact)
        slope = (cot_block.astype(jnp.float32) * sig * (1.0 + preact * (1.0 - sig))).astype(jnp.bfloat16)
        grad_weight = grad_weight + jnp.dot(gram_flat.T, slope, preferred_element_type=jnp.float32)
        gram_grad = jnp.dot(slope, out_weight.T, preferred_element_type=jnp.float32).astype(jnp.bfloat16)
        gram_grad = gram_grad.reshape(block, F, K).astype(jnp.float32)
        mixed_grad = (jnp.einsum('bfk,bfe->bke', gram_grad, feats) * scale).astype(jnp.bfloat16)
        mixed_grad32 = mixed_grad.astype(jnp.float32)
        grad_projection = grad_projection + jnp.einsum('bfe,bke->fk', feats, mixed_grad32)
        feat_grad = (jnp.einsum('bfk,bke->bfe', gram_grad, mixed.astype(jnp.float32)) * scale
                     + jnp.einsum('fk,bke->bfe', proj32, mixed_grad32)).astype(jnp.bfloat16)
        global_seg = (seg_block + owner_base[None, :]).astype(jnp.int32)
        grad_rows = grad_rows + jax.ops.segment_sum(feat_grad.reshape(block * F, E).astype(jnp.float32),
                                                    global_seg.reshape(-1), num_segments=DEVICES * UNIQUE_CAP)
        return (grad_weight, grad_projection, grad_rows), None

    start = (jnp.zeros((F * K, H), jnp.float32), jnp.zeros((F, K), jnp.float32),
             jnp.zeros((DEVICES * UNIQUE_CAP, E), jnp.float32))
    inputs = (pooled.reshape(count_blocks, block, F * E), cotangent.reshape(count_blocks, block, H),
              segments.reshape(count_blocks, block, F))
    (grad_weight, grad_projection, grad_rows), _ = lax.scan(advance, start, inputs)
    return grad_weight, grad_projection, grad_rows
```

```python
import functools

import jax
import jax.numpy as jnp
from jax import lax
from jax.experimental import pallas as pl
from jax.experimental.pallas import tpu as pltpu
from jax.sharding import PartitionSpec as P

F = 256
E = 192
K = 96
H = 128
UNIQUE_CAP = 1024
PAIRS = F // 2
ROWS = 16
SCALE = E ** (-0.5)
BF = jnp.bfloat16
F32 = jnp.float32
VMEM_LIMIT = 60 * 1024 * 1024
NT = (((1,), (1,)), ((), ()))
TN = (((0,), (0,)), ((), ()))


def interleave(even, odd):
    width = even.shape[-1]
    both = jnp.concatenate([even.reshape(16, 8, width), odd.reshape(16, 8, width)], axis=1)
    return both.reshape(F, width)


def lower_half(rows):
    return lax.broadcasted_iota(jnp.int32, (rows, 128), 1) < 64


def front_kernel(x_ref, projt_ref, xs_ref, mixed_ref, gram_ref, wide, turned):
    def spread(step, carry):
        for inner in range(8):
            tile = step * 8 + inner
            wide[pl.ds(pl.multiple_of(tile * ROWS, ROWS), ROWS), :] = x_ref[
                :, pl.ds(pl.multiple_of(tile * 128, 128), 128)
            ].astype(F32)
        return carry

    lax.fori_loop(0, F * E // 1024, spread, 0)
    low = lower_half(PAIRS)

    def sample(b):
        a0 = wide[pl.ds(b, PAIRS, stride=3 * ROWS), :]
        a1 = wide[pl.ds(b + ROWS, PAIRS, stride=3 * ROWS), :]
        a2 = wide[pl.ds(b + 2 * ROWS, PAIRS, stride=3 * ROWS), :]
        r1 = pltpu.roll(a1, 64, 1)
        r2 = pltpu.roll(a2, 64, 1)
        even = jnp.concatenate([a0, jnp.where(low, a1, 0.0)], axis=1)
        odd = jnp.concatenate([jnp.where(low, r1, r2), jnp.where(low, r2, 0.0)], axis=1)
        xb = interleave(even, odd).astype(BF)
        xs_ref[b] = xb
        mixed = jnp.dot(projt_ref[...], xb, preferred_element_type=F32).astype(BF)
        mixed_ref[b] = mixed
        gram = lax.dot_general(mixed, xb, NT, preferred_element_type=F32) * SCALE
        turned[0, pl.ds(b, K, stride=ROWS), :] = gram[:, :128]
        turned[1, pl.ds(b, K, stride=ROWS), :] = gram[:, 128:]

    def samples(step, carry):
        for inner in range(4):
            sample(step * 4 + inner)
        return carry

    lax.fori_loop(0, ROWS // 4, samples, 0)
    for half in range(2):
        gram_ref[:, :, half * 128 : half * 128 + 128] = (
            turned[half].reshape(K, ROWS, 128).astype(BF)
        )


def front(x, projt):
    batch = x.shape[0]
    return pl.pallas_call(
        front_kernel,
        grid=(batch // ROWS,),
        in_specs=[
            pl.BlockSpec((ROWS, F * E), lambda i: (i, 0)),
            pl.BlockSpec((K, F), lambda i: (0, 0)),
        ],
        out_specs=[
            pl.BlockSpec((ROWS, F, 256), lambda i: (i, 0, 0)),
            pl.BlockSpec((ROWS, K, 256), lambda i: (i, 0, 0)),
            pl.BlockSpec((K, ROWS, F), lambda i: (0, i, 0)),
        ],
        out_shape=[
            jax.ShapeDtypeStruct((batch, F, 256), BF),
            jax.ShapeDtypeStruct((batch, K, 256), BF),
            jax.ShapeDtypeStruct((K, batch, F), BF),
        ],
        scratch_shapes=[
            pltpu.VMEM((F * E // 128 * ROWS, 128), F32),
            pltpu.VMEM((2, K * ROWS, 128), F32),
        ],
        compiler_params=pltpu.CompilerParams(vmem_limit_bytes=VMEM_LIMIT),
        cost_estimate=pl.CostEstimate(
            flops=4 * batch * F * E * K, bytes_accessed=42_000_000, transcendentals=0
        ),
        name="front",
    )(x, projt)


def middle_kernel(gram_ref, w_ref, cot_ref, wgrad_ref, gg_ref, turned):
    batch = gram_ref.shape[1]

    def weight(k):
        return w_ref[:, k].reshape(F, H)

    def product(step, total):
        for inner in range(8):
            k = step * 8 + inner
            total = total + jnp.dot(gram_ref[k], weight(k), preferred_element_type=F32)
        return total

    preact = lax.fori_loop(0, K // 8, product, jnp.zeros((batch, H), F32))
    sig = jax.nn.sigmoid(preact)
    slope = (cot_ref[...].astype(F32) * sig * (1.0 + preact * (1.0 - sig))).astype(BF)

    def gradients(step, carry):
        for inner in range(4):
            k = step * 4 + inner
            wgrad = lax.dot_general(gram_ref[k], slope, TN, preferred_element_type=F32)
            for block in range(16):
                for parity in range(2):
                    at = block * 16 + parity * 8
                    wgrad_ref[pl.ds(block * 8 * 2 * K + parity * K + k, 8, stride=2 * K), :] = wgrad[
                        at : at + 8
                    ]
            gg = lax.dot_general(slope, weight(k), NT, preferred_element_type=F32)
            turned[0, pl.ds(k, batch, stride=K), :] = gg[:, :128]
            turned[1, pl.ds(k, batch, stride=K), :] = gg[:, 128:]
        return carry

    lax.fori_loop(0, K // 4, gradients, 0)

    def pack(b, carry):
        at = pl.ds(pl.multiple_of(b * K, K), K)
        gg_ref[b] = jnp.concatenate([turned[0, at, :], turned[1, at, :]], axis=1).astype(BF)
        return carry

    lax.fori_loop(0, batch, pack, 0)


def middle(gram, w, cot):
    batch = gram.shape[1]
    whole = pl.BlockSpec(memory_space=pltpu.VMEM)
    return pl.pallas_call(
        middle_kernel,
        in_specs=[whole] * 3,
        out_specs=[whole] * 2,
        out_shape=[
            jax.ShapeDtypeStruct((F * K, H), F32),
            jax.ShapeDtypeStruct((batch, K, F), BF),
        ],
        scratch_shapes=[pltpu.VMEM((2, batch * K, 128), F32)],
        compiler_params=pltpu.CompilerParams(vmem_limit_bytes=VMEM_LIMIT),
        cost_estimate=pl.CostEstimate(
            flops=6 * batch * F * K * H, bytes_accessed=33_000_000, transcendentals=batch * H
        ),
        name="middle",
    )(gram, w, cot)


def back_kernel(xs_ref, mixed_ref, gg_ref, projt_ref, fg_ref, pg_ref, wide):
    low = lower_half(PAIRS)

    @pl.when(pl.program_id(0) == 0)
    def _():
        pg_ref[...] = jnp.zeros_like(pg_ref)

    def sample(b):
        xb = xs_ref[b]
        gg = gg_ref[b]
        mg = jnp.dot(gg, xb, preferred_element_type=F32).astype(BF)
        pg = lax.dot_general(mg, xb, NT, preferred_element_type=F32)
        left = jnp.concatenate([gg, projt_ref[...]], axis=0)
        right = jnp.concatenate([mixed_ref[b], mg], axis=0)
        fg = lax.dot_general(left, right, TN, preferred_element_type=F32) * SCALE
        fg = fg.reshape(16, 2, 8, 256)
        even = fg[:, 0].reshape(PAIRS, 256)
        odd = fg[:, 1].reshape(PAIRS, 256)
        r0 = pltpu.roll(odd[:, :128], 64, 1)
        r1 = pltpu.roll(odd[:, 128:], 64, 1)
        wide[pl.ds(b, PAIRS, stride=3 * ROWS), :] = even[:, :128]
        wide[pl.ds(b + ROWS, PAIRS, stride=3 * ROWS), :] = jnp.where(low, even[:, 128:], r0)
        wide[pl.ds(b + 2 * ROWS, PAIRS, stride=3 * ROWS), :] = jnp.where(low, r0, r1)
        return pg

    def samples(step, total):
        for inner in range(4):
            total = total + sample(step * 4 + inner)
        return total

    pg_ref[...] += lax.fori_loop(0, ROWS // 4, samples, jnp.zeros((K, F), F32)) * SCALE

    def pack(p, carry):
        for tile in range(3):
            at = pl.ds(pl.multiple_of(p * 3 * ROWS + tile * ROWS, ROWS), ROWS)
            fg_ref[p, :, tile * 128 : tile * 128 + 128] = wide[at, :].astype(BF)
        return carry

    lax.fori_loop(0, PAIRS, pack, 0, unroll=4)


def back(xs, mixed, gg, projt):
    batch = xs.shape[0]
    return pl.pallas_call(
        back_kernel,
        grid=(batch // ROWS,),
        in_specs=[
            pl.BlockSpec((ROWS, F, 256), lambda i: (i, 0, 0)),
            pl.BlockSpec((ROWS, K, 256), lambda i: (i, 0, 0)),
            pl.BlockSpec((ROWS, K, F), lambda i: (i, 0, 0)),
            pl.BlockSpec((K, F), lambda i: (0, 0)),
        ],
        out_specs=[
            pl.BlockSpec((PAIRS, ROWS, 2 * E), lambda i: (0, i, 0)),
            pl.BlockSpec((K, F), lambda i: (0, 0)),
        ],
        out_shape=[
            jax.ShapeDtypeStruct((PAIRS, batch, 2 * E), BF),
            jax.ShapeDtypeStruct((K, F), F32),
        ],
        scratch_shapes=[pltpu.VMEM((F * E // 128 * ROWS, 128), F32)],
        compiler_params=pltpu.CompilerParams(vmem_limit_bytes=VMEM_LIMIT),
        cost_estimate=pl.CostEstimate(
            flops=8 * batch * F * E * K, bytes_accessed=42_000_000, transcendentals=0
        ),
        name="back",
    )(xs, mixed, gg, projt)


CHUNK = 2048
SLOT_BLOCK = 256


def rows_kernel(data_ref, seg_ref, out_ref, even, odd):
    step = pl.program_id(0)

    @pl.when(step == 0)
    def _():
        even[...] = jnp.zeros_like(even)
        odd[...] = jnp.zeros_like(odd)

    slot = lax.broadcasted_iota(jnp.int32, (SLOT_BLOCK, CHUNK), 0)
    for block in range(UNIQUE_CAP // SLOT_BLOCK):
        at = pl.ds(block * SLOT_BLOCK, SLOT_BLOCK)
        for parity, total in ((0, even), (1, odd)):
            seg = seg_ref[parity : parity + 1, :] - block * SLOT_BLOCK
            hot = jnp.where(slot == seg, 1.0, 0.0).astype(BF)
            total[at, :] += jnp.dot(
                hot, data_ref[:, parity * 128 : parity * 128 + 256], preferred_element_type=F32
            )

    @pl.when(step == pl.num_programs(0) - 1)
    def _():
        low = lower_half(UNIQUE_CAP)
        r0 = pltpu.roll(odd[:, :128], 64, 1)
        r1 = pltpu.roll(odd[:, 128:], 64, 1)
        out_ref[:, :128] = even[:, :128] + jnp.where(low, r0, r1)
        out_ref[:, 128:] = (even[:, 128:] + r1)[:, :64]


def row_sums(data, seg):
    count = data.shape[0]
    return pl.pallas_call(
        rows_kernel,
        grid=(count // CHUNK,),
        in_specs=[
            pl.BlockSpec((CHUNK, 2 * E), lambda i: (i, 0)),
            pl.BlockSpec((2, CHUNK), lambda i: (0, i)),
        ],
        out_specs=pl.BlockSpec((UNIQUE_CAP, E), lambda i: (0, 0)),
        out_shape=jax.ShapeDtypeStruct((UNIQUE_CAP, E), F32),
        scratch_shapes=[pltpu.VMEM((UNIQUE_CAP, 256), F32)] * 2,
        compiler_params=pltpu.CompilerParams(vmem_limit_bytes=VMEM_LIMIT),
        cost_estimate=pl.CostEstimate(
            flops=4 * UNIQUE_CAP * count * 256, bytes_accessed=14_000_000, transcendentals=0
        ),
        name="row_sums",
    )(data, seg)


def turn_features(a):
    rest = a.shape[1:]
    return a.reshape((-1, 8, 2) + rest).swapaxes(1, 2).reshape(a.shape)


def unturn_features(a):
    rest = a.shape[1:]
    return a.reshape((-1, 2, 8) + rest).swapaxes(1, 2).reshape(a.shape)


def on_device(pooled, projection, out_weight, cotangent, segments):
    batch = pooled.shape[0]
    own = turn_features(out_weight.reshape(-1, K, H)).swapaxes(0, 1)
    weight = lax.all_gather(own, "fsdp", axis=0)
    projt = turn_features(projection).T
    xs, mixed, gram = front(pooled, projt)
    wgrad, gg = middle(gram, weight, cotangent)
    fg, pg = back(xs, mixed, gg, projt)
    received = lax.all_to_all(fg, ("fsdp", "emb"), split_axis=0, concat_axis=0, tiled=True)
    proj_grad = lax.psum(unturn_features(pg.T), ("fsdp", "emb"))
    weight_grad = lax.psum_scatter(wgrad, ("fsdp", "emb"), scatter_dimension=0, tiled=True)
    row_grad = row_sums(received.reshape(-1, 2 * E), segments.T)
    return (weight_grad, proj_grad, row_grad)


def solution(mesh):
    placed = (
        P(("fsdp", "emb"), None),
        P(),
        P("fsdp", None),
        P(("fsdp", "emb"), None),
        P(None, ("fsdp", "emb")),
    )
    return jax.shard_map(
        on_device,
        mesh=mesh,
        in_specs=placed,
        out_specs=(P(("fsdp", "emb"), None), P(), P(("fsdp", "emb"), None)),
        check_vma=False,
    )
```

```python
import functools

import jax
import jax.numpy as jnp
from jax import lax
from jax.experimental import pallas as pl
from jax.experimental.pallas import tpu as pltpu
from jax.sharding import PartitionSpec as P

F = 256
E = 192
K = 96
H = 128
UNIQUE_CAP = 1024
PAIRS = F // 2
ROWS = 16
SCALE = E ** (-0.5)
BF = jnp.bfloat16
F32 = jnp.float32
VMEM_LIMIT = 60 * 1024 * 1024
NT = (((1,), (1,)), ((), ()))
TN = (((0,), (0,)), ((), ()))


def interleave(even, odd):
    width = even.shape[-1]
    both = jnp.concatenate([even.reshape(16, 8, width), odd.reshape(16, 8, width)], axis=1)
    return both.reshape(F, width)


def lower_half(rows):
    return lax.broadcasted_iota(jnp.int32, (rows, 128), 1) < 64


def front_kernel(x_ref, projt_ref, xs_ref, mixed_ref, gram_ref, wide, turned):
    def spread(step, carry):
        for inner in range(8):
            tile = step * 8 + inner
            wide[pl.ds(pl.multiple_of(tile * ROWS, ROWS), ROWS), :] = x_ref[
                :, pl.ds(pl.multiple_of(tile * 128, 128), 128)
            ].astype(F32)
        return carry

    lax.fori_loop(0, F * E // 1024, spread, 0)
    low = lower_half(PAIRS)

    def sample(b):
        a0 = wide[pl.ds(b, PAIRS, stride=3 * ROWS), :]
        a1 = wide[pl.ds(b + ROWS, PAIRS, stride=3 * ROWS), :]
        a2 = wide[pl.ds(b + 2 * ROWS, PAIRS, stride=3 * ROWS), :]
        r1 = pltpu.roll(a1, 64, 1)
        r2 = pltpu.roll(a2, 64, 1)
        even = jnp.concatenate([a0, jnp.where(low, a1, 0.0)], axis=1)
        odd = jnp.concatenate([jnp.where(low, r1, r2), jnp.where(low, r2, 0.0)], axis=1)
        xb = interleave(even, odd).astype(BF)
        xs_ref[b] = xb
        mixed = jnp.dot(projt_ref[...], xb, preferred_element_type=F32).astype(BF)
        mixed_ref[b] = mixed
        gram = lax.dot_general(mixed, xb, NT, preferred_element_type=F32) * SCALE
        turned[0, pl.ds(b, K, stride=ROWS), :] = gram[:, :128]
        turned[1, pl.ds(b, K, stride=ROWS), :] = gram[:, 128:]

    def samples(step, carry):
        for inner in range(4):
            sample(step * 4 + inner)
        return carry

    lax.fori_loop(0, ROWS // 4, samples, 0)
    for half in range(2):
        gram_ref[:, :, half * 128 : half * 128 + 128] = (
            turned[half].reshape(K, ROWS, 128).astype(BF)
        )


def front(x, projt):
    batch = x.shape[0]
    return pl.pallas_call(
        front_kernel,
        grid=(batch // ROWS,),
        in_specs=[
            pl.BlockSpec((ROWS, F * E), lambda i: (i, 0)),
            pl.BlockSpec((K, F), lambda i: (0, 0)),
        ],
        out_specs=[
            pl.BlockSpec((ROWS, F, 256), lambda i: (i, 0, 0)),
            pl.BlockSpec((ROWS, K, 256), lambda i: (i, 0, 0)),
            pl.BlockSpec((K, ROWS, F), lambda i: (0, i, 0)),
        ],
        out_shape=[
            jax.ShapeDtypeStruct((batch, F, 256), BF),
            jax.ShapeDtypeStruct((batch, K, 256), BF),
            jax.ShapeDtypeStruct((K, batch, F), BF),
        ],
        scratch_shapes=[
            pltpu.VMEM((F * E // 128 * ROWS, 128), F32),
            pltpu.VMEM((2, K * ROWS, 128), F32),
        ],
        compiler_params=pltpu.CompilerParams(vmem_limit_bytes=VMEM_LIMIT),
        cost_estimate=pl.CostEstimate(
            flops=4 * batch * F * E * K, bytes_accessed=42_000_000, transcendentals=0
        ),
        name="front",
    )(x, projt)


def middle_kernel(gram_ref, w_ref, cot_ref, wgrad_ref, gg_ref, turned):
    batch = gram_ref.shape[1]

    def weight(k):
        return w_ref[:, k].reshape(F, H)

    def product(step, total):
        for inner in range(8):
            k = step * 8 + inner
            total = total + jnp.dot(gram_ref[k], weight(k), preferred_element_type=F32)
        return total

    preact = lax.fori_loop(0, K // 8, product, jnp.zeros((batch, H), F32))
    sig = jax.nn.sigmoid(preact)
    slope = (cot_ref[...].astype(F32) * sig * (1.0 + preact * (1.0 - sig))).astype(BF)

    def gradients(step, carry):
        for inner in range(4):
            k = step * 4 + inner
            wgrad = lax.dot_general(gram_ref[k], slope, TN, preferred_element_type=F32)
            for block in range(16):
                for parity in range(2):
                    at = block * 16 + parity * 8
                    wgrad_ref[pl.ds(block * 8 * 2 * K + parity * K + k, 8, stride=2 * K), :] = wgrad[
                        at : at + 8
                    ]
            gg = lax.dot_general(slope, weight(k), NT, preferred_element_type=F32)
            turned[0, pl.ds(k, batch, stride=K), :] = gg[:, :128]
            turned[1, pl.ds(k, batch, stride=K), :] = gg[:, 128:]
        return carry

    lax.fori_loop(0, K // 4, gradients, 0)

    def pack(b, carry):
        at = pl.ds(pl.multiple_of(b * K, K), K)
        gg_ref[b] = jnp.concatenate([turned[0, at, :], turned[1, at, :]], axis=1).astype(BF)
        return carry

    lax.fori_loop(0, batch, pack, 0)


def middle(gram, w, cot):
    batch = gram.shape[1]
    whole = pl.BlockSpec(memory_space=pltpu.VMEM)
    return pl.pallas_call(
        middle_kernel,
        in_specs=[whole] * 3,
        out_specs=[whole] * 2,
        out_shape=[
            jax.ShapeDtypeStruct((F * K, H), F32),
            jax.ShapeDtypeStruct((batch, K, F), BF),
        ],
        scratch_shapes=[pltpu.VMEM((2, batch * K, 128), F32)],
        compiler_params=pltpu.CompilerParams(vmem_limit_bytes=VMEM_LIMIT),
        cost_estimate=pl.CostEstimate(
            flops=6 * batch * F * K * H, bytes_accessed=33_000_000, transcendentals=batch * H
        ),
        name="middle",
    )(gram, w, cot)


MESH = pl.DeviceIdType.MESH


def place():
    fsdp = lax.axis_index("fsdp")
    emb = lax.axis_index("emb")
    return fsdp // 4, fsdp % 4, emb // 2, emb % 2


def device(x, y, z, core):
    return (x * 4 + y, z * 2 + core)


def back_kernel(
    xs_ref, mixed_ref, gg_ref, projt_ref, wgrad_ref,
    pg_ref, rows_ref, other_ref,
    wide, stage, send_sem, recv_sem, own_sem, pair_sem,
):
    low = lower_half(PAIRS)
    step = pl.program_id(0)
    steps = pl.num_programs(0)
    x, y, z, core = place()
    line = jnp.where(core == 0, x, y)
    slot = lax.rem(step, 2)
    sibling = device(x, y, z, 1 - core)

    def weight_copy():
        return pltpu.make_async_remote_copy(
            src_ref=wgrad_ref.at[:, 1 - core],
            dst_ref=other_ref,
            send_sem=pair_sem.at[0],
            recv_sem=pair_sem.at[1],
            device_id=sibling,
            device_id_type=MESH,
        )

    def copies(block, where):
        at_x = pl.ds((x * 2 + core) * 128 + block * ROWS, ROWS)
        at_y = pl.ds((y * 2 + core) * 128 + block * ROWS, ROWS)
        found = []
        for d in range(1, 4):
            tx = lax.rem(x + d, 4)
            ty = lax.rem(y + d, 4)
            for kind, group, rows, target in (
                (0, tx, at_x, device(tx, y, z, 0)),
                (1, 4 + ty, at_y, device(x, ty, z, 1)),
            ):
                found.append(
                    pltpu.make_async_remote_copy(
                        src_ref=stage.at[where, pl.ds(group * 16, 16)],
                        dst_ref=rows_ref.at[:, rows],
                        send_sem=send_sem.at[where, kind * 3 + d - 1],
                        recv_sem=recv_sem.at[block, d * 2 + core],
                        device_id=target,
                        device_id_type=MESH,
                    )
                )
        group = jnp.where(core == 0, 4 + y, x)
        there = pl.ds((jnp.where(core == 0, y, x) * 2 + core) * 128 + block * ROWS, ROWS)
        found.append(
            pltpu.make_async_remote_copy(
                src_ref=stage.at[where, pl.ds(group * 16, 16)],
                dst_ref=rows_ref.at[:, there],
                send_sem=send_sem.at[where, 6],
                recv_sem=recv_sem.at[block, 0],
                device_id=sibling,
                device_id_type=MESH,
            )
        )
        return found

    def own_copy(block, where):
        group = jnp.where(core == 0, x, 4 + y)
        here = pl.ds((line * 2 + core) * 128 + block * ROWS, ROWS)
        return pltpu.make_async_copy(
            stage.at[where, pl.ds(group * 16, 16)], rows_ref.at[:, here], own_sem.at[where]
        )

    @pl.when(step == 0)
    def _():
        pg_ref[...] = jnp.zeros_like(pg_ref)
        barrier = pltpu.get_barrier_semaphore()
        pl.semaphore_signal(barrier, inc=1, device_id=sibling, device_id_type=MESH)
        for d in range(1, 4):
            from_x = jnp.where(core == 0, lax.rem(x + d, 4), x)
            from_y = jnp.where(core == 0, y, lax.rem(y + d, 4))
            for other in range(2):
                pl.semaphore_signal(
                    barrier, inc=1, device_id=device(from_x, from_y, z, other), device_id_type=MESH
                )
        pl.semaphore_wait(barrier, 7)
        weight_copy().start()

    def sample(b):
        xb = xs_ref[b]
        gg = gg_ref[b]
        mg = jnp.dot(gg, xb, preferred_element_type=F32).astype(BF)
        pg = lax.dot_general(mg, xb, NT, preferred_element_type=F32)
        left = jnp.concatenate([gg, projt_ref[...]], axis=0)
        right = jnp.concatenate([mixed_ref[b], mg], axis=0)
        fg = lax.dot_general(left, right, TN, preferred_element_type=F32) * SCALE
        fg = fg.reshape(16, 2, 8, 256)
        even = fg[:, 0].reshape(PAIRS, 256)
        odd = fg[:, 1].reshape(PAIRS, 256)
        r0 = pltpu.roll(odd[:, :128], 64, 1)
        r1 = pltpu.roll(odd[:, 128:], 64, 1)
        wide[pl.ds(b, PAIRS, stride=3 * ROWS), :] = even[:, :128]
        wide[pl.ds(b + ROWS, PAIRS, stride=3 * ROWS), :] = jnp.where(low, even[:, 128:], r0)
        wide[pl.ds(b + 2 * ROWS, PAIRS, stride=3 * ROWS), :] = jnp.where(low, r0, r1)
        return pg

    def samples(turn, total):
        for inner in range(4):
            total = total + sample(turn * 4 + inner)
        return total

    pg_ref[...] += lax.fori_loop(0, ROWS // 4, samples, jnp.zeros((K, F), F32)) * SCALE

    @pl.when(step >= 2)
    def _():
        for copy in copies(step - 2, slot):
            copy.wait_send()
        own_copy(step - 2, slot).wait()

    def pack(q, carry):
        for kind in range(2):
            for last in range(4):
                first, second = q // 4, q % 4
                if kind == 0:
                    owner = ((first * 4 + second) * 4 + last) * 2
                else:
                    owner = ((second * 4 + first) * 4 + last) * 2 + 1
                for tile in range(3):
                    at = pl.ds(pl.multiple_of(owner * 3 * ROWS + tile * ROWS, ROWS), ROWS)
                    stage[slot, kind * 64 + q * 4 + last, :, tile * 128 : tile * 128 + 128] = wide[
                        at, :
                    ].astype(BF)
        return carry

    lax.fori_loop(0, 16, pack, 0)
    for copy in copies(step, slot):
        copy.start()
    own_copy(step, slot).start()

    @pl.when(step == steps - 1)
    def _():
        for block, where in ((step - 1, 1 - slot), (step, slot)):
            for copy in copies(block, where):
                copy.wait_send()
            own_copy(block, where).wait()
        copy = weight_copy()
        copy.wait_send()
        copy.wait_recv()

        def arrived(block, carry):
            def wait(sender, sem):
                at = pl.ds(sender * 128 + block * ROWS, ROWS)
                pltpu.make_async_remote_copy(
                    src_ref=stage.at[0, pl.ds(0, 16)],
                    dst_ref=rows_ref.at[:, at],
                    send_sem=send_sem.at[0, 0],
                    recv_sem=recv_sem.at[block, sem],
                    device_id=sibling,
                    device_id_type=MESH,
                ).wait_recv()

            wait(line * 2 + 1 - core, 0)
            for d in range(1, 4):
                for other in range(2):
                    wait(lax.rem(line + 4 - d, 4) * 2 + other, d * 2 + other)
            return carry

        lax.fori_loop(0, steps, arrived, 0)


def back(xs, mixed, gg, projt, wgrad):
    batch = xs.shape[0]
    any_space = pl.BlockSpec(memory_space=pl.ANY)
    return pl.pallas_call(
        back_kernel,
        grid=(batch // ROWS,),
        in_specs=[
            pl.BlockSpec((ROWS, F, 256), lambda i: (i, 0, 0)),
            pl.BlockSpec((ROWS, K, 256), lambda i: (i, 0, 0)),
            pl.BlockSpec((ROWS, K, F), lambda i: (i, 0, 0)),
            pl.BlockSpec((K, F), lambda i: (0, 0)),
            any_space,
        ],
        out_specs=[pl.BlockSpec((K, F), lambda i: (0, 0)), any_space, any_space],
        out_shape=[
            jax.ShapeDtypeStruct((K, F), F32),
            jax.ShapeDtypeStruct((16, 8 * batch, 2 * E), BF),
            jax.ShapeDtypeStruct((64, 2 * K, H), F32),
        ],
        scratch_shapes=[
            pltpu.VMEM((F * E // 128 * ROWS, 128), F32),
            pltpu.VMEM((2, PAIRS, ROWS, 2 * E), BF),
            pltpu.SemaphoreType.DMA((2, 7)),
            pltpu.SemaphoreType.DMA((batch // ROWS, 8)),
            pltpu.SemaphoreType.DMA((2,)),
            pltpu.SemaphoreType.DMA((2,)),
        ],
        compiler_params=pltpu.CompilerParams(
            vmem_limit_bytes=VMEM_LIMIT, collective_id=1, has_side_effects=True
        ),
        cost_estimate=pl.CostEstimate(
            flops=8 * batch * F * E * K, bytes_accessed=42_000_000, transcendentals=0
        ),
        name="back",
    )(xs, mixed, gg, projt, wgrad)


SLOT_BLOCK = 256
HALF = UNIQUE_CAP // 2


def sums_kernel(
    rows_ref, seg_ref, wgrad_ref, other_ref, pg_ref,
    wout_ref, pout_ref, out_ref,
    data, table, table_z, sum_v, table_v,
    own, other, w2, w2_in, w3, w3_in, w4, w4_in, pu, pv, pz, pc,
    load_sem, own_sem, z_send, z_recv, v_send, v_recv, w_send, w_recv, p_send, p_recv,
):
    x, y, z, core = place()
    u = jnp.where(core == 0, x, y)
    v = jnp.where(core == 0, y, x)
    low = lower_half(SLOT_BLOCK)

    def at_u(d):
        moved = lax.rem(u + d, 4)
        return device(jnp.where(core == 0, moved, x), jnp.where(core == 0, y, moved), z, core)

    def at_v(d):
        moved = lax.rem(v + d, 4)
        return device(jnp.where(core == 0, x, moved), jnp.where(core == 0, moved, y), z, core)

    def at_z(d):
        return device(x, y, lax.rem(z + d, 4), core)

    sibling = device(x, y, z, 1 - core)

    def remote(source, target, send, recv, to):
        return pltpu.make_async_remote_copy(
            src_ref=source,
            dst_ref=target,
            send_sem=send,
            recv_sem=recv,
            device_id=to,
            device_id_type=MESH,
        )

    def load(j):
        return pltpu.make_async_copy(rows_ref.at[j], data.at[j], load_sem.at[j])

    own_copy = pltpu.make_async_copy(wgrad_ref.at[:, core], own, own_sem.at[0])
    other_copy = pltpu.make_async_copy(other_ref, other, own_sem.at[1])
    order = [1, 2, 3, 0]

    def group_of(g):
        return lax.rem(z + g, 4)

    for g in order:
        for n in range(4):
            load(n * 4 + group_of(g)).start()
        if g == 1:
            own_copy.start()
            other_copy.start()

    barrier = pltpu.get_barrier_semaphore()
    for d in range(1, 4):
        for to in (at_u(d), at_v(d), at_z(d)):
            pl.semaphore_signal(barrier, inc=1, device_id=to, device_id_type=MESH)
    pl.semaphore_signal(barrier, inc=1, device_id=sibling, device_id_type=MESH)
    pl.semaphore_wait(barrier, 10)

    def spread(buffer, mine, stage, to):
        return [
            remote(buffer.at[mine], buffer.at[mine], p_send.at[stage, d - 1], p_recv.at[stage, d - 1], to(d))
            for d in range(1, 4)
        ]

    def gathered(buffer, mine, stage, to):
        for d in range(1, 4):
            sender = lax.rem(mine + 4 - d, 4)
            remote(
                buffer.at[sender], buffer.at[sender], p_send.at[stage, d - 1], p_recv.at[stage, d - 1], to(d)
            ).wait_recv()
        return (buffer[0] + buffer[1]) + (buffer[2] + buffer[3])

    def start(copies):
        for copy in copies:
            copy.start()
        return copies

    pending = []

    def send_table(g, n):
        return remote(
            table.at[g, n],
            table_z.at[g - 1, n],
            z_send.at[g - 1, n],
            z_recv.at[g - 1, n],
            at_z(g),
        )

    def presum(g):
        def one(n, carry):
            j = n * 4 + group_of(g)
            load(j).wait()
            slot = lax.broadcasted_iota(jnp.int32, (SLOT_BLOCK, 8 * 128), 0)

            def part(block, parity):
                seg = seg_ref[j, parity : parity + 1, :] - block * SLOT_BLOCK
                hot = jnp.where(slot == seg, 1.0, 0.0).astype(BF)
                found = jnp.dot(
                    hot, data[j, :, parity * 128 : parity * 128 + 256], preferred_element_type=F32
                )
                return found[:, :128], found[:, 128:]

            for block in range(HALF // SLOT_BLOCK):
                at = pl.ds(block * SLOT_BLOCK, SLOT_BLOCK)
                even0, even1 = part(block, 0)
                odd0, odd1 = part(block, 1)
                r0 = pltpu.roll(odd0, 64, 1)
                r1 = pltpu.roll(odd1, 64, 1)
                table[g, n, at, 0:128] = (even0 + jnp.where(low, r0, r1)).astype(BF)
                first = even1 + r1
                even0, even1 = part(block + HALF // SLOT_BLOCK, 0)
                odd0, odd1 = part(block + HALF // SLOT_BLOCK, 1)
                r0 = pltpu.roll(even0, 64, 1)
                r1 = pltpu.roll(even1, 64, 1)
                table[g, n, at, 128:256] = jnp.where(low, first, r0 + odd0).astype(BF)
                table[g, n, at, 256:384] = (jnp.where(low, r0, r1) + odd1).astype(BF)
            if g > 0:
                send_table(g, n).start()
            return carry

        lax.fori_loop(0, 4, one, 0)

    def add_four(first, rest, target, parts):
        def one(n, carry):
            total = first[n].astype(F32) + rest[0, n].astype(F32)
            total = total + (rest[1, n].astype(F32) + rest[2, n].astype(F32))
            target[n] = total.astype(target.dtype)
            return carry

        lax.fori_loop(0, parts, one, 0)

    def w_copies(source, arrive, stage, to, line, size):
        return [
            remote(
                source.at[pl.ds(lax.rem(line + d, 4) * size, size)],
                arrive.at[d - 1],
                w_send.at[stage, d - 1],
                w_recv.at[stage, d - 1],
                to(d),
            )
            for d in range(1, 4)
        ]

    pu[u] = pg_ref[...]
    p0 = start(spread(pu, u, 0, at_u))
    presum(1)

    own_copy.wait()
    other_copy.wait()

    def pair_sum(n, carry):
        first, second, last = n // 16, (n // 4) % 4, n % 4
        source = jnp.where(core == 0, first * 16 + second * 4, second * 16 + first * 4) + last
        w2[n] = (own[source] + other[source]).astype(BF)
        return carry

    lax.fori_loop(0, 64, pair_sum, 0)
    s2 = start(w_copies(w2, w2_in, 0, at_u, u, 16))
    pv[v] = gathered(pu, u, 0, at_u)
    p1 = start(spread(pv, v, 1, at_v))
    presum(2)
    for copy in s2:
        copy.wait_recv()
    add_four(w2.at[pl.ds(u * 16, 16)], w2_in, w3, 16)
    s3 = start(w_copies(w3, w3_in, 1, at_v, v, 4))
    pz[z] = gathered(pv, v, 1, at_v)
    p2 = start(spread(pz, z, 2, at_z))
    presum(3)
    for copy in s3:
        copy.wait_recv()
    add_four(w3.at[pl.ds(v * 4, 4)], w3_in, w4, 4)
    s4 = start(w_copies(w4, w4_in, 2, at_z, z, 1))
    pc[core] = gathered(pz, z, 2, at_z)
    p3 = remote(pc.at[core], pc.at[core], p_send.at[3, 0], p_recv.at[3, 0], sibling)
    p3.start()
    presum(0)
    for copy in s4:
        copy.wait_recv()
    total = w4[z].astype(F32) + w4_in[0, 0].astype(F32)
    wout_ref[...] = total + (w4_in[1, 0].astype(F32) + w4_in[2, 0].astype(F32))
    remote(pc.at[1 - core], pc.at[1 - core], p_send.at[3, 0], p_recv.at[3, 0], sibling).wait_recv()
    pout_ref[...] = pc[0] + pc[1]

    def v_copy(d):
        return remote(sum_v.at[d], table_v.at[d - 1], v_send.at[d - 1], v_recv.at[d - 1], at_v(d))

    for d in order:
        n = lax.rem(v + d, 4)
        for g in range(1, 4):
            send_table(g, n).wait_recv()

        def add(part, carry):
            at = pl.ds(pl.multiple_of(part * 64, 64), 64)
            total = table[0, n, at].astype(F32) + table_z[0, n, at].astype(F32)
            total = total + (table_z[1, n, at].astype(F32) + table_z[2, n, at].astype(F32))
            sum_v[d, at] = total.astype(BF)
            return carry

        lax.fori_loop(0, HALF // 64, add, 0)
        if d > 0:
            v_copy(d).start()
    for d in range(1, 4):
        v_copy(d).wait_recv()

    def finish(part, carry):
        at = pl.ds(pl.multiple_of(part * 64, 64), 64)
        after = pl.ds(pl.multiple_of(part * 64 + HALF, 64), 64)
        total = sum_v[0, at].astype(F32) + table_v[0, at].astype(F32)
        total = total + (table_v[1, at].astype(F32) + table_v[2, at].astype(F32))
        out_ref[at, :] = total[:, :E]
        r1 = pltpu.roll(total[:, 128:256], 64, 1)
        r2 = pltpu.roll(total[:, 256:], 64, 1)
        out_ref[after, :128] = jnp.where(lower_half(64), r1, r2)
        out_ref[after, 128:] = r2[:, :64]
        return carry

    lax.fori_loop(0, HALF // 64, finish, 0)

    for copy in p0 + p1 + p2 + [p3] + s2 + s3 + s4:
        copy.wait_send()
    for d in range(1, 4):
        v_copy(d).wait_send()
        for n in range(4):
            send_table(d, n).wait_send()


def sums(rows, seg, wgrad, other, pg):
    any_space = pl.BlockSpec(memory_space=pl.ANY)
    whole = pl.BlockSpec(memory_space=pltpu.VMEM)
    dma = pltpu.SemaphoreType.DMA
    return pl.pallas_call(
        sums_kernel,
        in_specs=[any_space, whole, any_space, any_space, whole],
        out_specs=[whole] * 3,
        out_shape=[
            jax.ShapeDtypeStruct((2 * K, H), F32),
            jax.ShapeDtypeStruct((K, F), F32),
            jax.ShapeDtypeStruct((UNIQUE_CAP, E), F32),
        ],
        scratch_shapes=[
            pltpu.VMEM(rows.shape, BF),
            pltpu.VMEM((4, 4, HALF, 2 * E), BF),
            pltpu.VMEM((3, 4, HALF, 2 * E), BF),
            pltpu.VMEM((4, HALF, 2 * E), BF),
            pltpu.VMEM((3, HALF, 2 * E), BF),
            pltpu.VMEM((64, 2 * K, H), F32),
            pltpu.VMEM((64, 2 * K, H), F32),
            pltpu.VMEM((64, 2 * K, H), BF),
            pltpu.VMEM((3, 16, 2 * K, H), BF),
            pltpu.VMEM((16, 2 * K, H), BF),
            pltpu.VMEM((3, 4, 2 * K, H), BF),
            pltpu.VMEM((4, 2 * K, H), BF),
            pltpu.VMEM((3, 1, 2 * K, H), BF),
            pltpu.VMEM((4, K, F), F32),
            pltpu.VMEM((4, K, F), F32),
            pltpu.VMEM((4, K, F), F32),
            pltpu.VMEM((2, K, F), F32),
            dma((16,)),
            dma((2,)),
            dma((3, 4)),
            dma((3, 4)),
            dma((3,)),
            dma((3,)),
            dma((3, 3)),
            dma((3, 3)),
            dma((4, 3)),
            dma((4, 3)),
        ],
        compiler_params=pltpu.CompilerParams(
            vmem_limit_bytes=VMEM_LIMIT, collective_id=2, has_side_effects=True
        ),
        cost_estimate=pl.CostEstimate(
            flops=16 * 4 * UNIQUE_CAP * 1024 * 256, bytes_accessed=30_000_000, transcendentals=0
        ),
        name="sums",
    )(rows, seg, wgrad, other, pg)


def turn_features(a):
    rest = a.shape[1:]
    return a.reshape((-1, 8, 2) + rest).swapaxes(1, 2).reshape(a.shape)


def unturn_features(a):
    rest = a.shape[1:]
    return a.reshape((-1, 2, 8) + rest).swapaxes(1, 2).reshape(a.shape)


def seg_groups():
    groups = []
    for x in range(4):
        groups.append([(x * 4 + y) * 8 + z * 2 for y in range(4) for z in range(4)])
    for y in range(4):
        groups.append([(x * 4 + y) * 8 + z * 2 + 1 for x in range(4) for z in range(4)])
    return groups


def spread_segments(segments):
    core = lax.axis_index("emb") % 2
    seg = segments.T.reshape(2, 4, 4, 4, 2, 128)
    along_x = seg.transpose(2, 3, 0, 1, 4, 5).reshape(16, 2, 1024)
    along_y = seg.transpose(1, 3, 0, 2, 4, 5).reshape(16, 2, 1024)
    return lax.all_to_all(
        jnp.where(core == 0, along_x, along_y),
        ("fsdp", "emb"),
        split_axis=0,
        concat_axis=0,
        axis_index_groups=seg_groups(),
        tiled=True,
    )


def on_device(pooled, projection, out_weight, cotangent, segments):
    own = turn_features(out_weight.reshape(-1, K, H)).swapaxes(0, 1)
    weight = lax.all_gather(own, "fsdp", axis=0)
    seg = spread_segments(segments)
    projt = turn_features(projection).T
    xs, mixed, gram = front(pooled, projt)
    wgrad, gg = middle(gram, weight, cotangent)
    wgrad = wgrad.reshape(64, 2, 2 * K, H)
    pg, rows, other = back(xs, mixed, gg, projt, wgrad)
    weight_grad, pg, row_grad = sums(rows, seg, wgrad, other, pg)
    return (weight_grad, unturn_features(pg.T), row_grad)


def solution(mesh):
    placed = (
        P(("fsdp", "emb"), None),
        P(),
        P("fsdp", None),
        P(("fsdp", "emb"), None),
        P(None, ("fsdp", "emb")),
    )
    return jax.shard_map(
        on_device,
        mesh=mesh,
        in_specs=placed,
        out_specs=(P(("fsdp", "emb"), None), P(), P(("fsdp", "emb"), None)),
        check_vma=False,
    )
```

```python
import functools

import jax
import jax.numpy as jnp
from jax import lax
from jax.experimental import pallas as pl
from jax.experimental.pallas import tpu as pltpu
from jax.sharding import PartitionSpec as P

F = 256
E = 192
K = 96
H = 128
UNIQUE_CAP = 1024
PAIRS = F // 2
ROWS = 16
SCALE = E ** (-0.5)
BF = jnp.bfloat16
F32 = jnp.float32
VMEM_LIMIT = 60 * 1024 * 1024
NT = (((1,), (1,)), ((), ()))
TN = (((0,), (0,)), ((), ()))


def interleave(even, odd):
    width = even.shape[-1]
    both = jnp.concatenate([even.reshape(16, 8, width), odd.reshape(16, 8, width)], axis=1)
    return both.reshape(F, width)


def lower_half(rows):
    return lax.broadcasted_iota(jnp.int32, (rows, 128), 1) < 64


MESH = pl.DeviceIdType.MESH


def place():
    fsdp = lax.axis_index("fsdp")
    emb = lax.axis_index("emb")
    return fsdp // 4, fsdp % 4, emb // 2, emb % 2


def device(x, y, z, core):
    return (x * 4 + y, z * 2 + core)


def turn(at, d):
    return lax.rem(at + 4 + d, 4)


def greet(devices):
    barrier = pltpu.get_barrier_semaphore()
    for to in devices:
        pl.semaphore_signal(barrier, inc=1, device_id=to, device_id_type=MESH)
    pl.semaphore_wait(barrier, len(devices))


def remote(source, target, send, recv, to):
    return pltpu.make_async_remote_copy(
        src_ref=source,
        dst_ref=target,
        send_sem=send,
        recv_sem=recv,
        device_id=to,
        device_id_type=MESH,
    )


def front_kernel(
    x_ref, projt_ref, own_ref, cut_ref,
    xs_ref, mixed_ref, gram_ref, weight_ref, seg_ref,
    wide, turned, u_send, u_recv, v_send, v_recv, s_send, s_recv, g_send, g_recv, own_sem,
):
    step = pl.program_id(0)
    x, y, z, core = place()
    u = jnp.where(core == 0, x, y)
    v = jnp.where(core == 0, y, x)
    half = pl.ds(pl.multiple_of(core * (K // 2), K // 2), K // 2)
    other_half = pl.ds(pl.multiple_of((1 - core) * (K // 2), K // 2), K // 2)
    sibling = device(x, y, z, 1 - core)

    def at(du, dv, dz):
        moved_u, moved_v = turn(u, du), turn(v, dv)
        return device(
            jnp.where(core == 0, moved_u, moved_v),
            jnp.where(core == 0, moved_v, moved_u),
            turn(z, dz),
            core,
        )

    def block(du, dv):
        moved_u, moved_v = turn(u, du), turn(v, dv)
        return jnp.where(core == 0, moved_u * 4 + moved_v, moved_v * 4 + moved_u)

    def along_u(d):
        return remote(
            own_ref.at[half], weight_ref.at[block(0, 0), half], u_send.at[d - 1], u_recv.at[d - 1], at(d, 0, 0)
        )

    def from_u(d):
        there = weight_ref.at[block(-d, 0), half]
        return remote(there, there, u_send.at[d - 1], u_recv.at[d - 1], at(d, 0, 0))

    def along_v(d, du):
        there = weight_ref.at[block(du, 0), half]
        source = own_ref.at[half] if du == 0 else there
        return remote(source, there, v_send.at[d - 1, du], v_recv.at[d - 1, du], at(0, d, 0))

    def from_v(d, du):
        there = weight_ref.at[block(du, -d), half]
        return remote(there, there, v_send.at[d - 1, du], v_recv.at[d - 1, du], at(0, d, 0))

    def to_sibling(du, dv):
        there = weight_ref.at[block(du, dv), half]
        return remote(there, there, s_send.at[du, dv % 4], s_recv.at[du, dv % 4], sibling)

    def from_sibling(du, dv):
        first = jnp.where(core == 0, turn(x, dv), turn(x, du))
        second = jnp.where(core == 0, turn(y, du), turn(y, dv))
        there = weight_ref.at[first * 4 + second, other_half]
        return remote(there, there, s_send.at[du, dv % 4], s_recv.at[du, dv % 4], sibling)

    def segments_to(dv, dz):
        there = turn(v, dv) * 4 + turn(z, dz)
        return remote(
            cut_ref.at[there], seg_ref.at[v * 4 + z], g_send.at[dv, dz], g_recv.at[dv, dz], at(0, dv, dz)
        )

    def segments_from(dv, dz):
        there = seg_ref.at[turn(v, -dv) * 4 + turn(z, -dz)]
        return remote(there, there, g_send.at[dv, dz], g_recv.at[dv, dz], at(0, dv, dz))

    plane = [(dv, dz) for dv in range(4) for dz in range(4) if dv or dz]
    blocks = [(du, dv) for du in range(4) for dv in range(4) if du or dv]
    weight_copy = pltpu.make_async_copy(own_ref, weight_ref.at[block(0, 0)], own_sem.at[0])
    seg_copy = pltpu.make_async_copy(cut_ref.at[v * 4 + z], seg_ref.at[v * 4 + z], own_sem.at[1])

    @pl.when(step == 0)
    def _():
        greet([at(d, 0, 0) for d in range(1, 4)] + [at(0, dv, dz) for dv, dz in plane] + [sibling])
        for d in range(1, 4):
            along_u(d).start()
        for d in range(1, 4):
            along_v(d, 0).start()
        weight_copy.start()
        seg_copy.start()
        for dv, dz in plane:
            segments_to(dv, dz).start()

    @pl.when(step == 2)
    def _():
        for d in range(1, 4):
            from_u(d).wait_recv()
            for dv in range(1, 4):
                along_v(dv, 4 - d).start()
            to_sibling(4 - d, 0).start()

    @pl.when(step == pl.num_programs(0) - 1)
    def _():
        for du in range(4):
            for d in range(1, 4):
                from_v(d, du).wait_recv()
                to_sibling(du, 4 - d).start()

    def spread(step, carry):
        for inner in range(8):
            tile = step * 8 + inner
            wide[pl.ds(pl.multiple_of(tile * ROWS, ROWS), ROWS), :] = x_ref[
                :, pl.ds(pl.multiple_of(tile * 128, 128), 128)
            ].astype(F32)
        return carry

    lax.fori_loop(0, F * E // 1024, spread, 0)
    low = lower_half(PAIRS)

    def sample(b):
        a0 = wide[pl.ds(b, PAIRS, stride=3 * ROWS), :]
        a1 = wide[pl.ds(b + ROWS, PAIRS, stride=3 * ROWS), :]
        a2 = wide[pl.ds(b + 2 * ROWS, PAIRS, stride=3 * ROWS), :]
        r1 = pltpu.roll(a1, 64, 1)
        r2 = pltpu.roll(a2, 64, 1)
        even = jnp.concatenate([a0, jnp.where(low, a1, 0.0)], axis=1)
        odd = jnp.concatenate([jnp.where(low, r1, r2), jnp.where(low, r2, 0.0)], axis=1)
        xb = interleave(even, odd).astype(BF)
        xs_ref[b] = xb
        mixed = jnp.dot(projt_ref[...], xb, preferred_element_type=F32).astype(BF)
        mixed_ref[b] = mixed
        gram = lax.dot_general(mixed, xb, NT, preferred_element_type=F32) * SCALE
        turned[0, pl.ds(b, K, stride=ROWS), :] = gram[:, :128]
        turned[1, pl.ds(b, K, stride=ROWS), :] = gram[:, 128:]

    def samples(step, carry):
        for inner in range(4):
            sample(step * 4 + inner)
        return carry

    lax.fori_loop(0, ROWS // 4, samples, 0)
    for part in range(2):
        gram_ref[:, :, part * 128 : part * 128 + 128] = (
            turned[part].reshape(K, ROWS, 128).astype(BF)
        )

    @pl.when(step == pl.num_programs(0) - 1)
    def _():
        for du, dv in blocks:
            from_sibling(du, dv).wait_recv()
            to_sibling(du, dv).wait_send()
        for dv, dz in plane:
            segments_from(dv, dz).wait_recv()
            segments_to(dv, dz).wait_send()
        for d in range(1, 4):
            along_u(d).wait_send()
            for du in range(4):
                along_v(d, du).wait_send()
        weight_copy.wait()
        seg_copy.wait()


def front(x, projt, own, cut):
    batch = x.shape[0]
    any_space = pl.BlockSpec(memory_space=pl.ANY)
    dma = pltpu.SemaphoreType.DMA
    return pl.pallas_call(
        front_kernel,
        grid=(batch // ROWS,),
        in_specs=[
            pl.BlockSpec((ROWS, F * E), lambda i: (i, 0)),
            pl.BlockSpec((K, F), lambda i: (0, 0)),
            any_space,
            any_space,
        ],
        out_specs=[
            pl.BlockSpec((ROWS, F, 256), lambda i: (i, 0, 0)),
            pl.BlockSpec((ROWS, K, 256), lambda i: (i, 0, 0)),
            pl.BlockSpec((K, ROWS, F), lambda i: (0, i, 0)),
            any_space,
            any_space,
        ],
        out_shape=[
            jax.ShapeDtypeStruct((batch, F, 256), BF),
            jax.ShapeDtypeStruct((batch, K, 256), BF),
            jax.ShapeDtypeStruct((K, batch, F), BF),
            jax.ShapeDtypeStruct((16,) + own.shape, BF),
            jax.ShapeDtypeStruct(cut.shape, jnp.int32),
        ],
        scratch_shapes=[
            pltpu.VMEM((F * E // 128 * ROWS, 128), F32),
            pltpu.VMEM((2, K * ROWS, 128), F32),
            dma((3,)),
            dma((3,)),
            dma((3, 4)),
            dma((3, 4)),
            dma((4, 4)),
            dma((4, 4)),
            dma((4, 4)),
            dma((4, 4)),
            dma((2,)),
        ],
        compiler_params=pltpu.CompilerParams(
            vmem_limit_bytes=VMEM_LIMIT, collective_id=3, has_side_effects=True
        ),
        cost_estimate=pl.CostEstimate(
            flops=4 * batch * F * E * K, bytes_accessed=42_000_000, transcendentals=0
        ),
        name="front",
    )(x, projt, own, cut)


def middle_kernel(gram_ref, w_ref, cot_ref, wgrad_ref, gg_ref, turned):
    batch = gram_ref.shape[1]

    def weight(k):
        return w_ref[:, k].reshape(F, H)

    def product(step, total):
        for inner in range(8):
            k = step * 8 + inner
            total = total + jnp.dot(gram_ref[k], weight(k), preferred_element_type=F32)
        return total

    preact = lax.fori_loop(0, K // 8, product, jnp.zeros((batch, H), F32))
    sig = jax.nn.sigmoid(preact)
    slope = (cot_ref[...].astype(F32) * sig * (1.0 + preact * (1.0 - sig))).astype(BF)

    def gradients(step, carry):
        for inner in range(4):
            k = step * 4 + inner
            wgrad = lax.dot_general(gram_ref[k], slope, TN, preferred_element_type=F32)
            for block in range(16):
                for parity in range(2):
                    at = block * 16 + parity * 8
                    wgrad_ref[pl.ds(block * 8 * 2 * K + parity * K + k, 8, stride=2 * K), :] = wgrad[
                        at : at + 8
                    ]
            gg = lax.dot_general(slope, weight(k), NT, preferred_element_type=F32)
            turned[0, pl.ds(k, batch, stride=K), :] = gg[:, :128]
            turned[1, pl.ds(k, batch, stride=K), :] = gg[:, 128:]
        return carry

    lax.fori_loop(0, K // 4, gradients, 0)

    def pack(b, carry):
        at = pl.ds(pl.multiple_of(b * K, K), K)
        gg_ref[b] = jnp.concatenate([turned[0, at, :], turned[1, at, :]], axis=1).astype(BF)
        return carry

    lax.fori_loop(0, batch, pack, 0)


def middle(gram, w, cot):
    batch = gram.shape[1]
    whole = pl.BlockSpec(memory_space=pltpu.VMEM)
    return pl.pallas_call(
        middle_kernel,
        in_specs=[whole] * 3,
        out_specs=[whole] * 2,
        out_shape=[
            jax.ShapeDtypeStruct((F * K, H), F32),
            jax.ShapeDtypeStruct((batch, K, F), BF),
        ],
        scratch_shapes=[pltpu.VMEM((2, batch * K, 128), F32)],
        compiler_params=pltpu.CompilerParams(vmem_limit_bytes=VMEM_LIMIT),
        cost_estimate=pl.CostEstimate(
            flops=6 * batch * F * K * H, bytes_accessed=33_000_000, transcendentals=batch * H
        ),
        name="middle",
    )(gram, w, cot)


def back_kernel(
    xs_ref, mixed_ref, gg_ref, projt_ref, wgrad_ref,
    pg_ref, rows_ref, wz_ref,
    wide, stage, own, other, w2, w2_in, send_sem, recv_sem, own_sem, pair_sem, z_send, z_recv,
):
    low = lower_half(PAIRS)
    step = pl.program_id(0)
    steps = pl.num_programs(0)
    x, y, z, core = place()
    line = jnp.where(core == 0, x, y)
    slot = lax.rem(step, 2)
    sibling = device(x, y, z, 1 - core)

    def weight_copy():
        return remote(wgrad_ref.at[:, 1 - core], other, pair_sem.at[0], pair_sem.at[1], sibling)

    def weight_own():
        return pltpu.make_async_copy(wgrad_ref.at[:, core], own, pair_sem.at[2])

    def weight_z(d):
        there = turn(z, d)
        to = device(x, y, there, core)
        return remote(w2.at[there], w2_in.at[d - 1], z_send.at[d - 1], z_recv.at[d - 1], to)

    def copies(block, where):
        at_x = pl.ds((x * 2 + core) * 128 + block * ROWS, ROWS)
        at_y = pl.ds((y * 2 + core) * 128 + block * ROWS, ROWS)
        found = []
        for d in range(1, 4):
            tx = lax.rem(x + d, 4)
            ty = lax.rem(y + d, 4)
            for kind, group, rows, target in (
                (0, tx, at_x, device(tx, y, z, 0)),
                (1, 4 + ty, at_y, device(x, ty, z, 1)),
            ):
                found.append(
                    pltpu.make_async_remote_copy(
                        src_ref=stage.at[where, pl.ds(group * 16, 16)],
                        dst_ref=rows_ref.at[:, rows],
                        send_sem=send_sem.at[where, kind * 3 + d - 1],
                        recv_sem=recv_sem.at[block, d * 2 + core],
                        device_id=target,
                        device_id_type=MESH,
                    )
                )
        group = jnp.where(core == 0, 4 + y, x)
        there = pl.ds((jnp.where(core == 0, y, x) * 2 + core) * 128 + block * ROWS, ROWS)
        found.append(
            pltpu.make_async_remote_copy(
                src_ref=stage.at[where, pl.ds(group * 16, 16)],
                dst_ref=rows_ref.at[:, there],
                send_sem=send_sem.at[where, 6],
                recv_sem=recv_sem.at[block, 0],
                device_id=sibling,
                device_id_type=MESH,
            )
        )
        return found

    def own_copy(block, where):
        group = jnp.where(core == 0, x, 4 + y)
        here = pl.ds((line * 2 + core) * 128 + block * ROWS, ROWS)
        return pltpu.make_async_copy(
            stage.at[where, pl.ds(group * 16, 16)], rows_ref.at[:, here], own_sem.at[where]
        )

    @pl.when(step == 0)
    def _():
        pg_ref[...] = jnp.zeros_like(pg_ref)
        senders = [sibling]
        for d in range(1, 4):
            from_x = jnp.where(core == 0, lax.rem(x + d, 4), x)
            from_y = jnp.where(core == 0, y, lax.rem(y + d, 4))
            senders += [device(from_x, from_y, z, other_core) for other_core in range(2)]
            senders.append(device(x, y, turn(z, d), core))
        greet(senders)
        weight_copy().start()
        weight_own().start()

    @pl.when(step == 2)
    def _():
        weight_own().wait()
        weight_copy().wait_send()
        weight_copy().wait_recv()

        def pair_sum(n, carry):
            to_z, first, second = n // 16, (n // 4) % 4, n % 4
            source = jnp.where(core == 0, first * 4 + second, second * 4 + first) * 4 + to_z
            w2[to_z, n % 16] = (own[source] + other[source]).astype(BF)
            return carry

        lax.fori_loop(0, 64, pair_sum, 0)
        for d in range(1, 4):
            weight_z(d).start()

    def sample(b):
        xb = xs_ref[b]
        gg = gg_ref[b]
        mg = jnp.dot(gg, xb, preferred_element_type=F32).astype(BF)
        pg = lax.dot_general(mg, xb, NT, preferred_element_type=F32)
        left = jnp.concatenate([gg, projt_ref[...]], axis=0)
        right = jnp.concatenate([mixed_ref[b], mg], axis=0)
        fg = lax.dot_general(left, right, TN, preferred_element_type=F32) * SCALE
        fg = fg.reshape(16, 2, 8, 256)
        even = fg[:, 0].reshape(PAIRS, 256)
        odd = fg[:, 1].reshape(PAIRS, 256)
        r0 = pltpu.roll(odd[:, :128], 64, 1)
        r1 = pltpu.roll(odd[:, 128:], 64, 1)
        wide[pl.ds(b, PAIRS, stride=3 * ROWS), :] = even[:, :128]
        wide[pl.ds(b + ROWS, PAIRS, stride=3 * ROWS), :] = jnp.where(low, even[:, 128:], r0)
        wide[pl.ds(b + 2 * ROWS, PAIRS, stride=3 * ROWS), :] = jnp.where(low, r0, r1)
        return pg

    def samples(turn, total):
        for inner in range(4):
            total = total + sample(turn * 4 + inner)
        return total

    pg_ref[...] += lax.fori_loop(0, ROWS // 4, samples, jnp.zeros((K, F), F32)) * SCALE

    @pl.when(step >= 2)
    def _():
        for copy in copies(step - 2, slot):
            copy.wait_send()
        own_copy(step - 2, slot).wait()

    def pack(q, carry):
        for kind in range(2):
            for last in range(4):
                first, second = q // 4, q % 4
                if kind == 0:
                    owner = ((first * 4 + second) * 4 + last) * 2
                else:
                    owner = ((second * 4 + first) * 4 + last) * 2 + 1
                for tile in range(3):
                    at = pl.ds(pl.multiple_of(owner * 3 * ROWS + tile * ROWS, ROWS), ROWS)
                    stage[slot, kind * 64 + q * 4 + last, :, tile * 128 : tile * 128 + 128] = wide[
                        at, :
                    ].astype(BF)
        return carry

    lax.fori_loop(0, 16, pack, 0)
    for copy in copies(step, slot):
        copy.start()
    own_copy(step, slot).start()

    @pl.when(step == steps - 1)
    def _():
        for block, where in ((step - 1, 1 - slot), (step, slot)):
            for copy in copies(block, where):
                copy.wait_send()
            own_copy(block, where).wait()
        for d in range(1, 4):
            weight_z(d).wait_recv()

        def sum_z(n, carry):
            total = w2[z, n].astype(F32) + w2_in[0, n].astype(F32)
            total = total + (w2_in[1, n].astype(F32) + w2_in[2, n].astype(F32))
            wz_ref[n] = total.astype(BF)
            return carry

        lax.fori_loop(0, 16, sum_z, 0)
        for d in range(1, 4):
            weight_z(d).wait_send()

        def arrived(block, carry):
            def wait(sender, sem):
                at = pl.ds(sender * 128 + block * ROWS, ROWS)
                pltpu.make_async_remote_copy(
                    src_ref=stage.at[0, pl.ds(0, 16)],
                    dst_ref=rows_ref.at[:, at],
                    send_sem=send_sem.at[0, 0],
                    recv_sem=recv_sem.at[block, sem],
                    device_id=sibling,
                    device_id_type=MESH,
                ).wait_recv()

            wait(line * 2 + 1 - core, 0)
            for d in range(1, 4):
                for other in range(2):
                    wait(lax.rem(line + 4 - d, 4) * 2 + other, d * 2 + other)
            return carry

        lax.fori_loop(0, steps, arrived, 0)


def back(xs, mixed, gg, projt, wgrad):
    batch = xs.shape[0]
    any_space = pl.BlockSpec(memory_space=pl.ANY)
    return pl.pallas_call(
        back_kernel,
        grid=(batch // ROWS,),
        in_specs=[
            pl.BlockSpec((ROWS, F, 256), lambda i: (i, 0, 0)),
            pl.BlockSpec((ROWS, K, 256), lambda i: (i, 0, 0)),
            pl.BlockSpec((ROWS, K, F), lambda i: (i, 0, 0)),
            pl.BlockSpec((K, F), lambda i: (0, 0)),
            any_space,
        ],
        out_specs=[
            pl.BlockSpec((K, F), lambda i: (0, 0)),
            any_space,
            pl.BlockSpec((16, 2 * K, H), lambda i: (0, 0, 0)),
        ],
        out_shape=[
            jax.ShapeDtypeStruct((K, F), F32),
            jax.ShapeDtypeStruct((16, 8 * batch, 2 * E), BF),
            jax.ShapeDtypeStruct((16, 2 * K, H), BF),
        ],
        scratch_shapes=[
            pltpu.VMEM((F * E // 128 * ROWS, 128), F32),
            pltpu.VMEM((2, PAIRS, ROWS, 2 * E), BF),
            pltpu.VMEM((64, 2 * K, H), F32),
            pltpu.VMEM((64, 2 * K, H), F32),
            pltpu.VMEM((4, 16, 2 * K, H), BF),
            pltpu.VMEM((3, 16, 2 * K, H), BF),
            pltpu.SemaphoreType.DMA((2, 7)),
            pltpu.SemaphoreType.DMA((batch // ROWS, 8)),
            pltpu.SemaphoreType.DMA((2,)),
            pltpu.SemaphoreType.DMA((3,)),
            pltpu.SemaphoreType.DMA((3,)),
            pltpu.SemaphoreType.DMA((3,)),
        ],
        compiler_params=pltpu.CompilerParams(
            vmem_limit_bytes=VMEM_LIMIT, collective_id=1, has_side_effects=True
        ),
        cost_estimate=pl.CostEstimate(
            flops=8 * batch * F * E * K, bytes_accessed=42_000_000, transcendentals=0
        ),
        name="back",
    )(xs, mixed, gg, projt, wgrad)


SLOT_BLOCK = 256
HALF = UNIQUE_CAP // 2
FIRST = 128
ORDER = (1, 2, 3, 0)


def sums_kernel(
    rows_ref, seg_ref, wz_ref, pg_ref,
    wout_ref, pout_ref, out_ref,
    data, table, az, bv, sum_a, sum_b, va, zb, w3_in, w4, w4_in, pu, pv, pz, pc,
    load_sem, az_send, az_recv, bv_send, bv_recv, va_send, va_recv, zb_send, zb_recv,
    w_send, w_recv, p_send, p_recv,
):
    x, y, z, core = place()
    u = jnp.where(core == 0, x, y)
    v = jnp.where(core == 0, y, x)
    low = lower_half(SLOT_BLOCK)

    def at_u(d):
        moved = turn(u, d)
        return device(jnp.where(core == 0, moved, x), jnp.where(core == 0, y, moved), z, core)

    def at_v(d):
        moved = turn(v, d)
        return device(jnp.where(core == 0, x, moved), jnp.where(core == 0, moved, y), z, core)

    def at_z(d):
        return device(x, y, turn(z, d), core)

    sibling = device(x, y, z, 1 - core)

    def load(dz, dv):
        j = turn(v, dv) * 4 + turn(z, dz)
        return pltpu.make_async_copy(rows_ref.at[j], data.at[dz, dv], load_sem.at[dz, dv])

    for dz in ORDER:
        for dv in ORDER:
            load(dz, dv).start()

    greet([to(d) for d in range(1, 4) for to in (at_u, at_v, at_z)] + [sibling])

    def spread(buffer, mine, stage, to):
        return [
            remote(buffer.at[mine], buffer.at[mine], p_send.at[stage, d - 1], p_recv.at[stage, d - 1], to(d))
            for d in range(1, 4)
        ]

    def gathered(buffer, mine, stage, to):
        for d in range(1, 4):
            there = buffer.at[turn(mine, -d)]
            remote(there, there, p_send.at[stage, d - 1], p_recv.at[stage, d - 1], to(d)).wait_recv()
        return (buffer[0] + buffer[1]) + (buffer[2] + buffer[3])

    def start(copies):
        for copy in copies:
            copy.start()
        return copies

    def send_a(dz, dv):
        return remote(
            table.at[dz, dv, pl.ds(0, FIRST)],
            az.at[dz - 1, dv],
            az_send.at[dz - 1, dv],
            az_recv.at[dz - 1, dv],
            at_z(dz),
        )

    def send_b(dv, dz):
        return remote(
            table.at[dz, dv, pl.ds(FIRST, HALF - FIRST)],
            bv.at[dv - 1, dz],
            bv_send.at[dv - 1, dz],
            bv_recv.at[dv - 1, dz],
            at_v(dv),
        )

    def second_a(dv):
        return remote(sum_a.at[dv], va.at[dv - 1], va_send.at[dv - 1], va_recv.at[dv - 1], at_v(dv))

    def second_b(dz):
        return remote(sum_b.at[dz], zb.at[dz - 1], zb_send.at[dz - 1], zb_recv.at[dz - 1], at_z(dz))

    def one_table(dz, dv):
        load(dz, dv).wait()
        j = turn(v, dv) * 4 + turn(z, dz)
        slot = lax.broadcasted_iota(jnp.int32, (SLOT_BLOCK, 8 * 128), 0)

        def part(block, parity):
            seg = seg_ref[j, parity : parity + 1, :] - block * SLOT_BLOCK
            hot = jnp.where(slot == seg, 1.0, 0.0).astype(BF)
            found = jnp.dot(
                hot, data[dz, dv, :, parity * 128 : parity * 128 + 256], preferred_element_type=F32
            )
            return found[:, :128], found[:, 128:]

        for block in range(HALF // SLOT_BLOCK):
            at = pl.ds(block * SLOT_BLOCK, SLOT_BLOCK)
            even0, even1 = part(block, 0)
            odd0, odd1 = part(block, 1)
            r0 = pltpu.roll(odd0, 64, 1)
            r1 = pltpu.roll(odd1, 64, 1)
            table[dz, dv, at, 0:128] = (even0 + jnp.where(low, r0, r1)).astype(BF)
            first = even1 + r1
            even0, even1 = part(block + HALF // SLOT_BLOCK, 0)
            odd0, odd1 = part(block + HALF // SLOT_BLOCK, 1)
            r0 = pltpu.roll(even0, 64, 1)
            r1 = pltpu.roll(even1, 64, 1)
            table[dz, dv, at, 128:256] = jnp.where(low, first, r0 + odd0).astype(BF)
            table[dz, dv, at, 256:384] = (jnp.where(low, r0, r1) + odd1).astype(BF)

    def tables(dz):
        def one(turns, carry):
            dv = lax.rem(turns + 1, 4)
            one_table(dz, dv)
            if dz > 0:
                send_a(dz, dv).start()

            @pl.when(dv > 0)
            def _():
                send_b(dv, dz).start()

            return carry

        lax.fori_loop(0, 4, one, 0)

    def add_four(first, second, third, fourth, target, size):
        rows = first.shape[0]

        def one(n, carry):
            at = pl.ds(pl.multiple_of(n * size, size), size)
            total = (first[at].astype(F32) + second[at].astype(F32)) + (
                third[at].astype(F32) + fourth[at].astype(F32)
            )
            target[at] = total.astype(target.dtype)
            return carry

        lax.fori_loop(0, rows // size, one, 0)

    def total_b(dz):
        for dv in range(1, 4):
            send_b(dv, dz).wait_recv()
        mine = table.at[dz, 0, pl.ds(FIRST, HALF - FIRST)]
        add_four(mine, bv.at[0, dz], bv.at[1, dz], bv.at[2, dz], sum_b.at[dz], 64)
        if dz > 0:
            second_b(dz).start()

    def total_a(dv):
        for dz in range(1, 4):
            send_a(dz, dv).wait_recv()
        mine = table.at[0, dv, pl.ds(0, FIRST)]
        add_four(mine, az.at[0, dv], az.at[1, dv], az.at[2, dv], sum_a.at[dv], 64)
        if dv > 0:
            second_a(dv).start()

    def w_copies(source, arrive, stage, to, line, size):
        return [
            remote(
                source.at[pl.ds(turn(line, d) * size, size)],
                arrive.at[d - 1],
                w_send.at[stage, d - 1],
                w_recv.at[stage, d - 1],
                to(d),
            )
            for d in range(1, 4)
        ]

    pu[u] = pg_ref[...]
    p0 = start(spread(pu, u, 0, at_u))
    s3 = start(w_copies(wz_ref, w3_in, 0, at_u, u, 4))
    tables(1)
    pv[v] = gathered(pu, u, 0, at_u)
    p1 = start(spread(pv, v, 1, at_v))
    for copy in s3:
        copy.wait_recv()
    add_four(wz_ref.at[pl.ds(u * 4, 4)], w3_in.at[0], w3_in.at[1], w3_in.at[2], w4, 1)
    s4 = start(w_copies(w4, w4_in, 1, at_v, v, 1))
    tables(2)
    total_b(1)
    pz[z] = gathered(pv, v, 1, at_v)
    p2 = start(spread(pz, z, 2, at_z))
    tables(3)
    total_b(2)
    pc[core] = gathered(pz, z, 2, at_z)
    p3 = remote(pc.at[core], pc.at[core], p_send.at[3, 0], p_recv.at[3, 0], sibling)
    p3.start()
    for copy in s4:
        copy.wait_recv()
    total = w4[v].astype(F32) + w4_in[0, 0].astype(F32)
    wout_ref[...] = total + (w4_in[1, 0].astype(F32) + w4_in[2, 0].astype(F32))
    tables(0)
    total_b(3)
    for dv in ORDER:
        total_a(dv)
    total_b(0)
    remote(pc.at[1 - core], pc.at[1 - core], p_send.at[3, 0], p_recv.at[3, 0], sibling).wait_recv()
    pout_ref[...] = pc[0] + pc[1]

    def finish(mine, others, start_row, rows):
        def one(part, carry):
            at = pl.ds(pl.multiple_of(part * 64, 64), 64)
            before = pl.ds(pl.multiple_of(part * 64 + start_row, 64), 64)
            after = pl.ds(pl.multiple_of(part * 64 + start_row + HALF, 64), 64)
            total = mine[at, :].astype(F32) + others[0, at].astype(F32)
            total = total + (others[1, at].astype(F32) + others[2, at].astype(F32))
            out_ref[before, :] = total[:, :E]
            r1 = pltpu.roll(total[:, 128:256], 64, 1)
            r2 = pltpu.roll(total[:, 256:], 64, 1)
            out_ref[after, :128] = jnp.where(lower_half(64), r1, r2)
            out_ref[after, 128:] = r2[:, :64]
            return carry

        lax.fori_loop(0, rows // 64, one, 0)

    for d in range(1, 4):
        second_a(d).wait_recv()
    finish(sum_a.at[0], va, 0, FIRST)
    for d in range(1, 4):
        second_b(d).wait_recv()
    finish(sum_b.at[0], zb, FIRST, HALF - FIRST)

    for copy in p0 + p1 + p2 + [p3] + s3 + s4:
        copy.wait_send()
    for d in range(1, 4):
        second_a(d).wait_send()
        second_b(d).wait_send()
        for n in range(4):
            send_a(d, n).wait_send()
            send_b(d, n).wait_send()


def sums(rows, seg, wz, pg):
    any_space = pl.BlockSpec(memory_space=pl.ANY)
    whole = pl.BlockSpec(memory_space=pltpu.VMEM)
    dma = pltpu.SemaphoreType.DMA
    rest = HALF - FIRST
    return pl.pallas_call(
        sums_kernel,
        in_specs=[any_space, whole, whole, whole],
        out_specs=[whole] * 3,
        out_shape=[
            jax.ShapeDtypeStruct((2 * K, H), F32),
            jax.ShapeDtypeStruct((K, F), F32),
            jax.ShapeDtypeStruct((UNIQUE_CAP, E), F32),
        ],
        scratch_shapes=[
            pltpu.VMEM((4, 4) + rows.shape[1:], BF),
            pltpu.VMEM((4, 4, HALF, 2 * E), BF),
            pltpu.VMEM((3, 4, FIRST, 2 * E), BF),
            pltpu.VMEM((3, 4, rest, 2 * E), BF),
            pltpu.VMEM((4, FIRST, 2 * E), BF),
            pltpu.VMEM((4, rest, 2 * E), BF),
            pltpu.VMEM((3, FIRST, 2 * E), BF),
            pltpu.VMEM((3, rest, 2 * E), BF),
            pltpu.VMEM((3, 4, 2 * K, H), BF),
            pltpu.VMEM((4, 2 * K, H), BF),
            pltpu.VMEM((3, 1, 2 * K, H), BF),
            pltpu.VMEM((4, K, F), F32),
            pltpu.VMEM((4, K, F), F32),
            pltpu.VMEM((4, K, F), F32),
            pltpu.VMEM((2, K, F), F32),
            dma((4, 4)),
            dma((3, 4)),
            dma((3, 4)),
            dma((3, 4)),
            dma((3, 4)),
            dma((3,)),
            dma((3,)),
            dma((3,)),
            dma((3,)),
            dma((2, 3)),
            dma((2, 3)),
            dma((4, 3)),
            dma((4, 3)),
        ],
        compiler_params=pltpu.CompilerParams(
            vmem_limit_bytes=VMEM_LIMIT, collective_id=2, has_side_effects=True
        ),
        cost_estimate=pl.CostEstimate(
            flops=16 * 4 * UNIQUE_CAP * 1024 * 256, bytes_accessed=30_000_000, transcendentals=0
        ),
        name="sums",
    )(rows, seg, wz, pg)


def turn_features(a):
    rest = a.shape[1:]
    return a.reshape((-1, 8, 2) + rest).swapaxes(1, 2).reshape(a.shape)


def unturn_features(a):
    rest = a.shape[1:]
    return a.reshape((-1, 2, 8) + rest).swapaxes(1, 2).reshape(a.shape)


def cut_segments(segments):
    core = lax.axis_index("emb") % 2
    seg = segments.T.reshape(2, 4, 4, 4, 2, 128)
    along_x = seg.transpose(2, 3, 0, 1, 4, 5).reshape(16, 2, 1024)
    along_y = seg.transpose(1, 3, 0, 2, 4, 5).reshape(16, 2, 1024)
    return jnp.where(core == 0, along_x, along_y)


def on_device(pooled, projection, out_weight, cotangent, segments):
    own = turn_features(out_weight.reshape(-1, K, H)).swapaxes(0, 1)
    projt = turn_features(projection).T
    xs, mixed, gram, weight, seg = front(pooled, projt, own, cut_segments(segments))
    wgrad, gg = middle(gram, weight, cotangent)
    wgrad = wgrad.reshape(64, 2, 2 * K, H)
    pg, rows, wz = back(xs, mixed, gg, projt, wgrad)
    weight_grad, pg, row_grad = sums(rows, seg, wz, pg)
    return (weight_grad, unturn_features(pg.T), row_grad)


def solution(mesh):
    placed = (
        P(("fsdp", "emb"), None),
        P(),
        P("fsdp", None),
        P(("fsdp", "emb"), None),
        P(None, ("fsdp", "emb")),
    )
    return jax.shard_map(
        on_device,
        mesh=mesh,
        in_specs=placed,
        out_specs=(P(("fsdp", "emb"), None), P(), P(("fsdp", "emb"), None)),
        check_vma=False,
    )
```

```python
import functools

import jax
import jax.numpy as jnp
from jax import lax
from jax.experimental import pallas as pl
from jax.experimental.pallas import tpu as pltpu
from jax.sharding import PartitionSpec as P

F = 256
E = 192
K = 96
H = 128
UNIQUE_CAP = 1024
PAIRS = F // 2
ROWS = 16
SCALE = E ** (-0.5)
BF = jnp.bfloat16
F32 = jnp.float32
VMEM_LIMIT = 60 * 1024 * 1024
NT = (((1,), (1,)), ((), ()))
TN = (((0,), (0,)), ((), ()))


def interleave(even, odd):
    width = even.shape[-1]
    both = jnp.concatenate([even.reshape(16, 8, width), odd.reshape(16, 8, width)], axis=1)
    return both.reshape(F, width)


def lower_half(rows):
    return lax.broadcasted_iota(jnp.int32, (rows, 128), 1) < 64


MESH = pl.DeviceIdType.MESH


def place():
    fsdp = lax.axis_index("fsdp")
    emb = lax.axis_index("emb")
    return fsdp // 4, fsdp % 4, emb // 2, emb % 2


def device(x, y, z, core):
    return (x * 4 + y, z * 2 + core)


def turn(at, d):
    return lax.rem(at + 4 + d, 4)


def greet(devices):
    barrier = pltpu.get_barrier_semaphore()
    for to in devices:
        pl.semaphore_signal(barrier, inc=1, device_id=to, device_id_type=MESH)
    pl.semaphore_wait(barrier, len(devices))


def remote(source, target, send, recv, to):
    return pltpu.make_async_remote_copy(
        src_ref=source,
        dst_ref=target,
        send_sem=send,
        recv_sem=recv,
        device_id=to,
        device_id_type=MESH,
    )


def front_kernel(
    x_ref, projt_ref, own_ref, cut_ref,
    xs_ref, mixed_ref, gram_ref, weight_ref, seg_ref,
    wide, turned, u_send, u_recv, v_send, v_recv, s_send, s_recv, g_send, g_recv, own_sem,
):
    step = pl.program_id(0)
    x, y, z, core = place()
    u = jnp.where(core == 0, x, y)
    v = jnp.where(core == 0, y, x)
    half = pl.ds(pl.multiple_of(core * (K // 2), K // 2), K // 2)
    other_half = pl.ds(pl.multiple_of((1 - core) * (K // 2), K // 2), K // 2)
    sibling = device(x, y, z, 1 - core)

    def at(du, dv, dz):
        moved_u, moved_v = turn(u, du), turn(v, dv)
        return device(
            jnp.where(core == 0, moved_u, moved_v),
            jnp.where(core == 0, moved_v, moved_u),
            turn(z, dz),
            core,
        )

    def block(du, dv):
        moved_u, moved_v = turn(u, du), turn(v, dv)
        return jnp.where(core == 0, moved_u * 4 + moved_v, moved_v * 4 + moved_u)

    def along_u(d):
        return remote(
            own_ref.at[half], weight_ref.at[block(0, 0), half], u_send.at[d - 1], u_recv.at[d - 1], at(d, 0, 0)
        )

    def from_u(d):
        there = weight_ref.at[block(-d, 0), half]
        return remote(there, there, u_send.at[d - 1], u_recv.at[d - 1], at(d, 0, 0))

    def along_v(d, du):
        there = weight_ref.at[block(du, 0), half]
        source = own_ref.at[half] if du == 0 else there
        return remote(source, there, v_send.at[d - 1, du], v_recv.at[d - 1, du], at(0, d, 0))

    def from_v(d, du):
        there = weight_ref.at[block(du, -d), half]
        return remote(there, there, v_send.at[d - 1, du], v_recv.at[d - 1, du], at(0, d, 0))

    def to_sibling(du, dv):
        there = weight_ref.at[block(du, dv), half]
        return remote(there, there, s_send.at[du, dv % 4], s_recv.at[du, dv % 4], sibling)

    def from_sibling(du, dv):
        first = jnp.where(core == 0, turn(x, dv), turn(x, du))
        second = jnp.where(core == 0, turn(y, du), turn(y, dv))
        there = weight_ref.at[first * 4 + second, other_half]
        return remote(there, there, s_send.at[du, dv % 4], s_recv.at[du, dv % 4], sibling)

    def segments_to(dv, dz):
        there = turn(v, dv) * 4 + turn(z, dz)
        return remote(
            cut_ref.at[there], seg_ref.at[v * 4 + z], g_send.at[dv, dz], g_recv.at[dv, dz], at(0, dv, dz)
        )

    def segments_from(dv, dz):
        there = seg_ref.at[turn(v, -dv) * 4 + turn(z, -dz)]
        return remote(there, there, g_send.at[dv, dz], g_recv.at[dv, dz], at(0, dv, dz))

    plane = [(dv, dz) for dv in range(4) for dz in range(4) if dv or dz]
    blocks = [(du, dv) for du in range(4) for dv in range(4) if du or dv]
    weight_copy = pltpu.make_async_copy(own_ref, weight_ref.at[block(0, 0)], own_sem.at[0])
    seg_copy = pltpu.make_async_copy(cut_ref.at[v * 4 + z], seg_ref.at[v * 4 + z], own_sem.at[1])

    @pl.when(step == 0)
    def _():
        greet([at(d, 0, 0) for d in range(1, 4)] + [at(0, dv, dz) for dv, dz in plane] + [sibling])
        for d in range(1, 4):
            along_u(d).start()
        for d in range(1, 4):
            along_v(d, 0).start()
        weight_copy.start()
        seg_copy.start()
        for dv, dz in plane:
            segments_to(dv, dz).start()

    @pl.when(step == 1)
    def _():
        for d in (1, 3, 2):
            from_u(d).wait_recv()
            for dv in range(1, 4):
                along_v(dv, 4 - d).start()
            to_sibling(4 - d, 0).start()

    for when, arrived in ((3, (0,)), (6, (1, 3)), (7, (2,))):

        @pl.when(step == when)
        def _(arrived=arrived):
            for du in arrived:
                for d in range(1, 4):
                    from_v(d, du).wait_recv()
                    to_sibling(du, 4 - d).start()

    def spread(step, carry):
        for inner in range(8):
            tile = step * 8 + inner
            wide[pl.ds(pl.multiple_of(tile * ROWS, ROWS), ROWS), :] = x_ref[
                :, pl.ds(pl.multiple_of(tile * 128, 128), 128)
            ].astype(F32)
        return carry

    lax.fori_loop(0, F * E // 1024, spread, 0)
    low = lower_half(PAIRS)

    def sample(b):
        a0 = wide[pl.ds(b, PAIRS, stride=3 * ROWS), :]
        a1 = wide[pl.ds(b + ROWS, PAIRS, stride=3 * ROWS), :]
        a2 = wide[pl.ds(b + 2 * ROWS, PAIRS, stride=3 * ROWS), :]
        r1 = pltpu.roll(a1, 64, 1)
        r2 = pltpu.roll(a2, 64, 1)
        even = jnp.concatenate([a0, jnp.where(low, a1, 0.0)], axis=1)
        odd = jnp.concatenate([jnp.where(low, r1, r2), jnp.where(low, r2, 0.0)], axis=1)
        xb = interleave(even, odd).astype(BF)
        xs_ref[b] = xb
        mixed = jnp.dot(projt_ref[...], xb, preferred_element_type=F32).astype(BF)
        mixed_ref[b] = mixed
        gram = lax.dot_general(mixed, xb, NT, preferred_element_type=F32) * SCALE
        turned[0, pl.ds(b, K, stride=ROWS), :] = gram[:, :128]
        turned[1, pl.ds(b, K, stride=ROWS), :] = gram[:, 128:]

    def samples(step, carry):
        for inner in range(4):
            sample(step * 4 + inner)
        return carry

    lax.fori_loop(0, ROWS // 4, samples, 0)
    for part in range(2):
        gram_ref[:, :, part * 128 : part * 128 + 128] = (
            turned[part].reshape(K, ROWS, 128).astype(BF)
        )

    @pl.when(step == pl.num_programs(0) - 1)
    def _():
        for du, dv in blocks:
            from_sibling(du, dv).wait_recv()
            to_sibling(du, dv).wait_send()
        for dv, dz in plane:
            segments_from(dv, dz).wait_recv()
            segments_to(dv, dz).wait_send()
        for d in range(1, 4):
            along_u(d).wait_send()
            for du in range(4):
                along_v(d, du).wait_send()
        weight_copy.wait()
        seg_copy.wait()


def front(x, projt, own, cut):
    batch = x.shape[0]
    any_space = pl.BlockSpec(memory_space=pl.ANY)
    dma = pltpu.SemaphoreType.DMA
    return pl.pallas_call(
        front_kernel,
        grid=(batch // ROWS,),
        in_specs=[
            pl.BlockSpec((ROWS, F * E), lambda i: (i, 0)),
            pl.BlockSpec((K, F), lambda i: (0, 0)),
            any_space,
            any_space,
        ],
        out_specs=[
            pl.BlockSpec((ROWS, F, 256), lambda i: (i, 0, 0)),
            pl.BlockSpec((ROWS, K, 256), lambda i: (i, 0, 0)),
            pl.BlockSpec((K, ROWS, F), lambda i: (0, i, 0)),
            any_space,
            any_space,
        ],
        out_shape=[
            jax.ShapeDtypeStruct((batch, F, 256), BF),
            jax.ShapeDtypeStruct((batch, K, 256), BF),
            jax.ShapeDtypeStruct((K, batch, F), BF),
            jax.ShapeDtypeStruct((16,) + own.shape, BF),
            jax.ShapeDtypeStruct(cut.shape, jnp.int32),
        ],
        scratch_shapes=[
            pltpu.VMEM((F * E // 128 * ROWS, 128), F32),
            pltpu.VMEM((2, K * ROWS, 128), F32),
            dma((3,)),
            dma((3,)),
            dma((3, 4)),
            dma((3, 4)),
            dma((4, 4)),
            dma((4, 4)),
            dma((4, 4)),
            dma((4, 4)),
            dma((2,)),
        ],
        compiler_params=pltpu.CompilerParams(
            vmem_limit_bytes=VMEM_LIMIT, collective_id=3, has_side_effects=True
        ),
        cost_estimate=pl.CostEstimate(
            flops=4 * batch * F * E * K, bytes_accessed=42_000_000, transcendentals=0
        ),
        name="front",
    )(x, projt, own, cut)


CHUNKS = 8
DEPTH = K // CHUNKS


def back_kernel(
    xs_ref, mixed_ref, projt_ref, gram_any, w_any, cot_ref,
    pg_ref, rows_ref, wz_ref,
    wide, stage, gram, w, slope_ref, gg_all, turned, give, other, w2, w2_in,
    send_sem, recv_sem, own_sem, pair_sem, z_send, z_recv, gram_sem, w_sem,
):
    low = lower_half(PAIRS)
    step = pl.program_id(0)
    steps = pl.num_programs(0)
    x, y, z, core = place()
    line = jnp.where(core == 0, x, y)
    slot = lax.rem(step, 2)
    sibling = device(x, y, z, 1 - core)

    batch = gram.shape[1]

    def loads(n):
        at = pl.ds(n * DEPTH, DEPTH)
        return (
            pltpu.make_async_copy(gram_any.at[at], gram.at[at], gram_sem.at[n]),
            pltpu.make_async_copy(w_any.at[:, at], w.at[:, at], w_sem.at[n]),
        )

    def weight_copy():
        return remote(give, other, pair_sem.at[0], pair_sem.at[1], sibling)

    def weight_z(d):
        there = turn(z, d)
        to = device(x, y, there, core)
        return remote(w2.at[there], w2_in.at[d - 1], z_send.at[d - 1], z_recv.at[d - 1], to)

    def copies(block, where):
        at_x = pl.ds((x * 2 + core) * 128 + block * ROWS, ROWS)
        at_y = pl.ds((y * 2 + core) * 128 + block * ROWS, ROWS)
        found = []
        for d in range(1, 4):
            tx = lax.rem(x + d, 4)
            ty = lax.rem(y + d, 4)
            for kind, group, rows, target in (
                (0, tx, at_x, device(tx, y, z, 0)),
                (1, 4 + ty, at_y, device(x, ty, z, 1)),
            ):
                found.append(
                    pltpu.make_async_remote_copy(
                        src_ref=stage.at[where, pl.ds(group * 16, 16)],
                        dst_ref=rows_ref.at[:, rows],
                        send_sem=send_sem.at[where, kind * 3 + d - 1],
                        recv_sem=recv_sem.at[block, d * 2 + core],
                        device_id=target,
                        device_id_type=MESH,
                    )
                )
        group = jnp.where(core == 0, 4 + y, x)
        there = pl.ds((jnp.where(core == 0, y, x) * 2 + core) * 128 + block * ROWS, ROWS)
        found.append(
            pltpu.make_async_remote_copy(
                src_ref=stage.at[where, pl.ds(group * 16, 16)],
                dst_ref=rows_ref.at[:, there],
                send_sem=send_sem.at[where, 6],
                recv_sem=recv_sem.at[block, 0],
                device_id=sibling,
                device_id_type=MESH,
            )
        )
        return found

    def own_copy(block, where):
        group = jnp.where(core == 0, x, 4 + y)
        here = pl.ds((line * 2 + core) * 128 + block * ROWS, ROWS)
        return pltpu.make_async_copy(
            stage.at[where, pl.ds(group * 16, 16)], rows_ref.at[:, here], own_sem.at[where]
        )

    @pl.when(step == 0)
    def _():
        pg_ref[...] = jnp.zeros_like(pg_ref)
        senders = [sibling]
        for d in range(1, 4):
            from_x = jnp.where(core == 0, lax.rem(x + d, 4), x)
            from_y = jnp.where(core == 0, y, lax.rem(y + d, 4))
            senders += [device(from_x, from_y, z, other_core) for other_core in range(2)]
            senders.append(device(x, y, turn(z, d), core))
        for n in range(CHUNKS):
            for copy in loads(n):
                copy.start()
        greet(senders)

        def product(n, total):
            for copy in loads(n):
                copy.wait()
            for inner in range(DEPTH):
                k = n * DEPTH + inner
                total = total + jnp.dot(
                    gram[k], w[:, k].reshape(F, H), preferred_element_type=F32
                )
            return total

        preact = lax.fori_loop(0, CHUNKS, product, jnp.zeros((batch, H), F32))
        sig = jax.nn.sigmoid(preact)
        slope_ref[...] = (
            cot_ref[...].astype(F32) * sig * (1.0 + preact * (1.0 - sig))
        ).astype(BF)

        for part in range(2):

            def gram_grad(turns, carry):
                for inner in range(4):
                    k = turns * 4 + inner
                    gg = lax.dot_general(
                        slope_ref[...],
                        w[part * 8 : part * 8 + 8, k].reshape(128, H),
                        NT,
                        preferred_element_type=F32,
                    )
                    turned[pl.ds(k, batch, stride=K + 1), :] = gg
                return carry

            lax.fori_loop(0, K // 4, gram_grad, 0)

            def pack_gg(turns, carry):
                for inner in range(4):
                    b = turns * 4 + inner
                    gg_all[b, :, part * 128 : part * 128 + 128] = turned[
                        pl.ds(b * (K + 1), K), :
                    ].astype(BF)
                return carry

            lax.fori_loop(0, batch // 4, pack_gg, 0)

    def weight_grads(first):
        def one(turns, carry):
            for inner in range(4):
                k = first + turns * 4 + inner
                wgrad = lax.dot_general(gram[k], slope_ref[...], TN, preferred_element_type=F32)
                for block in range(16):
                    for parity in range(2):
                        at = block * 16 + parity * 8
                        turned[
                            pl.ds(block * 8 * (2 * K + 1) + parity * K + k, 8, stride=2 * K + 1), :
                        ] = wgrad[at : at + 8]
            return carry

        lax.fori_loop(0, K // 8, one, 0)

    @pl.when(step == 2)
    def _():
        weight_copy().wait_send()
        weight_copy().wait_recv()

        def pair_sum(n, carry):
            to_z, first, second = n // 16, (n // 4) % 4, n % 4
            chip = jnp.where(core == 0, first * 4 + second, second * 4 + first) * 4 + to_z
            mine = turned[pl.ds((chip * 2 + core) * (2 * K + 1), 2 * K), :]
            w2[to_z, n % 16] = (mine + other[chip].astype(F32)).astype(BF)
            return carry

        lax.fori_loop(0, 64, pair_sum, 0)
        for d in range(1, 4):
            weight_z(d).start()

    def sample(b):
        xb = xs_ref[b]
        gg = gg_all[step * ROWS + b]
        mg = jnp.dot(gg, xb, preferred_element_type=F32).astype(BF)
        pg = lax.dot_general(mg, xb, NT, preferred_element_type=F32)
        left = jnp.concatenate([gg, projt_ref[...]], axis=0)
        right = jnp.concatenate([mixed_ref[b], mg], axis=0)
        fg = lax.dot_general(left, right, TN, preferred_element_type=F32) * SCALE
        fg = fg.reshape(16, 2, 8, 256)
        even = fg[:, 0].reshape(PAIRS, 256)
        odd = fg[:, 1].reshape(PAIRS, 256)
        r0 = pltpu.roll(odd[:, :128], 64, 1)
        r1 = pltpu.roll(odd[:, 128:], 64, 1)
        wide[pl.ds(b, PAIRS, stride=3 * ROWS), :] = even[:, :128]
        wide[pl.ds(b + ROWS, PAIRS, stride=3 * ROWS), :] = jnp.where(low, even[:, 128:], r0)
        wide[pl.ds(b + 2 * ROWS, PAIRS, stride=3 * ROWS), :] = jnp.where(low, r0, r1)
        return pg

    def samples(turn, total):
        for inner in range(4):
            total = total + sample(turn * 4 + inner)
        return total

    pg_ref[...] += lax.fori_loop(0, ROWS // 4, samples, jnp.zeros((K, F), F32)) * SCALE

    @pl.when(step >= 2)
    def _():
        for copy in copies(step - 2, slot):
            copy.wait_send()
        own_copy(step - 2, slot).wait()

    def pack(q, carry):
        for kind in range(2):
            for last in range(4):
                first, second = q // 4, q % 4
                if kind == 0:
                    owner = ((first * 4 + second) * 4 + last) * 2
                else:
                    owner = ((second * 4 + first) * 4 + last) * 2 + 1
                for tile in range(3):
                    at = pl.ds(pl.multiple_of(owner * 3 * ROWS + tile * ROWS, ROWS), ROWS)
                    stage[slot, kind * 64 + q * 4 + last, :, tile * 128 : tile * 128 + 128] = wide[
                        at, :
                    ].astype(BF)
        return carry

    lax.fori_loop(0, 16, pack, 0)
    for copy in copies(step, slot):
        copy.start()
    own_copy(step, slot).start()

    @pl.when(step == 0)
    def _():
        weight_grads(0)

    @pl.when(step == 1)
    def _():
        weight_grads(K // 2)

        def pack_wgrad(chip, carry):
            give[chip] = turned[
                pl.ds((chip * 2 + 1 - core) * (2 * K + 1), 2 * K), :
            ].astype(BF)
            return carry

        lax.fori_loop(0, 64, pack_wgrad, 0)
        weight_copy().start()

    @pl.when(step == steps - 1)
    def _():
        for block, where in ((step - 1, 1 - slot), (step, slot)):
            for copy in copies(block, where):
                copy.wait_send()
            own_copy(block, where).wait()
        for d in range(1, 4):
            weight_z(d).wait_recv()

        def sum_z(n, carry):
            total = w2[z, n].astype(F32) + w2_in[0, n].astype(F32)
            total = total + (w2_in[1, n].astype(F32) + w2_in[2, n].astype(F32))
            wz_ref[n] = total.astype(BF)
            return carry

        lax.fori_loop(0, 16, sum_z, 0)
        for d in range(1, 4):
            weight_z(d).wait_send()

        def arrived(block, carry):
            def wait(sender, sem):
                at = pl.ds(sender * 128 + block * ROWS, ROWS)
                pltpu.make_async_remote_copy(
                    src_ref=stage.at[0, pl.ds(0, 16)],
                    dst_ref=rows_ref.at[:, at],
                    send_sem=send_sem.at[0, 0],
                    recv_sem=recv_sem.at[block, sem],
                    device_id=sibling,
                    device_id_type=MESH,
                ).wait_recv()

            wait(line * 2 + 1 - core, 0)
            for d in range(1, 4):
                for other in range(2):
                    wait(lax.rem(line + 4 - d, 4) * 2 + other, d * 2 + other)
            return carry

        lax.fori_loop(0, steps, arrived, 0)


def back(xs, mixed, projt, gram, w, cot):
    batch = xs.shape[0]
    any_space = pl.BlockSpec(memory_space=pl.ANY)
    return pl.pallas_call(
        back_kernel,
        grid=(batch // ROWS,),
        in_specs=[
            pl.BlockSpec((ROWS, F, 256), lambda i: (i, 0, 0)),
            pl.BlockSpec((ROWS, K, 256), lambda i: (i, 0, 0)),
            pl.BlockSpec((K, F), lambda i: (0, 0)),
            any_space,
            any_space,
            pl.BlockSpec((batch, H), lambda i: (0, 0)),
        ],
        out_specs=[
            pl.BlockSpec((K, F), lambda i: (0, 0)),
            any_space,
            pl.BlockSpec((16, 2 * K, H), lambda i: (0, 0, 0)),
        ],
        out_shape=[
            jax.ShapeDtypeStruct((K, F), F32),
            jax.ShapeDtypeStruct((16, 8 * batch, 2 * E), BF),
            jax.ShapeDtypeStruct((16, 2 * K, H), BF),
        ],
        scratch_shapes=[
            pltpu.VMEM((F * E // 128 * ROWS, 128), F32),
            pltpu.VMEM((2, PAIRS, ROWS, 2 * E), BF),
            pltpu.VMEM(gram.shape, BF),
            pltpu.VMEM(w.shape, BF),
            pltpu.VMEM((batch, H), BF),
            pltpu.VMEM((batch, K, F), BF),
            pltpu.VMEM((PAIRS * (2 * K + 1), H), F32),
            pltpu.VMEM((64, 2 * K, H), BF),
            pltpu.VMEM((64, 2 * K, H), BF),
            pltpu.VMEM((4, 16, 2 * K, H), BF),
            pltpu.VMEM((3, 16, 2 * K, H), BF),
            pltpu.SemaphoreType.DMA((2, 7)),
            pltpu.SemaphoreType.DMA((batch // ROWS, 8)),
            pltpu.SemaphoreType.DMA((2,)),
            pltpu.SemaphoreType.DMA((2,)),
            pltpu.SemaphoreType.DMA((3,)),
            pltpu.SemaphoreType.DMA((3,)),
            pltpu.SemaphoreType.DMA((CHUNKS,)),
            pltpu.SemaphoreType.DMA((CHUNKS,)),
        ],
        compiler_params=pltpu.CompilerParams(
            vmem_limit_bytes=VMEM_LIMIT, collective_id=1, has_side_effects=True
        ),
        cost_estimate=pl.CostEstimate(
            flops=14 * batch * F * E * K, bytes_accessed=60_000_000, transcendentals=0
        ),
        name="back",
    )(xs, mixed, projt, gram, w, cot)


SLOT_BLOCK = 256
HALF = UNIQUE_CAP // 2
FIRST = 128
ORDER = (1, 2, 3, 0)


def sums_kernel(
    rows_ref, seg_ref, wz_ref, pg_ref,
    wout_ref, pout_ref, out_ref,
    data, table, az, bv, sum_a, sum_b, va, zb, w3_in, w4, w4_in, pu, pv, pz, pc,
    load_sem, az_send, az_recv, bv_send, bv_recv, va_send, va_recv, zb_send, zb_recv,
    w_send, w_recv, p_send, p_recv,
):
    x, y, z, core = place()
    u = jnp.where(core == 0, x, y)
    v = jnp.where(core == 0, y, x)
    low = lower_half(SLOT_BLOCK)

    def at_u(d):
        moved = turn(u, d)
        return device(jnp.where(core == 0, moved, x), jnp.where(core == 0, y, moved), z, core)

    def at_v(d):
        moved = turn(v, d)
        return device(jnp.where(core == 0, x, moved), jnp.where(core == 0, moved, y), z, core)

    def at_z(d):
        return device(x, y, turn(z, d), core)

    sibling = device(x, y, z, 1 - core)

    def load(dz, dv):
        j = turn(v, dv) * 4 + turn(z, dz)
        return pltpu.make_async_copy(rows_ref.at[j], data.at[dz, dv], load_sem.at[dz, dv])

    for dz in ORDER:
        for dv in ORDER:
            load(dz, dv).start()

    greet([to(d) for d in range(1, 4) for to in (at_u, at_v, at_z)] + [sibling])

    def spread(buffer, mine, stage, to):
        return [
            remote(buffer.at[mine], buffer.at[mine], p_send.at[stage, d - 1], p_recv.at[stage, d - 1], to(d))
            for d in range(1, 4)
        ]

    def gathered(buffer, mine, stage, to):
        for d in range(1, 4):
            there = buffer.at[turn(mine, -d)]
            remote(there, there, p_send.at[stage, d - 1], p_recv.at[stage, d - 1], to(d)).wait_recv()
        return (buffer[0] + buffer[1]) + (buffer[2] + buffer[3])

    def start(copies):
        for copy in copies:
            copy.start()
        return copies

    def send_a(dz, dv):
        return remote(
            table.at[dz, dv, pl.ds(0, FIRST)],
            az.at[dz - 1, dv],
            az_send.at[dz - 1, dv],
            az_recv.at[dz - 1, dv],
            at_z(dz),
        )

    def send_b(dv, dz):
        return remote(
            table.at[dz, dv, pl.ds(FIRST, HALF - FIRST)],
            bv.at[dv - 1, dz],
            bv_send.at[dv - 1, dz],
            bv_recv.at[dv - 1, dz],
            at_v(dv),
        )

    def second_a(dv):
        return remote(sum_a.at[dv], va.at[dv - 1], va_send.at[dv - 1], va_recv.at[dv - 1], at_v(dv))

    def second_b(dz):
        return remote(sum_b.at[dz], zb.at[dz - 1], zb_send.at[dz - 1], zb_recv.at[dz - 1], at_z(dz))

    def one_table(dz, dv):
        load(dz, dv).wait()
        j = turn(v, dv) * 4 + turn(z, dz)
        slot = lax.broadcasted_iota(jnp.int32, (SLOT_BLOCK, 8 * 128), 0)

        def part(block, parity):
            seg = seg_ref[j, parity : parity + 1, :] - block * SLOT_BLOCK
            hot = jnp.where(slot == seg, 1.0, 0.0).astype(BF)
            found = jnp.dot(
                hot, data[dz, dv, :, parity * 128 : parity * 128 + 256], preferred_element_type=F32
            )
            return found[:, :128], found[:, 128:]

        for block in range(HALF // SLOT_BLOCK):
            at = pl.ds(block * SLOT_BLOCK, SLOT_BLOCK)
            even0, even1 = part(block, 0)
            odd0, odd1 = part(block, 1)
            r0 = pltpu.roll(odd0, 64, 1)
            r1 = pltpu.roll(odd1, 64, 1)
            table[dz, dv, at, 0:128] = (even0 + jnp.where(low, r0, r1)).astype(BF)
            first = even1 + r1
            even0, even1 = part(block + HALF // SLOT_BLOCK, 0)
            odd0, odd1 = part(block + HALF // SLOT_BLOCK, 1)
            r0 = pltpu.roll(even0, 64, 1)
            r1 = pltpu.roll(even1, 64, 1)
            table[dz, dv, at, 128:256] = jnp.where(low, first, r0 + odd0).astype(BF)
            table[dz, dv, at, 256:384] = (jnp.where(low, r0, r1) + odd1).astype(BF)

    def tables(dz):
        def one(turns, carry):
            dv = lax.rem(turns + 1, 4)
            one_table(dz, dv)
            if dz > 0:
                send_a(dz, dv).start()

            @pl.when(dv > 0)
            def _():
                send_b(dv, dz).start()

            return carry

        lax.fori_loop(0, 4, one, 0)

    def add_four(first, second, third, fourth, target, size):
        rows = first.shape[0]

        def one(n, carry):
            at = pl.ds(pl.multiple_of(n * size, size), size)
            total = (first[at].astype(F32) + second[at].astype(F32)) + (
                third[at].astype(F32) + fourth[at].astype(F32)
            )
            target[at] = total.astype(target.dtype)
            return carry

        lax.fori_loop(0, rows // size, one, 0)

    def total_b(dz):
        for dv in range(1, 4):
            send_b(dv, dz).wait_recv()
        mine = table.at[dz, 0, pl.ds(FIRST, HALF - FIRST)]
        add_four(mine, bv.at[0, dz], bv.at[1, dz], bv.at[2, dz], sum_b.at[dz], 64)
        if dz > 0:
            second_b(dz).start()

    def total_a(dv):
        for dz in range(1, 4):
            send_a(dz, dv).wait_recv()
        mine = table.at[0, dv, pl.ds(0, FIRST)]
        add_four(mine, az.at[0, dv], az.at[1, dv], az.at[2, dv], sum_a.at[dv], 64)
        if dv > 0:
            second_a(dv).start()

    def w_copies(source, arrive, stage, to, line, size):
        return [
            remote(
                source.at[pl.ds(turn(line, d) * size, size)],
                arrive.at[d - 1],
                w_send.at[stage, d - 1],
                w_recv.at[stage, d - 1],
                to(d),
            )
            for d in range(1, 4)
        ]

    pu[u] = pg_ref[...]
    p0 = start(spread(pu, u, 0, at_u))
    s3 = start(w_copies(wz_ref, w3_in, 0, at_u, u, 4))
    tables(1)
    pv[v] = gathered(pu, u, 0, at_u)
    p1 = start(spread(pv, v, 1, at_v))
    for copy in s3:
        copy.wait_recv()
    add_four(wz_ref.at[pl.ds(u * 4, 4)], w3_in.at[0], w3_in.at[1], w3_in.at[2], w4, 1)
    s4 = start(w_copies(w4, w4_in, 1, at_v, v, 1))
    tables(2)
    total_b(1)
    pz[z] = gathered(pv, v, 1, at_v)
    p2 = start(spread(pz, z, 2, at_z))
    tables(3)
    total_b(2)
    pc[core] = gathered(pz, z, 2, at_z)
    p3 = remote(pc.at[core], pc.at[core], p_send.at[3, 0], p_recv.at[3, 0], sibling)
    p3.start()
    for copy in s4:
        copy.wait_recv()
    total = w4[v].astype(F32) + w4_in[0, 0].astype(F32)
    wout_ref[...] = total + (w4_in[1, 0].astype(F32) + w4_in[2, 0].astype(F32))
    tables(0)
    total_b(3)
    for dv in ORDER:
        total_a(dv)
    total_b(0)
    remote(pc.at[1 - core], pc.at[1 - core], p_send.at[3, 0], p_recv.at[3, 0], sibling).wait_recv()
    pout_ref[...] = pc[0] + pc[1]

    def finish(mine, others, start_row, rows):
        def one(part, carry):
            at = pl.ds(pl.multiple_of(part * 64, 64), 64)
            before = pl.ds(pl.multiple_of(part * 64 + start_row, 64), 64)
            after = pl.ds(pl.multiple_of(part * 64 + start_row + HALF, 64), 64)
            total = mine[at, :].astype(F32) + others[0, at].astype(F32)
            total = total + (others[1, at].astype(F32) + others[2, at].astype(F32))
            out_ref[before, :] = total[:, :E]
            r1 = pltpu.roll(total[:, 128:256], 64, 1)
            r2 = pltpu.roll(total[:, 256:], 64, 1)
            out_ref[after, :128] = jnp.where(lower_half(64), r1, r2)
            out_ref[after, 128:] = r2[:, :64]
            return carry

        lax.fori_loop(0, rows // 64, one, 0)

    for d in range(1, 4):
        second_a(d).wait_recv()
    finish(sum_a.at[0], va, 0, FIRST)
    for d in range(1, 4):
        second_b(d).wait_recv()
    finish(sum_b.at[0], zb, FIRST, HALF - FIRST)

    for copy in p0 + p1 + p2 + [p3] + s3 + s4:
        copy.wait_send()
    for d in range(1, 4):
        second_a(d).wait_send()
        second_b(d).wait_send()
        for n in range(4):
            send_a(d, n).wait_send()
            send_b(d, n).wait_send()


def sums(rows, seg, wz, pg):
    any_space = pl.BlockSpec(memory_space=pl.ANY)
    whole = pl.BlockSpec(memory_space=pltpu.VMEM)
    dma = pltpu.SemaphoreType.DMA
    rest = HALF - FIRST
    return pl.pallas_call(
        sums_kernel,
        in_specs=[any_space, whole, whole, whole],
        out_specs=[whole] * 3,
        out_shape=[
            jax.ShapeDtypeStruct((2 * K, H), F32),
            jax.ShapeDtypeStruct((K, F), F32),
            jax.ShapeDtypeStruct((UNIQUE_CAP, E), F32),
        ],
        scratch_shapes=[
            pltpu.VMEM((4, 4) + rows.shape[1:], BF),
            pltpu.VMEM((4, 4, HALF, 2 * E), BF),
            pltpu.VMEM((3, 4, FIRST, 2 * E), BF),
            pltpu.VMEM((3, 4, rest, 2 * E), BF),
            pltpu.VMEM((4, FIRST, 2 * E), BF),
            pltpu.VMEM((4, rest, 2 * E), BF),
            pltpu.VMEM((3, FIRST, 2 * E), BF),
            pltpu.VMEM((3, rest, 2 * E), BF),
            pltpu.VMEM((3, 4, 2 * K, H), BF),
            pltpu.VMEM((4, 2 * K, H), BF),
            pltpu.VMEM((3, 1, 2 * K, H), BF),
            pltpu.VMEM((4, K, F), F32),
            pltpu.VMEM((4, K, F), F32),
            pltpu.VMEM((4, K, F), F32),
            pltpu.VMEM((2, K, F), F32),
            dma((4, 4)),
            dma((3, 4)),
            dma((3, 4)),
            dma((3, 4)),
            dma((3, 4)),
            dma((3,)),
            dma((3,)),
            dma((3,)),
            dma((3,)),
            dma((2, 3)),
            dma((2, 3)),
            dma((4, 3)),
            dma((4, 3)),
        ],
        compiler_params=pltpu.CompilerParams(
            vmem_limit_bytes=VMEM_LIMIT, collective_id=2, has_side_effects=True
        ),
        cost_estimate=pl.CostEstimate(
            flops=16 * 4 * UNIQUE_CAP * 1024 * 256, bytes_accessed=30_000_000, transcendentals=0
        ),
        name="sums",
    )(rows, seg, wz, pg)


def turn_features(a):
    rest = a.shape[1:]
    return a.reshape((-1, 8, 2) + rest).swapaxes(1, 2).reshape(a.shape)


def unturn_features(a):
    rest = a.shape[1:]
    return a.reshape((-1, 2, 8) + rest).swapaxes(1, 2).reshape(a.shape)


def cut_segments(segments):
    core = lax.axis_index("emb") % 2
    seg = segments.T.reshape(2, 4, 4, 4, 2, 128)
    along_x = seg.transpose(2, 3, 0, 1, 4, 5).reshape(16, 2, 1024)
    along_y = seg.transpose(1, 3, 0, 2, 4, 5).reshape(16, 2, 1024)
    return jnp.where(core == 0, along_x, along_y)


def on_device(pooled, projection, out_weight, cotangent, segments):
    own = turn_features(out_weight.reshape(-1, K, H)).swapaxes(0, 1)
    projt = turn_features(projection).T
    xs, mixed, gram, weight, seg = front(pooled, projt, own, cut_segments(segments))
    pg, rows, wz = back(xs, mixed, projt, gram, weight, cotangent)
    weight_grad, pg, row_grad = sums(rows, seg, wz, pg)
    return (weight_grad, unturn_features(pg.T), row_grad)


def solution(mesh):
    placed = (
        P(("fsdp", "emb"), None),
        P(),
        P("fsdp", None),
        P(("fsdp", "emb"), None),
        P(None, ("fsdp", "emb")),
    )
    return jax.shard_map(
        on_device,
        mesh=mesh,
        in_specs=placed,
        out_specs=(P(("fsdp", "emb"), None), P(), P(("fsdp", "emb"), None)),
        check_vma=False,
    )
```

```python
import functools

import jax
import jax.numpy as jnp
from jax import lax
from jax.experimental import pallas as pl
from jax.experimental.pallas import tpu as pltpu
from jax.sharding import PartitionSpec as P

F = 256
E = 192
K = 96
H = 128
UNIQUE_CAP = 1024
PAIRS = F // 2
ROWS = 16
SCALE = E ** (-0.5)
BF = jnp.bfloat16
F32 = jnp.float32
VMEM_LIMIT = 60 * 1024 * 1024
NT = (((1,), (1,)), ((), ()))
TN = (((0,), (0,)), ((), ()))


def interleave(even, odd):
    width = even.shape[-1]
    both = jnp.concatenate([even.reshape(16, 8, width), odd.reshape(16, 8, width)], axis=1)
    return both.reshape(F, width)


def lower_half(rows):
    return lax.broadcasted_iota(jnp.int32, (rows, 128), 1) < 64


MESH = pl.DeviceIdType.MESH


def place():
    fsdp = lax.axis_index("fsdp")
    emb = lax.axis_index("emb")
    return fsdp // 4, fsdp % 4, emb // 2, emb % 2


def device(x, y, z, core):
    return (x * 4 + y, z * 2 + core)


def turn(at, d):
    return lax.rem(at + 4 + d, 4)


def greet(devices):
    barrier = pltpu.get_barrier_semaphore()
    for to in devices:
        pl.semaphore_signal(barrier, inc=1, device_id=to, device_id_type=MESH)
    pl.semaphore_wait(barrier, len(devices))


def remote(source, target, send, recv, to):
    return pltpu.make_async_remote_copy(
        src_ref=source,
        dst_ref=target,
        send_sem=send,
        recv_sem=recv,
        device_id=to,
        device_id_type=MESH,
    )


SLOTS = 3
STEPS = 8


def main_kernel(
    x_ref, projt_ref, own_ref, cut_ref, cot_ref,
    pg_ref, rows_ref, wz_ref, seg_ref,
    wide, flat, mixed_all, gram, weight_ref, slope_ref, gg_all, turned, stage, give, other, w2_in,
    u_send, u_recv, v_send, v_recv, s_send, s_recv, g_send, g_recv, first_sem,
    send_sem, recv_sem, own_sem, pair_sem, z_send, z_recv,
):
    step = pl.program_id(0)
    batch = gram.shape[1]
    low = lower_half(PAIRS)
    x, y, z, core = place()
    u = jnp.where(core == 0, x, y)
    v = jnp.where(core == 0, y, x)
    line = u
    half = pl.ds(pl.multiple_of(core * (K // 2), K // 2), K // 2)
    other_half = pl.ds(pl.multiple_of((1 - core) * (K // 2), K // 2), K // 2)
    sibling = device(x, y, z, 1 - core)
    back = step - STEPS
    slot = lax.rem(step + SLOTS - STEPS % SLOTS, SLOTS)

    def at(du, dv, dz):
        moved_u, moved_v = turn(u, du), turn(v, dv)
        return device(
            jnp.where(core == 0, moved_u, moved_v),
            jnp.where(core == 0, moved_v, moved_u),
            turn(z, dz),
            core,
        )

    def block(du, dv):
        moved_u, moved_v = turn(u, du), turn(v, dv)
        return jnp.where(core == 0, moved_u * 4 + moved_v, moved_v * 4 + moved_u)

    def along_u(d):
        return remote(
            own_ref.at[half], weight_ref.at[block(0, 0), half], u_send.at[d - 1], u_recv.at[d - 1], at(d, 0, 0)
        )

    def from_u(d):
        there = weight_ref.at[block(-d, 0), half]
        return remote(there, there, u_send.at[d - 1], u_recv.at[d - 1], at(d, 0, 0))

    def along_v(d, du):
        there = weight_ref.at[block(du, 0), half]
        source = own_ref.at[half] if du == 0 else there
        return remote(source, there, v_send.at[d - 1, du], v_recv.at[d - 1, du], at(0, d, 0))

    def from_v(d, du):
        there = weight_ref.at[block(du, -d), half]
        return remote(there, there, v_send.at[d - 1, du], v_recv.at[d - 1, du], at(0, d, 0))

    def to_sibling(du, dv):
        there = weight_ref.at[block(du, dv), half]
        return remote(there, there, s_send.at[du, dv % 4], s_recv.at[du, dv % 4], sibling)

    def from_sibling(du, dv):
        first = jnp.where(core == 0, turn(x, dv), turn(x, du))
        second = jnp.where(core == 0, turn(y, du), turn(y, dv))
        there = weight_ref.at[first * 4 + second, other_half]
        return remote(there, there, s_send.at[du, dv % 4], s_recv.at[du, dv % 4], sibling)

    def segments_to(dv, dz):
        there = turn(v, dv) * 4 + turn(z, dz)
        return remote(
            cut_ref.at[there], seg_ref.at[v * 4 + z], g_send.at[dv, dz], g_recv.at[dv, dz], at(0, dv, dz)
        )

    def segments_from(dv, dz):
        there = seg_ref.at[turn(v, -dv) * 4 + turn(z, -dz)]
        return remote(there, there, g_send.at[dv, dz], g_recv.at[dv, dz], at(0, dv, dz))

    def weight_copy():
        return remote(give, other, pair_sem.at[0], pair_sem.at[1], sibling)

    def weight_z(d):
        there = turn(z, d)
        to = device(x, y, there, core)
        return remote(give.at[pl.ds(there * 16, 16)], w2_in.at[d - 1], z_send.at[d - 1], z_recv.at[d - 1], to)

    def copies(block, where):
        at_x = pl.ds((x * 2 + core) * 128 + block * ROWS, ROWS)
        at_y = pl.ds((y * 2 + core) * 128 + block * ROWS, ROWS)
        found = []
        for d in range(1, 4):
            tx = lax.rem(x + d, 4)
            ty = lax.rem(y + d, 4)
            for kind, group, rows, target in (
                (0, tx, at_x, device(tx, y, z, 0)),
                (1, 4 + ty, at_y, device(x, ty, z, 1)),
            ):
                found.append(
                    pltpu.make_async_remote_copy(
                        src_ref=stage.at[where, pl.ds(group * 16, 16)],
                        dst_ref=rows_ref.at[:, rows],
                        send_sem=send_sem.at[where, kind * 3 + d - 1],
                        recv_sem=recv_sem.at[block, d * 2 + core],
                        device_id=target,
                        device_id_type=MESH,
                    )
                )
        group = jnp.where(core == 0, 4 + y, x)
        there = pl.ds((jnp.where(core == 0, y, x) * 2 + core) * 128 + block * ROWS, ROWS)
        found.append(
            pltpu.make_async_remote_copy(
                src_ref=stage.at[where, pl.ds(group * 16, 16)],
                dst_ref=rows_ref.at[:, there],
                send_sem=send_sem.at[where, 6],
                recv_sem=recv_sem.at[block, 0],
                device_id=sibling,
                device_id_type=MESH,
            )
        )
        return found

    def own_copy(block, where):
        group = jnp.where(core == 0, x, 4 + y)
        here = pl.ds((line * 2 + core) * 128 + block * ROWS, ROWS)
        return pltpu.make_async_copy(
            stage.at[where, pl.ds(group * 16, 16)], rows_ref.at[:, here], own_sem.at[where]
        )

    plane = [(dv, dz) for dv in range(4) for dz in range(4) if dv or dz]
    blocks = [(du, dv) for du in range(4) for dv in range(4) if du or dv]
    weight_copy_own = pltpu.make_async_copy(own_ref, weight_ref.at[block(0, 0)], first_sem.at[0])
    seg_copy = pltpu.make_async_copy(cut_ref.at[v * 4 + z], seg_ref.at[v * 4 + z], first_sem.at[1])

    def pass_on(arrived):
        for du in arrived:
            for d in range(1, 4):
                from_v(d, du).wait_recv()
                to_sibling(du, 4 - d).start()

    @pl.when(step == 0)
    def _():
        pg_ref[...] = jnp.zeros_like(pg_ref)
        senders = [at(d, 0, 0) for d in range(1, 4)] + [at(0, dv, dz) for dv, dz in plane] + [sibling]
        for d in range(1, 4):
            moved = turn(u, d)
            senders.append(
                device(jnp.where(core == 0, moved, x), jnp.where(core == 0, y, moved), z, 1 - core)
            )
        greet(senders)
        for d in range(1, 4):
            along_u(d).start()
        for d in range(1, 4):
            along_v(d, 0).start()
        weight_copy_own.start()
        seg_copy.start()
        for dv, dz in plane:
            segments_to(dv, dz).start()

    @pl.when(step == 1)
    def _():
        for d in (1, 3, 2):
            from_u(d).wait_recv()
            for dv in range(1, 4):
                along_v(dv, 4 - d).start()
            to_sibling(4 - d, 0).start()

    @pl.when(step == 3)
    def _():
        pass_on((0,))

    @pl.when(step == 6)
    def _():
        pass_on((1, 3))

    def spread(turns, carry):
        for inner in range(8):
            tile = turns * 8 + inner
            wide[pl.ds(pl.multiple_of(tile * ROWS, ROWS), ROWS), :] = x_ref[
                :, pl.ds(pl.multiple_of(tile * 128, 128), 128)
            ].astype(F32)
        return carry

    lax.fori_loop(0, F * E // 1024, spread, 0)

    def matrix(b):
        a0 = wide[pl.ds(b, PAIRS, stride=3 * ROWS), :]
        a1 = wide[pl.ds(b + ROWS, PAIRS, stride=3 * ROWS), :]
        a2 = wide[pl.ds(b + 2 * ROWS, PAIRS, stride=3 * ROWS), :]
        r1 = pltpu.roll(a1, 64, 1)
        r2 = pltpu.roll(a2, 64, 1)
        even = jnp.concatenate([a0, jnp.where(low, a1, 0.0)], axis=1)
        odd = jnp.concatenate([jnp.where(low, r1, r2), jnp.where(low, r2, 0.0)], axis=1)
        return interleave(even, odd).astype(BF)

    @pl.when(step < STEPS)
    def _():
        def sample(b):
            xb = matrix(b)
            mixed = jnp.dot(projt_ref[...], xb, preferred_element_type=F32).astype(BF)
            mixed_all[step * ROWS + b] = mixed
            gram_b = lax.dot_general(mixed, xb, NT, preferred_element_type=F32) * SCALE
            flat[0, pl.ds(b, K, stride=ROWS), :] = gram_b[:, :128]
            flat[1, pl.ds(b, K, stride=ROWS), :] = gram_b[:, 128:]

        def samples(turns, carry):
            for inner in range(4):
                sample(turns * 4 + inner)
            return carry

        lax.fori_loop(0, ROWS // 4, samples, 0)
        rows = pl.ds(pl.multiple_of(step * ROWS, ROWS), ROWS)
        for part in range(2):
            gram[:, rows, part * 128 : part * 128 + 128] = (
                flat[part].reshape(K, ROWS, 128).astype(BF)
            )

    @pl.when(step == STEPS - 1)
    def _():
        pass_on((2,))

    def gram_grads(part):
        rows = pl.ds(part * (batch // 2), batch // 2)
        for lanes in range(2):

            def gram_grad(turns, carry):
                for inner in range(4):
                    k = turns * 4 + inner
                    gg = lax.dot_general(
                        slope_ref[rows, :],
                        weight_ref[lanes * 8 : lanes * 8 + 8, k].reshape(128, H),
                        NT,
                        preferred_element_type=F32,
                    )
                    turned[pl.ds(k, batch // 2, stride=K + 1), :] = gg
                return carry

            lax.fori_loop(0, K // 4, gram_grad, 0)

            def pack_gg(turns, carry):
                for inner in range(4):
                    b = turns * 4 + inner
                    gg_all[part * (batch // 2) + b, :, lanes * 128 : lanes * 128 + 128] = turned[
                        pl.ds(b * (K + 1), K), :
                    ].astype(BF)
                return carry

            lax.fori_loop(0, batch // 8, pack_gg, 0)

    def weight_grads(first):
        def one(turns, carry):
            for inner in range(4):
                k = first + turns * 4 + inner
                wgrad = lax.dot_general(gram[k], slope_ref[...], TN, preferred_element_type=F32)
                for block in range(16):
                    for parity in range(2):
                        at = block * 16 + parity * 8
                        turned[
                            pl.ds(block * 8 * (2 * K + 1) + parity * K + k, 8, stride=2 * K + 1), :
                        ] = wgrad[at : at + 8]
            return carry

        lax.fori_loop(0, K // 8, one, 0)

    @pl.when(step == STEPS)
    def _():
        weight_copy_own.wait()
        for du, dv in blocks:
            from_sibling(du, dv).wait_recv()

        def product(turns, total):
            for inner in range(8):
                k = turns * 8 + inner
                total = total + jnp.dot(
                    gram[k], weight_ref[:, k].reshape(F, H), preferred_element_type=F32
                )
            return total

        preact = lax.fori_loop(0, K // 8, product, jnp.zeros((batch, H), F32))
        sig = jax.nn.sigmoid(preact)
        slope_ref[...] = (
            cot_ref[...].astype(F32) * sig * (1.0 + preact * (1.0 - sig))
        ).astype(BF)
        gram_grads(0)

    @pl.when(back == 5)
    def _():
        weight_copy().wait_send()
        weight_copy().wait_recv()

        def pair_sum(n, carry):
            to_z, first, second = n // 16, (n // 4) % 4, n % 4
            chip = jnp.where(core == 0, first * 4 + second, second * 4 + first) * 4 + to_z
            mine = turned[pl.ds((chip * 2 + core) * (2 * K + 1), 2 * K), :]
            give[n] = (mine + other[chip].astype(F32)).astype(BF)
            return carry

        lax.fori_loop(0, 64, pair_sum, 0)
        for d in range(1, 4):
            weight_z(d).start()

    @pl.when(step >= STEPS)
    def _():
        def sample(b):
            xb = matrix(b)
            gg = gg_all[back * ROWS + b]
            mg = jnp.dot(gg, xb, preferred_element_type=F32).astype(BF)
            pg = lax.dot_general(mg, xb, NT, preferred_element_type=F32)
            left = jnp.concatenate([gg, projt_ref[...]], axis=0)
            right = jnp.concatenate([mixed_all[back * ROWS + b], mg], axis=0)
            fg = lax.dot_general(left, right, TN, preferred_element_type=F32) * SCALE
            fg = fg.reshape(16, 2, 8, 256)
            even = fg[:, 0].reshape(PAIRS, 256)
            odd = fg[:, 1].reshape(PAIRS, 256)
            r0 = pltpu.roll(odd[:, :128], 64, 1)
            r1 = pltpu.roll(odd[:, 128:], 64, 1)
            wide[pl.ds(b, PAIRS, stride=3 * ROWS), :] = even[:, :128]
            wide[pl.ds(b + ROWS, PAIRS, stride=3 * ROWS), :] = jnp.where(low, even[:, 128:], r0)
            wide[pl.ds(b + 2 * ROWS, PAIRS, stride=3 * ROWS), :] = jnp.where(low, r0, r1)
            return pg

        def samples(turns, total):
            for inner in range(4):
                total = total + sample(turns * 4 + inner)
            return total

        pg_ref[...] += lax.fori_loop(0, ROWS // 4, samples, jnp.zeros((K, F), F32)) * SCALE

        @pl.when(back >= SLOTS)
        def _():
            for copy in copies(back - SLOTS, slot):
                copy.wait_send()
            own_copy(back - SLOTS, slot).wait()

        def pack(q, carry):
            for kind in range(2):
                for last in range(4):
                    first, second = q // 4, q % 4
                    if kind == 0:
                        owner = ((first * 4 + second) * 4 + last) * 2
                    else:
                        owner = ((second * 4 + first) * 4 + last) * 2 + 1
                    for tile in range(3):
                        at = pl.ds(pl.multiple_of(owner * 3 * ROWS + tile * ROWS, ROWS), ROWS)
                        stage[slot, kind * 64 + q * 4 + last, :, tile * 128 : tile * 128 + 128] = wide[
                            at, :
                        ].astype(BF)
            return carry

        lax.fori_loop(0, 16, pack, 0)
        for copy in copies(back, slot):
            copy.start()
        own_copy(back, slot).start()

    @pl.when(back == 1)
    def _():
        gram_grads(1)

    @pl.when(back == 2)
    def _():
        weight_grads(0)

    @pl.when(back == 3)
    def _():
        weight_grads(K // 2)

        def pack_wgrad(chip, carry):
            give[chip] = turned[
                pl.ds((chip * 2 + 1 - core) * (2 * K + 1), 2 * K), :
            ].astype(BF)
            return carry

        lax.fori_loop(0, 64, pack_wgrad, 0)
        weight_copy().start()

    @pl.when(back == STEPS - 1)
    def _():
        for du, dv in blocks:
            to_sibling(du, dv).wait_send()
        for dv, dz in plane:
            segments_from(dv, dz).wait_recv()
            segments_to(dv, dz).wait_send()
        for d in range(1, 4):
            along_u(d).wait_send()
            for du in range(4):
                along_v(d, du).wait_send()
        seg_copy.wait()
        for ago in range(SLOTS):
            sent, where = back - ago, lax.rem(slot + SLOTS - ago, SLOTS)
            for copy in copies(sent, where):
                copy.wait_send()
            own_copy(sent, where).wait()
        for d in range(1, 4):
            weight_z(d).wait_recv()

        def sum_z(n, carry):
            total = give[z * 16 + n].astype(F32) + w2_in[0, n].astype(F32)
            total = total + (w2_in[1, n].astype(F32) + w2_in[2, n].astype(F32))
            wz_ref[n] = total.astype(BF)
            return carry

        lax.fori_loop(0, 16, sum_z, 0)
        for d in range(1, 4):
            weight_z(d).wait_send()

        def arrived(block, carry):
            def wait(sender, sem):
                at = pl.ds(sender * 128 + block * ROWS, ROWS)
                pltpu.make_async_remote_copy(
                    src_ref=stage.at[0, pl.ds(0, 16)],
                    dst_ref=rows_ref.at[:, at],
                    send_sem=send_sem.at[0, 0],
                    recv_sem=recv_sem.at[block, sem],
                    device_id=sibling,
                    device_id_type=MESH,
                ).wait_recv()

            wait(line * 2 + 1 - core, 0)
            for d in range(1, 4):
                for other in range(2):
                    wait(lax.rem(line + 4 - d, 4) * 2 + other, d * 2 + other)
            return carry

        lax.fori_loop(0, STEPS, arrived, 0)


def main(x, projt, own, cut, cot):
    batch = x.shape[0]
    any_space = pl.BlockSpec(memory_space=pl.ANY)
    dma = pltpu.SemaphoreType.DMA
    return pl.pallas_call(
        main_kernel,
        grid=(2 * STEPS,),
        in_specs=[
            pl.BlockSpec((ROWS, F * E), lambda i: (lax.rem(i, STEPS), 0)),
            pl.BlockSpec((K, F), lambda i: (0, 0)),
            any_space,
            any_space,
            pl.BlockSpec((batch, H), lambda i: (0, 0)),
        ],
        out_specs=[
            pl.BlockSpec((K, F), lambda i: (0, 0)),
            any_space,
            pl.BlockSpec((16, 2 * K, H), lambda i: (0, 0, 0)),
            any_space,
        ],
        out_shape=[
            jax.ShapeDtypeStruct((K, F), F32),
            jax.ShapeDtypeStruct((16, 8 * batch, 2 * E), BF),
            jax.ShapeDtypeStruct((16, 2 * K, H), BF),
            jax.ShapeDtypeStruct(cut.shape, jnp.int32),
        ],
        scratch_shapes=[
            pltpu.VMEM((F * E // 128 * ROWS, 128), F32),
            pltpu.VMEM((2, K * ROWS, 128), F32),
            pltpu.VMEM((batch, K, 256), BF),
            pltpu.VMEM((K, batch, F), BF),
            pltpu.VMEM((16,) + own.shape, BF),
            pltpu.VMEM((batch, H), BF),
            pltpu.VMEM((batch, K, F), BF),
            pltpu.VMEM((PAIRS * (2 * K + 1), H), F32),
            pltpu.VMEM((SLOTS, PAIRS, ROWS, 2 * E), BF),
            pltpu.VMEM((64, 2 * K, H), BF),
            pltpu.VMEM((64, 2 * K, H), BF),
            pltpu.VMEM((3, 16, 2 * K, H), BF),
            dma((3,)),
            dma((3,)),
            dma((3, 4)),
            dma((3, 4)),
            dma((4, 4)),
            dma((4, 4)),
            dma((4, 4)),
            dma((4, 4)),
            dma((2,)),
            dma((SLOTS, 7)),
            dma((STEPS, 8)),
            dma((SLOTS,)),
            dma((2,)),
            dma((3,)),
            dma((3,)),
        ],
        compiler_params=pltpu.CompilerParams(
            vmem_limit_bytes=VMEM_LIMIT, collective_id=1, has_side_effects=True
        ),
        cost_estimate=pl.CostEstimate(
            flops=18 * batch * F * E * K, bytes_accessed=60_000_000, transcendentals=batch * H
        ),
        name="main",
    )(x, projt, own, cut, cot)


SLOT_BLOCK = 256
HALF = UNIQUE_CAP // 2
FIRST = 128
ORDER = (1, 2, 3, 0)


def sums_kernel(
    rows_ref, seg_ref, wz_ref, pg_ref,
    wout_ref, pout_ref, out_ref,
    data, table, az, bv, sum_a, sum_b, va, zb, w3_in, w4, w4_in, pu, pv, pz, pc,
    load_sem, az_send, az_recv, bv_send, bv_recv, va_send, va_recv, zb_send, zb_recv,
    w_send, w_recv, p_send, p_recv,
):
    x, y, z, core = place()
    u = jnp.where(core == 0, x, y)
    v = jnp.where(core == 0, y, x)
    low = lower_half(SLOT_BLOCK)

    def at_u(d):
        moved = turn(u, d)
        return device(jnp.where(core == 0, moved, x), jnp.where(core == 0, y, moved), z, core)

    def at_v(d):
        moved = turn(v, d)
        return device(jnp.where(core == 0, x, moved), jnp.where(core == 0, moved, y), z, core)

    def at_z(d):
        return device(x, y, turn(z, d), core)

    sibling = device(x, y, z, 1 - core)

    def load(dz, dv):
        j = turn(v, dv) * 4 + turn(z, dz)
        return pltpu.make_async_copy(rows_ref.at[j], data.at[dz, dv], load_sem.at[dz, dv])

    for dz in ORDER:
        for dv in ORDER:
            load(dz, dv).start()

    greet([to(d) for d in range(1, 4) for to in (at_u, at_v, at_z)] + [sibling])

    def spread(buffer, mine, stage, to):
        return [
            remote(buffer.at[mine], buffer.at[mine], p_send.at[stage, d - 1], p_recv.at[stage, d - 1], to(d))
            for d in range(1, 4)
        ]

    def gathered(buffer, mine, stage, to):
        for d in range(1, 4):
            there = buffer.at[turn(mine, -d)]
            remote(there, there, p_send.at[stage, d - 1], p_recv.at[stage, d - 1], to(d)).wait_recv()
        return (buffer[0] + buffer[1]) + (buffer[2] + buffer[3])

    def start(copies):
        for copy in copies:
            copy.start()
        return copies

    def send_a(dz, dv):
        return remote(
            table.at[dz, dv, pl.ds(0, FIRST)],
            az.at[dz - 1, dv],
            az_send.at[dz - 1, dv],
            az_recv.at[dz - 1, dv],
            at_z(dz),
        )

    def send_b(dv, dz):
        return remote(
            table.at[dz, dv, pl.ds(FIRST, HALF - FIRST)],
            bv.at[dv - 1, dz],
            bv_send.at[dv - 1, dz],
            bv_recv.at[dv - 1, dz],
            at_v(dv),
        )

    def second_a(dv):
        return remote(sum_a.at[dv], va.at[dv - 1], va_send.at[dv - 1], va_recv.at[dv - 1], at_v(dv))

    def second_b(dz):
        return remote(sum_b.at[dz], zb.at[dz - 1], zb_send.at[dz - 1], zb_recv.at[dz - 1], at_z(dz))

    def one_table(dz, dv):
        load(dz, dv).wait()
        j = turn(v, dv) * 4 + turn(z, dz)
        slot = lax.broadcasted_iota(jnp.int32, (SLOT_BLOCK, 8 * 128), 0)

        def part(block, parity):
            seg = seg_ref[j, parity : parity + 1, :] - block * SLOT_BLOCK
            hot = jnp.where(slot == seg, 1.0, 0.0).astype(BF)
            found = jnp.dot(
                hot, data[dz, dv, :, parity * 128 : parity * 128 + 256], preferred_element_type=F32
            )
            return found[:, :128], found[:, 128:]

        for block in range(HALF // SLOT_BLOCK):
            at = pl.ds(block * SLOT_BLOCK, SLOT_BLOCK)
            even0, even1 = part(block, 0)
            odd0, odd1 = part(block, 1)
            r0 = pltpu.roll(odd0, 64, 1)
            r1 = pltpu.roll(odd1, 64, 1)
            table[dz, dv, at, 0:128] = (even0 + jnp.where(low, r0, r1)).astype(BF)
            first = even1 + r1
            even0, even1 = part(block + HALF // SLOT_BLOCK, 0)
            odd0, odd1 = part(block + HALF // SLOT_BLOCK, 1)
            r0 = pltpu.roll(even0, 64, 1)
            r1 = pltpu.roll(even1, 64, 1)
            table[dz, dv, at, 128:256] = jnp.where(low, first, r0 + odd0).astype(BF)
            table[dz, dv, at, 256:384] = (jnp.where(low, r0, r1) + odd1).astype(BF)

    def tables(dz):
        def one(turns, carry):
            dv = lax.rem(turns + 1, 4)
            one_table(dz, dv)
            if dz > 0:
                send_a(dz, dv).start()

            @pl.when(dv > 0)
            def _():
                send_b(dv, dz).start()

            return carry

        lax.fori_loop(0, 4, one, 0)

    def add_four(first, second, third, fourth, target, size):
        rows = first.shape[0]

        def one(n, carry):
            at = pl.ds(pl.multiple_of(n * size, size), size)
            total = (first[at].astype(F32) + second[at].astype(F32)) + (
                third[at].astype(F32) + fourth[at].astype(F32)
            )
            target[at] = total.astype(target.dtype)
            return carry

        lax.fori_loop(0, rows // size, one, 0)

    def total_b(dz):
        for dv in range(1, 4):
            send_b(dv, dz).wait_recv()
        mine = table.at[dz, 0, pl.ds(FIRST, HALF - FIRST)]
        add_four(mine, bv.at[0, dz], bv.at[1, dz], bv.at[2, dz], sum_b.at[dz], 64)
        if dz > 0:
            second_b(dz).start()

    def total_a(dv):
        for dz in range(1, 4):
            send_a(dz, dv).wait_recv()
        mine = table.at[0, dv, pl.ds(0, FIRST)]
        add_four(mine, az.at[0, dv], az.at[1, dv], az.at[2, dv], sum_a.at[dv], 64)
        if dv > 0:
            second_a(dv).start()

    def w_copies(source, arrive, stage, to, line, size):
        return [
            remote(
                source.at[pl.ds(turn(line, d) * size, size)],
                arrive.at[d - 1],
                w_send.at[stage, d - 1],
                w_recv.at[stage, d - 1],
                to(d),
            )
            for d in range(1, 4)
        ]

    pu[u] = pg_ref[...]
    p0 = start(spread(pu, u, 0, at_u))
    s3 = start(w_copies(wz_ref, w3_in, 0, at_u, u, 4))
    tables(1)
    pv[v] = gathered(pu, u, 0, at_u)
    p1 = start(spread(pv, v, 1, at_v))
    for copy in s3:
        copy.wait_recv()
    add_four(wz_ref.at[pl.ds(u * 4, 4)], w3_in.at[0], w3_in.at[1], w3_in.at[2], w4, 1)
    s4 = start(w_copies(w4, w4_in, 1, at_v, v, 1))
    tables(2)
    total_b(1)
    pz[z] = gathered(pv, v, 1, at_v)
    p2 = start(spread(pz, z, 2, at_z))
    tables(3)
    total_b(2)
    pc[core] = gathered(pz, z, 2, at_z)
    p3 = remote(pc.at[core], pc.at[core], p_send.at[3, 0], p_recv.at[3, 0], sibling)
    p3.start()
    for copy in s4:
        copy.wait_recv()
    total = w4[v].astype(F32) + w4_in[0, 0].astype(F32)
    wout_ref[...] = total + (w4_in[1, 0].astype(F32) + w4_in[2, 0].astype(F32))
    tables(0)
    total_b(3)
    for dv in ORDER:
        total_a(dv)
    total_b(0)
    remote(pc.at[1 - core], pc.at[1 - core], p_send.at[3, 0], p_recv.at[3, 0], sibling).wait_recv()
    pout_ref[...] = pc[0] + pc[1]

    def finish(mine, others, start_row, rows):
        def one(part, carry):
            at = pl.ds(pl.multiple_of(part * 64, 64), 64)
            before = pl.ds(pl.multiple_of(part * 64 + start_row, 64), 64)
            after = pl.ds(pl.multiple_of(part * 64 + start_row + HALF, 64), 64)
            total = mine[at, :].astype(F32) + others[0, at].astype(F32)
            total = total + (others[1, at].astype(F32) + others[2, at].astype(F32))
            out_ref[before, :] = total[:, :E]
            r1 = pltpu.roll(total[:, 128:256], 64, 1)
            r2 = pltpu.roll(total[:, 256:], 64, 1)
            out_ref[after, :128] = jnp.where(lower_half(64), r1, r2)
            out_ref[after, 128:] = r2[:, :64]
            return carry

        lax.fori_loop(0, rows // 64, one, 0)

    for d in range(1, 4):
        second_a(d).wait_recv()
    finish(sum_a.at[0], va, 0, FIRST)
    for d in range(1, 4):
        second_b(d).wait_recv()
    finish(sum_b.at[0], zb, FIRST, HALF - FIRST)

    for copy in p0 + p1 + p2 + [p3] + s3 + s4:
        copy.wait_send()
    for d in range(1, 4):
        second_a(d).wait_send()
        second_b(d).wait_send()
        for n in range(4):
            send_a(d, n).wait_send()
            send_b(d, n).wait_send()


def sums(rows, seg, wz, pg):
    any_space = pl.BlockSpec(memory_space=pl.ANY)
    whole = pl.BlockSpec(memory_space=pltpu.VMEM)
    dma = pltpu.SemaphoreType.DMA
    rest = HALF - FIRST
    return pl.pallas_call(
        sums_kernel,
        in_specs=[any_space, whole, whole, whole],
        out_specs=[whole] * 3,
        out_shape=[
            jax.ShapeDtypeStruct((2 * K, H), F32),
            jax.ShapeDtypeStruct((K, F), F32),
            jax.ShapeDtypeStruct((UNIQUE_CAP, E), F32),
        ],
        scratch_shapes=[
            pltpu.VMEM((4, 4) + rows.shape[1:], BF),
            pltpu.VMEM((4, 4, HALF, 2 * E), BF),
            pltpu.VMEM((3, 4, FIRST, 2 * E), BF),
            pltpu.VMEM((3, 4, rest, 2 * E), BF),
            pltpu.VMEM((4, FIRST, 2 * E), BF),
            pltpu.VMEM((4, rest, 2 * E), BF),
            pltpu.VMEM((3, FIRST, 2 * E), BF),
            pltpu.VMEM((3, rest, 2 * E), BF),
            pltpu.VMEM((3, 4, 2 * K, H), BF),
            pltpu.VMEM((4, 2 * K, H), BF),
            pltpu.VMEM((3, 1, 2 * K, H), BF),
            pltpu.VMEM((4, K, F), F32),
            pltpu.VMEM((4, K, F), F32),
            pltpu.VMEM((4, K, F), F32),
            pltpu.VMEM((2, K, F), F32),
            dma((4, 4)),
            dma((3, 4)),
            dma((3, 4)),
            dma((3, 4)),
            dma((3, 4)),
            dma((3,)),
            dma((3,)),
            dma((3,)),
            dma((3,)),
            dma((2, 3)),
            dma((2, 3)),
            dma((4, 3)),
            dma((4, 3)),
        ],
        compiler_params=pltpu.CompilerParams(
            vmem_limit_bytes=VMEM_LIMIT, collective_id=2, has_side_effects=True
        ),
        cost_estimate=pl.CostEstimate(
            flops=16 * 4 * UNIQUE_CAP * 1024 * 256, bytes_accessed=30_000_000, transcendentals=0
        ),
        name="sums",
    )(rows, seg, wz, pg)


def turn_features(a):
    rest = a.shape[1:]
    return a.reshape((-1, 8, 2) + rest).swapaxes(1, 2).reshape(a.shape)


def unturn_features(a):
    rest = a.shape[1:]
    return a.reshape((-1, 2, 8) + rest).swapaxes(1, 2).reshape(a.shape)


def cut_segments(segments):
    core = lax.axis_index("emb") % 2
    seg = segments.T.reshape(2, 4, 4, 4, 2, 128)
    along_x = seg.transpose(2, 3, 0, 1, 4, 5).reshape(16, 2, 1024)
    along_y = seg.transpose(1, 3, 0, 2, 4, 5).reshape(16, 2, 1024)
    return jnp.where(core == 0, along_x, along_y)


def on_device(pooled, projection, out_weight, cotangent, segments):
    own = turn_features(out_weight.reshape(-1, K, H)).swapaxes(0, 1)
    projt = turn_features(projection).T
    pg, rows, wz, seg = main(pooled, projt, own, cut_segments(segments), cotangent)
    weight_grad, pg, row_grad = sums(rows, seg, wz, pg)
    return (weight_grad, unturn_features(pg.T), row_grad)


def solution(mesh):
    placed = (
        P(("fsdp", "emb"), None),
        P(),
        P("fsdp", None),
        P(("fsdp", "emb"), None),
        P(None, ("fsdp", "emb")),
    )
    return jax.shard_map(
        on_device,
        mesh=mesh,
        in_specs=placed,
        out_specs=(P(("fsdp", "emb"), None), P(), P(("fsdp", "emb"), None)),
        check_vma=False,
    )
```

```python
import functools

import jax
import jax.numpy as jnp
from jax import lax
from jax.experimental import pallas as pl
from jax.experimental.pallas import tpu as pltpu
from jax.sharding import PartitionSpec as P

F = 256
E = 192
K = 96
H = 128
UNIQUE_CAP = 1024
PAIRS = F // 2
ROWS = 16
SCALE = E ** (-0.5)
BF = jnp.bfloat16
F32 = jnp.float32
VMEM_LIMIT = 60 * 1024 * 1024
NT = (((1,), (1,)), ((), ()))
TN = (((0,), (0,)), ((), ()))


def interleave(even, odd):
    width = even.shape[-1]
    both = jnp.concatenate([even.reshape(16, 8, width), odd.reshape(16, 8, width)], axis=1)
    return both.reshape(F, width)


def lower_half(rows):
    return lax.broadcasted_iota(jnp.int32, (rows, 128), 1) < 64


MESH = pl.DeviceIdType.MESH


def place():
    fsdp = lax.axis_index("fsdp")
    emb = lax.axis_index("emb")
    return fsdp // 4, fsdp % 4, emb // 2, emb % 2


def device(x, y, z, core):
    return (x * 4 + y, z * 2 + core)


def turn(at, d):
    return lax.rem(at + 4 + d, 4)


def greet(devices):
    barrier = pltpu.get_barrier_semaphore()
    for to in devices:
        pl.semaphore_signal(barrier, inc=1, device_id=to, device_id_type=MESH)
    pl.semaphore_wait(barrier, len(devices))


def remote(source, target, send, recv, to):
    return pltpu.make_async_remote_copy(
        src_ref=source,
        dst_ref=target,
        send_sem=send,
        recv_sem=recv,
        device_id=to,
        device_id_type=MESH,
    )


SLOTS = 3
PAD = ROWS + 1
STEPS = 8


def main_kernel(
    x_ref, projt_ref, own_ref, cut_ref, cot_ref,
    pg_ref, rows_ref, wz_ref, seg_ref,
    wide, ready, mixed_all, gram, weight_ref, slope_ref, gg_all, turned, stage, give, other, w2_in,
    u_send, u_recv, v_send, v_recv, s_send, s_recv, g_send, g_recv, first_sem,
    send_sem, recv_sem, own_sem, pair_sem, z_send, z_recv,
):
    step = pl.program_id(0)
    batch = gram.shape[1]
    low = lower_half(PAIRS)
    x, y, z, core = place()
    u = jnp.where(core == 0, x, y)
    v = jnp.where(core == 0, y, x)
    line = u
    half = pl.ds(pl.multiple_of(core * (K // 2), K // 2), K // 2)
    other_half = pl.ds(pl.multiple_of((1 - core) * (K // 2), K // 2), K // 2)
    sibling = device(x, y, z, 1 - core)
    back = step - STEPS
    slot = lax.rem(step + SLOTS - STEPS % SLOTS, SLOTS)

    def at(du, dv, dz):
        moved_u, moved_v = turn(u, du), turn(v, dv)
        return device(
            jnp.where(core == 0, moved_u, moved_v),
            jnp.where(core == 0, moved_v, moved_u),
            turn(z, dz),
            core,
        )

    def block(du, dv):
        moved_u, moved_v = turn(u, du), turn(v, dv)
        return jnp.where(core == 0, moved_u * 4 + moved_v, moved_v * 4 + moved_u)

    def along_u(d):
        return remote(
            own_ref.at[half], weight_ref.at[block(0, 0), half], u_send.at[d - 1], u_recv.at[d - 1], at(d, 0, 0)
        )

    def from_u(d):
        there = weight_ref.at[block(-d, 0), half]
        return remote(there, there, u_send.at[d - 1], u_recv.at[d - 1], at(d, 0, 0))

    def along_v(d, du):
        there = weight_ref.at[block(du, 0), half]
        source = own_ref.at[half] if du == 0 else there
        return remote(source, there, v_send.at[d - 1, du], v_recv.at[d - 1, du], at(0, d, 0))

    def from_v(d, du):
        there = weight_ref.at[block(du, -d), half]
        return remote(there, there, v_send.at[d - 1, du], v_recv.at[d - 1, du], at(0, d, 0))

    def to_sibling(du, dv):
        there = weight_ref.at[block(du, dv), half]
        return remote(there, there, s_send.at[du, dv % 4], s_recv.at[du, dv % 4], sibling)

    def from_sibling(du, dv):
        first = jnp.where(core == 0, turn(x, dv), turn(x, du))
        second = jnp.where(core == 0, turn(y, du), turn(y, dv))
        there = weight_ref.at[first * 4 + second, other_half]
        return remote(there, there, s_send.at[du, dv % 4], s_recv.at[du, dv % 4], sibling)

    def segments_to(dv, dz):
        there = turn(v, dv) * 4 + turn(z, dz)
        return remote(
            cut_ref.at[there], seg_ref.at[v * 4 + z], g_send.at[dv, dz], g_recv.at[dv, dz], at(0, dv, dz)
        )

    def segments_from(dv, dz):
        there = seg_ref.at[turn(v, -dv) * 4 + turn(z, -dz)]
        return remote(there, there, g_send.at[dv, dz], g_recv.at[dv, dz], at(0, dv, dz))

    def weight_copy():
        return remote(give, other, pair_sem.at[0], pair_sem.at[1], sibling)

    def weight_z(d):
        there = turn(z, d)
        to = device(x, y, there, core)
        return remote(give.at[pl.ds(there * 16, 16)], w2_in.at[d - 1], z_send.at[d - 1], z_recv.at[d - 1], to)

    def copies(block, where):
        at_x = pl.ds((x * 2 + core) * 128 + block * ROWS, ROWS)
        at_y = pl.ds((y * 2 + core) * 128 + block * ROWS, ROWS)
        found = []
        for d in range(1, 4):
            tx = lax.rem(x + d, 4)
            ty = lax.rem(y + d, 4)
            for kind, group, rows, target in (
                (0, tx, at_x, device(tx, y, z, 0)),
                (1, 4 + ty, at_y, device(x, ty, z, 1)),
            ):
                found.append(
                    pltpu.make_async_remote_copy(
                        src_ref=stage.at[where, pl.ds(group * 16, 16)],
                        dst_ref=rows_ref.at[:, rows],
                        send_sem=send_sem.at[where, kind * 3 + d - 1],
                        recv_sem=recv_sem.at[block, d * 2 + core],
                        device_id=target,
                        device_id_type=MESH,
                    )
                )
        group = jnp.where(core == 0, 4 + y, x)
        there = pl.ds((jnp.where(core == 0, y, x) * 2 + core) * 128 + block * ROWS, ROWS)
        found.append(
            pltpu.make_async_remote_copy(
                src_ref=stage.at[where, pl.ds(group * 16, 16)],
                dst_ref=rows_ref.at[:, there],
                send_sem=send_sem.at[where, 6],
                recv_sem=recv_sem.at[block, 0],
                device_id=sibling,
                device_id_type=MESH,
            )
        )
        return found

    def own_copy(block, where):
        group = jnp.where(core == 0, x, 4 + y)
        here = pl.ds((line * 2 + core) * 128 + block * ROWS, ROWS)
        return pltpu.make_async_copy(
            stage.at[where, pl.ds(group * 16, 16)], rows_ref.at[:, here], own_sem.at[where]
        )

    plane = [(dv, dz) for dv in range(4) for dz in range(4) if dv or dz]
    blocks = [(du, dv) for du in range(4) for dv in range(4) if du or dv]
    weight_copy_own = pltpu.make_async_copy(own_ref, weight_ref.at[block(0, 0)], first_sem.at[0])
    seg_copy = pltpu.make_async_copy(cut_ref.at[v * 4 + z], seg_ref.at[v * 4 + z], first_sem.at[1])

    def pass_on(arrived):
        for du in arrived:
            for d in range(1, 4):
                from_v(d, du).wait_recv()
                to_sibling(du, 4 - d).start()

    @pl.when(step == 0)
    def _():
        pg_ref[...] = jnp.zeros_like(pg_ref)
        senders = [at(d, 0, 0) for d in range(1, 4)] + [at(0, dv, dz) for dv, dz in plane] + [sibling]
        for d in range(1, 4):
            moved = turn(u, d)
            senders.append(
                device(jnp.where(core == 0, moved, x), jnp.where(core == 0, y, moved), z, 1 - core)
            )
        greet(senders)
        for d in range(1, 4):
            along_u(d).start()
        for d in range(1, 4):
            along_v(d, 0).start()
        weight_copy_own.start()
        seg_copy.start()
        for dv, dz in plane:
            segments_to(dv, dz).start()

    @pl.when(step == 1)
    def _():
        for d in (1, 3, 2):
            from_u(d).wait_recv()
            for dv in range(1, 4):
                along_v(dv, 4 - d).start()
            to_sibling(4 - d, 0).start()

    @pl.when(step == 3)
    def _():
        pass_on((0,))

    @pl.when(step == 6)
    def _():
        pass_on((1, 3))

    def spread(turns, carry):
        for inner in range(8):
            tile = turns * 8 + inner
            wide[pl.ds(pl.multiple_of(tile * ROWS, ROWS), ROWS), :] = x_ref[
                :, pl.ds(pl.multiple_of(tile * 128, 128), 128)
            ].astype(F32)
        return carry

    lax.fori_loop(0, F * E // 1024, spread, 0)

    def matrix(b):
        a0 = wide[pl.ds(b, PAIRS, stride=3 * ROWS), :]
        a1 = wide[pl.ds(b + ROWS, PAIRS, stride=3 * ROWS), :]
        a2 = wide[pl.ds(b + 2 * ROWS, PAIRS, stride=3 * ROWS), :]
        r1 = pltpu.roll(a1, 64, 1)
        r2 = pltpu.roll(a2, 64, 1)
        even = jnp.concatenate([a0, jnp.where(low, a1, 0.0)], axis=1)
        odd = jnp.concatenate([jnp.where(low, r1, r2), jnp.where(low, r2, 0.0)], axis=1)
        return interleave(even, odd).astype(BF)

    @pl.when(step < STEPS)
    def _():
        def samples(turns, carry):
            group = [turns * 4 + inner for inner in range(4)]
            xs = [matrix(b) for b in group]
            mixed = [
                jnp.dot(projt_ref[...], xb, preferred_element_type=F32).astype(BF) for xb in xs
            ]
            grams = [
                lax.dot_general(m, xb, NT, preferred_element_type=F32) * SCALE
                for m, xb in zip(mixed, xs)
            ]
            for b, m, gram_b in zip(group, mixed, grams):
                mixed_all[step * ROWS + b] = m
                turned[pl.ds(b, K, stride=PAD), :] = gram_b[:, :128]
                turned[pl.ds(K * PAD + b, K, stride=PAD), :] = gram_b[:, 128:]
            return carry

        lax.fori_loop(0, ROWS // 4, samples, 0)
        rows = pl.ds(pl.multiple_of(step * ROWS, ROWS), ROWS)

        def pack_gram(turns, carry):
            for inner in range(8):
                k = turns * 8 + inner
                for part in range(2):
                    at = pl.ds((part * K + k) * PAD, ROWS)
                    gram[k, rows, part * 128 : part * 128 + 128] = turned[at, :].astype(BF)
            return carry

        lax.fori_loop(0, K // 8, pack_gram, 0)

    @pl.when(step == STEPS - 1)
    def _():
        pass_on((2,))

    def gram_grads():
        def gram_grad(turns, carry):
            for inner in range(4):
                k = turns * 4 + inner
                gg = lax.dot_general(
                    slope_ref[...], weight_ref[:, k].reshape(F, H), NT, preferred_element_type=F32
                )
                turned[pl.ds(k, batch, stride=K + 1), :] = gg[:, :128]
                turned[pl.ds(batch * (K + 1) + k, batch, stride=K + 1), :] = gg[:, 128:]
            return carry

        lax.fori_loop(0, K // 4, gram_grad, 0)

        def pack_gg(turns, carry):
            for inner in range(4):
                b = turns * 4 + inner
                for part in range(2):
                    gg_all[b, :, part * 128 : part * 128 + 128] = turned[
                        pl.ds((part * batch + b) * (K + 1), K), :
                    ].astype(BF)
            return carry

        lax.fori_loop(0, batch // 4, pack_gg, 0)

    def weight_grads(first):
        def one(turns, carry):
            for inner in range(4):
                k = first + turns * 4 + inner
                wgrad = lax.dot_general(gram[k], slope_ref[...], TN, preferred_element_type=F32)
                for block in range(16):
                    for parity in range(2):
                        at = block * 16 + parity * 8
                        turned[
                            pl.ds(block * 8 * (2 * K + 1) + parity * K + k, 8, stride=2 * K + 1), :
                        ] = wgrad[at : at + 8]
            return carry

        lax.fori_loop(0, K // 8, one, 0)

    @pl.when(step == STEPS)
    def _():
        weight_copy_own.wait()
        for du, dv in blocks:
            from_sibling(du, dv).wait_recv()

        def product(turns, total):
            for inner in range(8):
                k = turns * 8 + inner
                total = total + jnp.dot(
                    gram[k], weight_ref[:, k].reshape(F, H), preferred_element_type=F32
                )
            return total

        preact = lax.fori_loop(0, K // 8, product, jnp.zeros((batch, H), F32))
        sig = jax.nn.sigmoid(preact)
        slope_ref[...] = (
            cot_ref[...].astype(F32) * sig * (1.0 + preact * (1.0 - sig))
        ).astype(BF)
        gram_grads()

    @pl.when(back == 2)
    def _():
        weight_copy().wait_send()
        weight_copy().wait_recv()

        def pair_sum(n, carry):
            to_z, first, second = n // 16, (n // 4) % 4, n % 4
            chip = jnp.where(core == 0, first * 4 + second, second * 4 + first) * 4 + to_z
            mine = turned[pl.ds((chip * 2 + core) * (2 * K + 1), 2 * K), :]
            give[n] = (mine + other[chip].astype(F32)).astype(BF)
            return carry

        lax.fori_loop(0, 64, pair_sum, 0)
        for d in range(1, 4):
            weight_z(d).start()

    @pl.when(step >= STEPS)
    def _():
        def samples(turns, total):
            group = [turns * 4 + inner for inner in range(4)]
            xs = [matrix(b) for b in group]
            ggs = [gg_all[back * ROWS + b] for b in group]
            mgs = [
                jnp.dot(gg, xb, preferred_element_type=F32).astype(BF) for gg, xb in zip(ggs, xs)
            ]
            for mg, xb in zip(mgs, xs):
                total = total + lax.dot_general(mg, xb, NT, preferred_element_type=F32)
            for b, gg, mg in zip(group, ggs, mgs):
                left = jnp.concatenate([gg, projt_ref[...]], axis=0)
                right = jnp.concatenate([mixed_all[back * ROWS + b], mg], axis=0)
                fg = lax.dot_general(left, right, TN, preferred_element_type=F32) * SCALE
                fg = fg.reshape(16, 2, 8, 256)
                even = fg[:, 0].reshape(PAIRS, 256)
                odd = fg[:, 1].reshape(PAIRS, 256)
                r0 = pltpu.roll(odd[:, :128], 64, 1)
                r1 = pltpu.roll(odd[:, 128:], 64, 1)
                ready[pl.ds(b, PAIRS, stride=3 * PAD), :] = even[:, :128]
                ready[pl.ds(b + PAD, PAIRS, stride=3 * PAD), :] = jnp.where(low, even[:, 128:], r0)
                ready[pl.ds(b + 2 * PAD, PAIRS, stride=3 * PAD), :] = jnp.where(low, r0, r1)
            return total

        pg_ref[...] += lax.fori_loop(0, ROWS // 4, samples, jnp.zeros((K, F), F32)) * SCALE

        @pl.when(back >= SLOTS)
        def _():
            for copy in copies(back - SLOTS, slot):
                copy.wait_send()
            own_copy(back - SLOTS, slot).wait()

        def pack(q, carry):
            for kind in range(2):
                for last in range(4):
                    first, second = q // 4, q % 4
                    if kind == 0:
                        owner = ((first * 4 + second) * 4 + last) * 2
                    else:
                        owner = ((second * 4 + first) * 4 + last) * 2 + 1
                    for tile in range(3):
                        at = pl.ds((owner * 3 + tile) * PAD, ROWS)
                        stage[slot, kind * 64 + q * 4 + last, :, tile * 128 : tile * 128 + 128] = ready[
                            at, :
                        ].astype(BF)
            return carry

        lax.fori_loop(0, 16, pack, 0)
        for copy in copies(back, slot):
            copy.start()
        own_copy(back, slot).start()

    @pl.when(back == 0)
    def _():
        weight_grads(0)

    @pl.when(back == 1)
    def _():
        weight_grads(K // 2)

        def pack_wgrad(chip, carry):
            give[chip] = turned[
                pl.ds((chip * 2 + 1 - core) * (2 * K + 1), 2 * K), :
            ].astype(BF)
            return carry

        lax.fori_loop(0, 64, pack_wgrad, 0)
        weight_copy().start()

    @pl.when(back == STEPS - 1)
    def _():
        for du, dv in blocks:
            to_sibling(du, dv).wait_send()
        for dv, dz in plane:
            segments_from(dv, dz).wait_recv()
            segments_to(dv, dz).wait_send()
        for d in range(1, 4):
            along_u(d).wait_send()
            for du in range(4):
                along_v(d, du).wait_send()
        seg_copy.wait()
        for ago in range(SLOTS):
            sent, where = back - ago, lax.rem(slot + SLOTS - ago, SLOTS)
            for copy in copies(sent, where):
                copy.wait_send()
            own_copy(sent, where).wait()
        for d in range(1, 4):
            weight_z(d).wait_recv()

        def sum_z(n, carry):
            total = give[z * 16 + n].astype(F32) + w2_in[0, n].astype(F32)
            total = total + (w2_in[1, n].astype(F32) + w2_in[2, n].astype(F32))
            wz_ref[n] = total.astype(BF)
            return carry

        lax.fori_loop(0, 16, sum_z, 0)
        for d in range(1, 4):
            weight_z(d).wait_send()

        def arrived(block, carry):
            def wait(sender, sem):
                at = pl.ds(sender * 128 + block * ROWS, ROWS)
                pltpu.make_async_remote_copy(
                    src_ref=stage.at[0, pl.ds(0, 16)],
                    dst_ref=rows_ref.at[:, at],
                    send_sem=send_sem.at[0, 0],
                    recv_sem=recv_sem.at[block, sem],
                    device_id=sibling,
                    device_id_type=MESH,
                ).wait_recv()

            wait(line * 2 + 1 - core, 0)
            for d in range(1, 4):
                for other in range(2):
                    wait(lax.rem(line + 4 - d, 4) * 2 + other, d * 2 + other)
            return carry

        lax.fori_loop(0, STEPS, arrived, 0)


def main(x, projt, own, cut, cot):
    batch = x.shape[0]
    any_space = pl.BlockSpec(memory_space=pl.ANY)
    dma = pltpu.SemaphoreType.DMA
    return pl.pallas_call(
        main_kernel,
        grid=(2 * STEPS,),
        in_specs=[
            pl.BlockSpec((ROWS, F * E), lambda i: (lax.rem(i, STEPS), 0)),
            pl.BlockSpec((K, F), lambda i: (0, 0)),
            any_space,
            any_space,
            pl.BlockSpec((batch, H), lambda i: (0, 0)),
        ],
        out_specs=[
            pl.BlockSpec((K, F), lambda i: (0, 0)),
            any_space,
            pl.BlockSpec((16, 2 * K, H), lambda i: (0, 0, 0)),
            any_space,
        ],
        out_shape=[
            jax.ShapeDtypeStruct((K, F), F32),
            jax.ShapeDtypeStruct((16, 8 * batch, 2 * E), BF),
            jax.ShapeDtypeStruct((16, 2 * K, H), BF),
            jax.ShapeDtypeStruct(cut.shape, jnp.int32),
        ],
        scratch_shapes=[
            pltpu.VMEM((F * E // 128 * ROWS, 128), F32),
            pltpu.VMEM((3 * PAIRS * PAD, 128), F32),
            pltpu.VMEM((batch, K, 256), BF),
            pltpu.VMEM((K, batch, F), BF),
            pltpu.VMEM((16,) + own.shape, BF),
            pltpu.VMEM((batch, H), BF),
            pltpu.VMEM((batch, K, F), BF),
            pltpu.VMEM((2 * batch * (K + 1), H), F32),
            pltpu.VMEM((SLOTS, PAIRS, ROWS, 2 * E), BF),
            pltpu.VMEM((64, 2 * K, H), BF),
            pltpu.VMEM((64, 2 * K, H), BF),
            pltpu.VMEM((3, 16, 2 * K, H), BF),
            dma((3,)),
            dma((3,)),
            dma((3, 4)),
            dma((3, 4)),
            dma((4, 4)),
            dma((4, 4)),
            dma((4, 4)),
            dma((4, 4)),
            dma((2,)),
            dma((SLOTS, 7)),
            dma((STEPS, 8)),
            dma((SLOTS,)),
            dma((2,)),
            dma((3,)),
            dma((3,)),
        ],
        compiler_params=pltpu.CompilerParams(
            vmem_limit_bytes=VMEM_LIMIT, collective_id=1, has_side_effects=True
        ),
        cost_estimate=pl.CostEstimate(
            flops=18 * batch * F * E * K, bytes_accessed=60_000_000, transcendentals=batch * H
        ),
        name="main",
    )(x, projt, own, cut, cot)


SLOT_BLOCK = 256
HALF = UNIQUE_CAP // 2
FIRST = 128
ORDER = (1, 2, 3, 0)


def sums_kernel(
    rows_ref, seg_ref, wz_ref, pg_ref,
    wout_ref, pout_ref, out_ref,
    data, table, az, bv, sum_a, sum_b, va, zb, w3_in, w4, w4_in, pu, pv, pz, pc,
    load_sem, az_send, az_recv, bv_send, bv_recv, va_send, va_recv, zb_send, zb_recv,
    w_send, w_recv, p_send, p_recv,
):
    x, y, z, core = place()
    u = jnp.where(core == 0, x, y)
    v = jnp.where(core == 0, y, x)
    low = lower_half(SLOT_BLOCK)

    def at_u(d):
        moved = turn(u, d)
        return device(jnp.where(core == 0, moved, x), jnp.where(core == 0, y, moved), z, core)

    def at_v(d):
        moved = turn(v, d)
        return device(jnp.where(core == 0, x, moved), jnp.where(core == 0, moved, y), z, core)

    def at_z(d):
        return device(x, y, turn(z, d), core)

    sibling = device(x, y, z, 1 - core)

    def load(dz, dv):
        j = turn(v, dv) * 4 + turn(z, dz)
        return pltpu.make_async_copy(rows_ref.at[j], data.at[dz, dv], load_sem.at[dz, dv])

    for dz in ORDER:
        for dv in ORDER:
            load(dz, dv).start()

    greet([to(d) for d in range(1, 4) for to in (at_u, at_v, at_z)] + [sibling])

    def spread(buffer, mine, stage, to):
        return [
            remote(buffer.at[mine], buffer.at[mine], p_send.at[stage, d - 1], p_recv.at[stage, d - 1], to(d))
            for d in range(1, 4)
        ]

    def gathered(buffer, mine, stage, to):
        for d in range(1, 4):
            there = buffer.at[turn(mine, -d)]
            remote(there, there, p_send.at[stage, d - 1], p_recv.at[stage, d - 1], to(d)).wait_recv()
        return (buffer[0] + buffer[1]) + (buffer[2] + buffer[3])

    def start(copies):
        for copy in copies:
            copy.start()
        return copies

    def send_a(dz, dv):
        return remote(
            table.at[dz, dv, pl.ds(0, FIRST)],
            az.at[dz - 1, dv],
            az_send.at[dz - 1, dv],
            az_recv.at[dz - 1, dv],
            at_z(dz),
        )

    def send_b(dv, dz):
        return remote(
            table.at[dz, dv, pl.ds(FIRST, HALF - FIRST)],
            bv.at[dv - 1, dz],
            bv_send.at[dv - 1, dz],
            bv_recv.at[dv - 1, dz],
            at_v(dv),
        )

    def second_a(dv):
        return remote(sum_a.at[dv], va.at[dv - 1], va_send.at[dv - 1], va_recv.at[dv - 1], at_v(dv))

    def second_b(dz):
        return remote(sum_b.at[dz], zb.at[dz - 1], zb_send.at[dz - 1], zb_recv.at[dz - 1], at_z(dz))

    def one_table(dz, dv):
        load(dz, dv).wait()
        j = turn(v, dv) * 4 + turn(z, dz)
        slot = lax.broadcasted_iota(jnp.int32, (SLOT_BLOCK, 8 * 128), 0)

        def part(block, parity):
            seg = seg_ref[j, parity : parity + 1, :] - block * SLOT_BLOCK
            hot = jnp.where(slot == seg, 1.0, 0.0).astype(BF)
            found = jnp.dot(
                hot, data[dz, dv, :, parity * 128 : parity * 128 + 256], preferred_element_type=F32
            )
            return found[:, :128], found[:, 128:]

        for block in range(HALF // SLOT_BLOCK):
            at = pl.ds(block * SLOT_BLOCK, SLOT_BLOCK)
            even0, even1 = part(block, 0)
            odd0, odd1 = part(block, 1)
            r0 = pltpu.roll(odd0, 64, 1)
            r1 = pltpu.roll(odd1, 64, 1)
            table[dz, dv, at, 0:128] = (even0 + jnp.where(low, r0, r1)).astype(BF)
            first = even1 + r1
            even0, even1 = part(block + HALF // SLOT_BLOCK, 0)
            odd0, odd1 = part(block + HALF // SLOT_BLOCK, 1)
            r0 = pltpu.roll(even0, 64, 1)
            r1 = pltpu.roll(even1, 64, 1)
            table[dz, dv, at, 128:256] = jnp.where(low, first, r0 + odd0).astype(BF)
            table[dz, dv, at, 256:384] = (jnp.where(low, r0, r1) + odd1).astype(BF)

    def tables(dz):
        def one(turns, carry):
            dv = lax.rem(turns + 1, 4)
            one_table(dz, dv)
            if dz > 0:
                send_a(dz, dv).start()

            @pl.when(dv > 0)
            def _():
                send_b(dv, dz).start()

            return carry

        lax.fori_loop(0, 4, one, 0)

    def add_four(first, second, third, fourth, target, size):
        rows = first.shape[0]

        def one(n, carry):
            at = pl.ds(pl.multiple_of(n * size, size), size)
            total = (first[at].astype(F32) + second[at].astype(F32)) + (
                third[at].astype(F32) + fourth[at].astype(F32)
            )
            target[at] = total.astype(target.dtype)
            return carry

        lax.fori_loop(0, rows // size, one, 0)

    def total_b(dz):
        for dv in range(1, 4):
            send_b(dv, dz).wait_recv()
        mine = table.at[dz, 0, pl.ds(FIRST, HALF - FIRST)]
        add_four(mine, bv.at[0, dz], bv.at[1, dz], bv.at[2, dz], sum_b.at[dz], 64)
        if dz > 0:
            second_b(dz).start()

    def total_a(dv):
        for dz in range(1, 4):
            send_a(dz, dv).wait_recv()
        mine = table.at[0, dv, pl.ds(0, FIRST)]
        add_four(mine, az.at[0, dv], az.at[1, dv], az.at[2, dv], sum_a.at[dv], 64)
        if dv > 0:
            second_a(dv).start()

    def w_copies(source, arrive, stage, to, line, size):
        return [
            remote(
                source.at[pl.ds(turn(line, d) * size, size)],
                arrive.at[d - 1],
                w_send.at[stage, d - 1],
                w_recv.at[stage, d - 1],
                to(d),
            )
            for d in range(1, 4)
        ]

    pu[u] = pg_ref[...]
    p0 = start(spread(pu, u, 0, at_u))
    s3 = start(w_copies(wz_ref, w3_in, 0, at_u, u, 4))
    tables(1)
    pv[v] = gathered(pu, u, 0, at_u)
    p1 = start(spread(pv, v, 1, at_v))
    for copy in s3:
        copy.wait_recv()
    add_four(wz_ref.at[pl.ds(u * 4, 4)], w3_in.at[0], w3_in.at[1], w3_in.at[2], w4, 1)
    s4 = start(w_copies(w4, w4_in, 1, at_v, v, 1))
    tables(2)
    total_b(1)
    pz[z] = gathered(pv, v, 1, at_v)
    p2 = start(spread(pz, z, 2, at_z))
    tables(3)
    total_b(2)
    pc[core] = gathered(pz, z, 2, at_z)
    p3 = remote(pc.at[core], pc.at[core], p_send.at[3, 0], p_recv.at[3, 0], sibling)
    p3.start()
    for copy in s4:
        copy.wait_recv()
    total = w4[v].astype(F32) + w4_in[0, 0].astype(F32)
    wout_ref[...] = total + (w4_in[1, 0].astype(F32) + w4_in[2, 0].astype(F32))
    tables(0)
    total_b(3)
    for dv in ORDER:
        total_a(dv)
    total_b(0)
    remote(pc.at[1 - core], pc.at[1 - core], p_send.at[3, 0], p_recv.at[3, 0], sibling).wait_recv()
    pout_ref[...] = pc[0] + pc[1]

    def finish(mine, others, start_row, rows):
        def one(part, carry):
            at = pl.ds(pl.multiple_of(part * 64, 64), 64)
            before = pl.ds(pl.multiple_of(part * 64 + start_row, 64), 64)
            after = pl.ds(pl.multiple_of(part * 64 + start_row + HALF, 64), 64)
            total = mine[at, :].astype(F32) + others[0, at].astype(F32)
            total = total + (others[1, at].astype(F32) + others[2, at].astype(F32))
            out_ref[before, :] = total[:, :E]
            r1 = pltpu.roll(total[:, 128:256], 64, 1)
            r2 = pltpu.roll(total[:, 256:], 64, 1)
            out_ref[after, :128] = jnp.where(lower_half(64), r1, r2)
            out_ref[after, 128:] = r2[:, :64]
            return carry

        lax.fori_loop(0, rows // 64, one, 0)

    for d in range(1, 4):
        second_a(d).wait_recv()
    finish(sum_a.at[0], va, 0, FIRST)
    for d in range(1, 4):
        second_b(d).wait_recv()
    finish(sum_b.at[0], zb, FIRST, HALF - FIRST)

    for copy in p0 + p1 + p2 + [p3] + s3 + s4:
        copy.wait_send()
    for d in range(1, 4):
        second_a(d).wait_send()
        second_b(d).wait_send()
        for n in range(4):
            send_a(d, n).wait_send()
            send_b(d, n).wait_send()


def sums(rows, seg, wz, pg):
    any_space = pl.BlockSpec(memory_space=pl.ANY)
    whole = pl.BlockSpec(memory_space=pltpu.VMEM)
    dma = pltpu.SemaphoreType.DMA
    rest = HALF - FIRST
    return pl.pallas_call(
        sums_kernel,
        in_specs=[any_space, whole, whole, whole],
        out_specs=[whole] * 3,
        out_shape=[
            jax.ShapeDtypeStruct((2 * K, H), F32),
            jax.ShapeDtypeStruct((K, F), F32),
            jax.ShapeDtypeStruct((UNIQUE_CAP, E), F32),
        ],
        scratch_shapes=[
            pltpu.VMEM((4, 4) + rows.shape[1:], BF),
            pltpu.VMEM((4, 4, HALF, 2 * E), BF),
            pltpu.VMEM((3, 4, FIRST, 2 * E), BF),
            pltpu.VMEM((3, 4, rest, 2 * E), BF),
            pltpu.VMEM((4, FIRST, 2 * E), BF),
            pltpu.VMEM((4, rest, 2 * E), BF),
            pltpu.VMEM((3, FIRST, 2 * E), BF),
            pltpu.VMEM((3, rest, 2 * E), BF),
            pltpu.VMEM((3, 4, 2 * K, H), BF),
            pltpu.VMEM((4, 2 * K, H), BF),
            pltpu.VMEM((3, 1, 2 * K, H), BF),
            pltpu.VMEM((4, K, F), F32),
            pltpu.VMEM((4, K, F), F32),
            pltpu.VMEM((4, K, F), F32),
            pltpu.VMEM((2, K, F), F32),
            dma((4, 4)),
            dma((3, 4)),
            dma((3, 4)),
            dma((3, 4)),
            dma((3, 4)),
            dma((3,)),
            dma((3,)),
            dma((3,)),
            dma((3,)),
            dma((2, 3)),
            dma((2, 3)),
            dma((4, 3)),
            dma((4, 3)),
        ],
        compiler_params=pltpu.CompilerParams(
            vmem_limit_bytes=VMEM_LIMIT, collective_id=2, has_side_effects=True
        ),
        cost_estimate=pl.CostEstimate(
            flops=16 * 4 * UNIQUE_CAP * 1024 * 256, bytes_accessed=30_000_000, transcendentals=0
        ),
        name="sums",
    )(rows, seg, wz, pg)


def turn_features(a):
    rest = a.shape[1:]
    return a.reshape((-1, 8, 2) + rest).swapaxes(1, 2).reshape(a.shape)


def unturn_features(a):
    rest = a.shape[1:]
    return a.reshape((-1, 2, 8) + rest).swapaxes(1, 2).reshape(a.shape)


def cut_segments(segments):
    core = lax.axis_index("emb") % 2
    seg = segments.T.reshape(2, 4, 4, 4, 2, 128)
    along_x = seg.transpose(2, 3, 0, 1, 4, 5).reshape(16, 2, 1024)
    along_y = seg.transpose(1, 3, 0, 2, 4, 5).reshape(16, 2, 1024)
    return jnp.where(core == 0, along_x, along_y)


def on_device(pooled, projection, out_weight, cotangent, segments):
    own = turn_features(out_weight.reshape(-1, K, H)).swapaxes(0, 1)
    projt = turn_features(projection).T
    pg, rows, wz, seg = main(pooled, projt, own, cut_segments(segments), cotangent)
    weight_grad, pg, row_grad = sums(rows, seg, wz, pg)
    return (weight_grad, unturn_features(pg.T), row_grad)


def solution(mesh):
    placed = (
        P(("fsdp", "emb"), None),
        P(),
        P("fsdp", None),
        P(("fsdp", "emb"), None),
        P(None, ("fsdp", "emb")),
    )
    return jax.shard_map(
        on_device,
        mesh=mesh,
        in_specs=placed,
        out_specs=(P(("fsdp", "emb"), None), P(), P(("fsdp", "emb"), None)),
        check_vma=False,
    )
```

```python
import functools

import jax
import jax.numpy as jnp
from jax import lax
from jax.experimental import pallas as pl
from jax.experimental.pallas import tpu as pltpu
from jax.sharding import PartitionSpec as P

F = 256
E = 192
K = 96
H = 128
UNIQUE_CAP = 1024
PAIRS = F // 2
ROWS = 16
SCALE = E ** (-0.5)
BF = jnp.bfloat16
F32 = jnp.float32
VMEM_LIMIT = 60 * 1024 * 1024
NT = (((1,), (1,)), ((), ()))
TN = (((0,), (0,)), ((), ()))


def interleave(even, odd):
    width = even.shape[-1]
    both = jnp.concatenate([even.reshape(16, 8, width), odd.reshape(16, 8, width)], axis=1)
    return both.reshape(F, width)


def reorder(dtype):
    column = lax.broadcasted_iota(jnp.int32, (F, F), 1)
    within = column & 15
    natural = (column - within) + (within & 7) * 2 + (within >> 3)
    return jnp.where(lax.broadcasted_iota(jnp.int32, (F, F), 0) == natural, 1.0, 0.0).astype(dtype)


def lower_half(rows):
    return lax.broadcasted_iota(jnp.int32, (rows, 128), 1) < 64


MESH = pl.DeviceIdType.MESH


def place():
    fsdp = lax.axis_index("fsdp")
    emb = lax.axis_index("emb")
    return fsdp // 4, fsdp % 4, emb // 2, emb % 2


def device(x, y, z, core):
    return (x * 4 + y, z * 2 + core)


def turn(at, d):
    return lax.rem(at + 4 + d, 4)


def greet(devices):
    barrier = pltpu.get_barrier_semaphore()
    for to in devices:
        pl.semaphore_signal(barrier, inc=1, device_id=to, device_id_type=MESH)
    pl.semaphore_wait(barrier, len(devices))


def remote(source, target, send, recv, to):
    return pltpu.make_async_remote_copy(
        src_ref=source,
        dst_ref=target,
        send_sem=send,
        recv_sem=recv,
        device_id=to,
        device_id_type=MESH,
    )


SLOTS = 3
PAD = ROWS + 1
STEPS = 8


def main_kernel(
    x_ref, natural_ref, own_ref, cut_ref, cot_ref,
    pg_ref, rows_ref, wz_ref, seg_ref,
    projt_ref, wide, ready, mixed_all, gram, weight_ref, slope_ref, gg_all, turned, stage, give, other, w2_in,
    u_send, u_recv, v_send, v_recv, s_send, s_recv, g_send, g_recv, first_sem,
    send_sem, recv_sem, own_sem, pair_sem, z_send, z_recv,
):
    step = pl.program_id(0)
    batch = gram.shape[1]
    low = lower_half(PAIRS)
    x, y, z, core = place()
    u = jnp.where(core == 0, x, y)
    v = jnp.where(core == 0, y, x)
    line = u
    half = pl.ds(pl.multiple_of(core * (K // 2), K // 2), K // 2)
    other_half = pl.ds(pl.multiple_of((1 - core) * (K // 2), K // 2), K // 2)
    sibling = device(x, y, z, 1 - core)
    back = step - STEPS
    slot = lax.rem(step + SLOTS - STEPS % SLOTS, SLOTS)

    def at(du, dv, dz):
        moved_u, moved_v = turn(u, du), turn(v, dv)
        return device(
            jnp.where(core == 0, moved_u, moved_v),
            jnp.where(core == 0, moved_v, moved_u),
            turn(z, dz),
            core,
        )

    def block(du, dv):
        moved_u, moved_v = turn(u, du), turn(v, dv)
        return jnp.where(core == 0, moved_u * 4 + moved_v, moved_v * 4 + moved_u)

    def along_u(d):
        return remote(
            own_ref.at[half], weight_ref.at[block(0, 0), half], u_send.at[d - 1], u_recv.at[d - 1], at(d, 0, 0)
        )

    def from_u(d):
        there = weight_ref.at[block(-d, 0), half]
        return remote(there, there, u_send.at[d - 1], u_recv.at[d - 1], at(d, 0, 0))

    def along_v(d, du):
        there = weight_ref.at[block(du, 0), half]
        source = own_ref.at[half] if du == 0 else there
        return remote(source, there, v_send.at[d - 1, du], v_recv.at[d - 1, du], at(0, d, 0))

    def from_v(d, du):
        there = weight_ref.at[block(du, -d), half]
        return remote(there, there, v_send.at[d - 1, du], v_recv.at[d - 1, du], at(0, d, 0))

    def to_sibling(du, dv):
        there = weight_ref.at[block(du, dv), half]
        return remote(there, there, s_send.at[du, dv % 4], s_recv.at[du, dv % 4], sibling)

    def from_sibling(du, dv):
        first = jnp.where(core == 0, turn(x, dv), turn(x, du))
        second = jnp.where(core == 0, turn(y, du), turn(y, dv))
        there = weight_ref.at[first * 4 + second, other_half]
        return remote(there, there, s_send.at[du, dv % 4], s_recv.at[du, dv % 4], sibling)

    def segment_parts(dv, dz):
        to_v, to_z = turn(v, dv), turn(z, dz)
        for along in range(4):
            chip = jnp.where(core == 0, along * 4 + to_v, to_v * 4 + along) * 4 + to_z
            source = cut_ref.at[:, pl.ds(pl.multiple_of(chip * 256, 256), 256)]
            yield along, source, seg_ref.at[v * 4 + z, :, pl.ds(along * 256, 256)]

    def segments_to(dv, dz):
        return [
            remote(source, there, g_send.at[dv, dz, n], g_recv.at[dv, dz, n], at(0, dv, dz))
            for n, source, there in segment_parts(dv, dz)
        ]

    def segments_from(dv, dz):
        found = []
        for n in range(4):
            there = seg_ref.at[turn(v, -dv) * 4 + turn(z, -dz), :, pl.ds(n * 256, 256)]
            found.append(remote(there, there, g_send.at[dv, dz, n], g_recv.at[dv, dz, n], at(0, dv, dz)))
        return found

    def segments_own():
        return [
            pltpu.make_async_copy(source, there, g_send.at[0, 0, n])
            for n, source, there in segment_parts(0, 0)
        ]

    def weight_copy():
        return remote(give, other, pair_sem.at[0], pair_sem.at[1], sibling)

    def weight_z(d):
        there = turn(z, d)
        to = device(x, y, there, core)
        return remote(give.at[pl.ds(there * 16, 16)], w2_in.at[d - 1], z_send.at[d - 1], z_recv.at[d - 1], to)

    def copies(block, where):
        at_x = pl.ds((x * 2 + core) * 128 + block * ROWS, ROWS)
        at_y = pl.ds((y * 2 + core) * 128 + block * ROWS, ROWS)
        found = []
        for d in range(1, 4):
            tx = lax.rem(x + d, 4)
            ty = lax.rem(y + d, 4)
            for kind, group, rows, target in (
                (0, tx, at_x, device(tx, y, z, 0)),
                (1, 4 + ty, at_y, device(x, ty, z, 1)),
            ):
                found.append(
                    pltpu.make_async_remote_copy(
                        src_ref=stage.at[where, pl.ds(group * 16, 16)],
                        dst_ref=rows_ref.at[:, rows],
                        send_sem=send_sem.at[where, kind * 3 + d - 1],
                        recv_sem=recv_sem.at[block, d * 2 + core],
                        device_id=target,
                        device_id_type=MESH,
                    )
                )
        group = jnp.where(core == 0, 4 + y, x)
        there = pl.ds((jnp.where(core == 0, y, x) * 2 + core) * 128 + block * ROWS, ROWS)
        found.append(
            pltpu.make_async_remote_copy(
                src_ref=stage.at[where, pl.ds(group * 16, 16)],
                dst_ref=rows_ref.at[:, there],
                send_sem=send_sem.at[where, 6],
                recv_sem=recv_sem.at[block, 0],
                device_id=sibling,
                device_id_type=MESH,
            )
        )
        return found

    def own_copy(block, where):
        group = jnp.where(core == 0, x, 4 + y)
        here = pl.ds((line * 2 + core) * 128 + block * ROWS, ROWS)
        return pltpu.make_async_copy(
            stage.at[where, pl.ds(group * 16, 16)], rows_ref.at[:, here], own_sem.at[where]
        )

    plane = [(dv, dz) for dv in range(4) for dz in range(4) if dv or dz]
    blocks = [(du, dv) for du in range(4) for dv in range(4) if du or dv]
    weight_copy_own = pltpu.make_async_copy(own_ref, weight_ref.at[block(0, 0)], first_sem.at[0])

    def pass_on(arrived):
        for du in arrived:
            for d in range(1, 4):
                from_v(d, du).wait_recv()
                to_sibling(du, 4 - d).start()

    @pl.when(step == 0)
    def _():
        pg_ref[...] = jnp.zeros_like(pg_ref)
        projt_ref[...] = jnp.dot(
            natural_ref[...], reorder(BF), preferred_element_type=F32
        ).astype(BF)
        senders = [at(d, 0, 0) for d in range(1, 4)] + [at(0, dv, dz) for dv, dz in plane] + [sibling]
        for d in range(1, 4):
            moved = turn(u, d)
            senders.append(
                device(jnp.where(core == 0, moved, x), jnp.where(core == 0, y, moved), z, 1 - core)
            )
        greet(senders)
        for d in range(1, 4):
            along_u(d).start()
        for d in range(1, 4):
            along_v(d, 0).start()
        weight_copy_own.start()

    @pl.when(step == 1)
    def _():
        for d in (1, 3, 2):
            from_u(d).wait_recv()
            for dv in range(1, 4):
                along_v(dv, 4 - d).start()
            to_sibling(4 - d, 0).start()

    @pl.when(step == 2)
    def _():
        for copy in segments_own():
            copy.start()
        for dv, dz in plane:
            for copy in segments_to(dv, dz):
                copy.start()

    @pl.when(step == 3)
    def _():
        pass_on((0,))

    @pl.when(step == 6)
    def _():
        pass_on((1, 3))

    def spread(turns, carry):
        for inner in range(8):
            tile = turns * 8 + inner
            wide[pl.ds(pl.multiple_of(tile * ROWS, ROWS), ROWS), :] = x_ref[
                :, pl.ds(pl.multiple_of(tile * 128, 128), 128)
            ].astype(F32)
        return carry

    lax.fori_loop(0, F * E // 1024, spread, 0)

    def matrix(b):
        a0 = wide[pl.ds(b, PAIRS, stride=3 * ROWS), :]
        a1 = wide[pl.ds(b + ROWS, PAIRS, stride=3 * ROWS), :]
        a2 = wide[pl.ds(b + 2 * ROWS, PAIRS, stride=3 * ROWS), :]
        r1 = pltpu.roll(a1, 64, 1)
        r2 = pltpu.roll(a2, 64, 1)
        even = jnp.concatenate([a0, jnp.where(low, a1, 0.0)], axis=1)
        odd = jnp.concatenate([jnp.where(low, r1, r2), jnp.where(low, r2, 0.0)], axis=1)
        return interleave(even, odd).astype(BF)

    @pl.when(step < STEPS)
    def _():
        def samples(turns, carry):
            group = [turns * 4 + inner for inner in range(4)]
            xs = [matrix(b) for b in group]
            mixed = [
                jnp.dot(projt_ref[...], xb, preferred_element_type=F32).astype(BF) for xb in xs
            ]
            grams = [
                lax.dot_general(m, xb, NT, preferred_element_type=F32) * SCALE
                for m, xb in zip(mixed, xs)
            ]
            for b, m, gram_b in zip(group, mixed, grams):
                mixed_all[step * ROWS + b] = m
                turned[pl.ds(b, K, stride=PAD), :] = gram_b[:, :128]
                turned[pl.ds(K * PAD + b, K, stride=PAD), :] = gram_b[:, 128:]
            return carry

        lax.fori_loop(0, ROWS // 4, samples, 0)
        rows = pl.ds(pl.multiple_of(step * ROWS, ROWS), ROWS)

        def pack_gram(turns, carry):
            for inner in range(8):
                k = turns * 8 + inner
                for part in range(2):
                    at = pl.ds((part * K + k) * PAD, ROWS)
                    gram[k, rows, part * 128 : part * 128 + 128] = turned[at, :].astype(BF)
            return carry

        lax.fori_loop(0, K // 8, pack_gram, 0)

    @pl.when(step == STEPS - 1)
    def _():
        pass_on((2,))

    def gram_grads():
        def gram_grad(turns, carry):
            for inner in range(4):
                k = turns * 4 + inner
                gg = lax.dot_general(
                    slope_ref[...], weight_ref[:, k].reshape(F, H), NT, preferred_element_type=F32
                )
                turned[pl.ds(k, batch, stride=K + 1), :] = gg[:, :128]
                turned[pl.ds(batch * (K + 1) + k, batch, stride=K + 1), :] = gg[:, 128:]
            return carry

        lax.fori_loop(0, K // 4, gram_grad, 0)

        def pack_gg(turns, carry):
            for inner in range(4):
                b = turns * 4 + inner
                for part in range(2):
                    gg_all[b, :, part * 128 : part * 128 + 128] = turned[
                        pl.ds((part * batch + b) * (K + 1), K), :
                    ].astype(BF)
            return carry

        lax.fori_loop(0, batch // 4, pack_gg, 0)

    def weight_grads(first):
        def one(turns, carry):
            for inner in range(4):
                k = first + turns * 4 + inner
                wgrad = lax.dot_general(gram[k], slope_ref[...], TN, preferred_element_type=F32)
                for block in range(16):
                    for parity in range(2):
                        at = block * 16 + parity * 8
                        turned[
                            pl.ds(block * 8 * (2 * K + 1) + parity * K + k, 8, stride=2 * K + 1), :
                        ] = wgrad[at : at + 8]
            return carry

        lax.fori_loop(0, K // 8, one, 0)

    @pl.when(step == STEPS)
    def _():
        weight_copy_own.wait()
        for du, dv in blocks:
            from_sibling(du, dv).wait_recv()

        def product(turns, total):
            for inner in range(8):
                k = turns * 8 + inner
                total = total + jnp.dot(
                    gram[k], weight_ref[:, k].reshape(F, H), preferred_element_type=F32
                )
            return total

        preact = lax.fori_loop(0, K // 8, product, jnp.zeros((batch, H), F32))
        sig = jax.nn.sigmoid(preact)
        slope_ref[...] = (
            cot_ref[...].astype(F32) * sig * (1.0 + preact * (1.0 - sig))
        ).astype(BF)
        gram_grads()

    @pl.when(back == 2)
    def _():
        weight_copy().wait_send()
        weight_copy().wait_recv()

        def pair_sum(n, carry):
            to_z, first, second = n // 16, (n // 4) % 4, n % 4
            chip = jnp.where(core == 0, first * 4 + second, second * 4 + first) * 4 + to_z
            mine = turned[pl.ds((chip * 2 + core) * (2 * K + 1), 2 * K), :]
            give[n] = (mine + other[chip].astype(F32)).astype(BF)
            return carry

        lax.fori_loop(0, 64, pair_sum, 0)
        for d in range(1, 4):
            weight_z(d).start()

    @pl.when(step >= STEPS)
    def _():
        def samples(turns, total):
            group = [turns * 4 + inner for inner in range(4)]
            xs = [matrix(b) for b in group]
            ggs = [gg_all[back * ROWS + b] for b in group]
            mgs = [
                jnp.dot(gg, xb, preferred_element_type=F32).astype(BF) for gg, xb in zip(ggs, xs)
            ]
            for mg, xb in zip(mgs, xs):
                total = total + lax.dot_general(mg, xb, NT, preferred_element_type=F32)
            for b, gg, mg in zip(group, ggs, mgs):
                left = jnp.concatenate([gg, projt_ref[...]], axis=0)
                right = jnp.concatenate([mixed_all[back * ROWS + b], mg], axis=0)
                fg = lax.dot_general(left, right, TN, preferred_element_type=F32) * SCALE
                fg = fg.reshape(16, 2, 8, 256)
                even = fg[:, 0].reshape(PAIRS, 256)
                odd = fg[:, 1].reshape(PAIRS, 256)
                r0 = pltpu.roll(odd[:, :128], 64, 1)
                r1 = pltpu.roll(odd[:, 128:], 64, 1)
                ready[pl.ds(b, PAIRS, stride=3 * PAD), :] = even[:, :128]
                ready[pl.ds(b + PAD, PAIRS, stride=3 * PAD), :] = jnp.where(low, even[:, 128:], r0)
                ready[pl.ds(b + 2 * PAD, PAIRS, stride=3 * PAD), :] = jnp.where(low, r0, r1)
            return total

        pg_ref[...] += lax.fori_loop(0, ROWS // 4, samples, jnp.zeros((K, F), F32)) * SCALE

        @pl.when(back >= SLOTS)
        def _():
            for copy in copies(back - SLOTS, slot):
                copy.wait_send()
            own_copy(back - SLOTS, slot).wait()

        def pack(q, carry):
            for kind in range(2):
                for last in range(4):
                    first, second = q // 4, q % 4
                    if kind == 0:
                        owner = ((first * 4 + second) * 4 + last) * 2
                    else:
                        owner = ((second * 4 + first) * 4 + last) * 2 + 1
                    for tile in range(3):
                        at = pl.ds((owner * 3 + tile) * PAD, ROWS)
                        stage[slot, kind * 64 + q * 4 + last, :, tile * 128 : tile * 128 + 128] = ready[
                            at, :
                        ].astype(BF)
            return carry

        lax.fori_loop(0, 16, pack, 0)
        for copy in copies(back, slot):
            copy.start()
        own_copy(back, slot).start()

    @pl.when(back == 0)
    def _():
        weight_grads(0)

    @pl.when(back == 1)
    def _():
        weight_grads(K // 2)

        def pack_wgrad(chip, carry):
            give[chip] = turned[
                pl.ds((chip * 2 + 1 - core) * (2 * K + 1), 2 * K), :
            ].astype(BF)
            return carry

        lax.fori_loop(0, 64, pack_wgrad, 0)
        weight_copy().start()

    @pl.when(back == STEPS - 1)
    def _():
        for du, dv in blocks:
            to_sibling(du, dv).wait_send()
        for dv, dz in plane:
            for copy in segments_from(dv, dz):
                copy.wait_recv()
            for copy in segments_to(dv, dz):
                copy.wait_send()
        for d in range(1, 4):
            along_u(d).wait_send()
            for du in range(4):
                along_v(d, du).wait_send()
        for copy in segments_own():
            copy.wait()
        for ago in range(SLOTS):
            sent, where = back - ago, lax.rem(slot + SLOTS - ago, SLOTS)
            for copy in copies(sent, where):
                copy.wait_send()
            own_copy(sent, where).wait()
        for d in range(1, 4):
            weight_z(d).wait_recv()

        def sum_z(n, carry):
            total = give[z * 16 + n].astype(F32) + w2_in[0, n].astype(F32)
            total = total + (w2_in[1, n].astype(F32) + w2_in[2, n].astype(F32))
            wz_ref[n] = total.astype(BF)
            return carry

        lax.fori_loop(0, 16, sum_z, 0)
        for d in range(1, 4):
            weight_z(d).wait_send()

        def arrived(block, carry):
            def wait(sender, sem):
                at = pl.ds(sender * 128 + block * ROWS, ROWS)
                pltpu.make_async_remote_copy(
                    src_ref=stage.at[0, pl.ds(0, 16)],
                    dst_ref=rows_ref.at[:, at],
                    send_sem=send_sem.at[0, 0],
                    recv_sem=recv_sem.at[block, sem],
                    device_id=sibling,
                    device_id_type=MESH,
                ).wait_recv()

            wait(line * 2 + 1 - core, 0)
            for d in range(1, 4):
                for other in range(2):
                    wait(lax.rem(line + 4 - d, 4) * 2 + other, d * 2 + other)
            return carry

        lax.fori_loop(0, STEPS, arrived, 0)


def main(x, projt, own, cut, cot):
    batch = x.shape[0]
    any_space = pl.BlockSpec(memory_space=pl.ANY)
    dma = pltpu.SemaphoreType.DMA
    return pl.pallas_call(
        main_kernel,
        grid=(2 * STEPS,),
        in_specs=[
            pl.BlockSpec((ROWS, F * E), lambda i: (lax.rem(i, STEPS), 0)),
            pl.BlockSpec((K, F), lambda i: (0, 0)),
            any_space,
            any_space,
            pl.BlockSpec((batch, H), lambda i: (0, 0)),
        ],
        out_specs=[
            pl.BlockSpec((K, F), lambda i: (0, 0)),
            any_space,
            pl.BlockSpec((16, 2 * K, H), lambda i: (0, 0, 0)),
            any_space,
        ],
        out_shape=[
            jax.ShapeDtypeStruct((K, F), F32),
            jax.ShapeDtypeStruct((16, 8 * batch, 2 * E), BF),
            jax.ShapeDtypeStruct((16, 2 * K, H), BF),
            jax.ShapeDtypeStruct((16, 2, 8 * batch), jnp.int32),
        ],
        scratch_shapes=[
            pltpu.VMEM((K, F), BF),
            pltpu.VMEM((F * E // 128 * ROWS, 128), F32),
            pltpu.VMEM((3 * PAIRS * PAD, 128), F32),
            pltpu.VMEM((batch, K, 256), BF),
            pltpu.VMEM((K, batch, F), BF),
            pltpu.VMEM((16,) + own.shape, BF),
            pltpu.VMEM((batch, H), BF),
            pltpu.VMEM((batch, K, F), BF),
            pltpu.VMEM((2 * batch * (K + 1), H), F32),
            pltpu.VMEM((SLOTS, PAIRS, ROWS, 2 * E), BF),
            pltpu.VMEM((64, 2 * K, H), BF),
            pltpu.VMEM((64, 2 * K, H), BF),
            pltpu.VMEM((3, 16, 2 * K, H), BF),
            dma((3,)),
            dma((3,)),
            dma((3, 4)),
            dma((3, 4)),
            dma((4, 4)),
            dma((4, 4)),
            dma((4, 4, 4)),
            dma((4, 4, 4)),
            dma((1,)),
            dma((SLOTS, 7)),
            dma((STEPS, 8)),
            dma((SLOTS,)),
            dma((2,)),
            dma((3,)),
            dma((3,)),
        ],
        compiler_params=pltpu.CompilerParams(
            vmem_limit_bytes=VMEM_LIMIT, collective_id=1, has_side_effects=True
        ),
        cost_estimate=pl.CostEstimate(
            flops=18 * batch * F * E * K, bytes_accessed=60_000_000, transcendentals=batch * H
        ),
        name="main",
    )(x, projt, own, cut, cot)


SLOT_BLOCK = 256
HALF = UNIQUE_CAP // 2
FIRST = 128
ORDER = (1, 2, 3, 0)


def sums_kernel(
    rows_ref, seg_ref, wz_ref, pg_ref,
    wout_ref, pout_ref, out_ref,
    data, table, az, bv, sum_a, sum_b, va, zb, w3_in, w4, w4_in, pu, pv, pz, pc,
    load_sem, az_send, az_recv, bv_send, bv_recv, va_send, va_recv, zb_send, zb_recv,
    w_send, w_recv, p_send, p_recv,
):
    x, y, z, core = place()
    u = jnp.where(core == 0, x, y)
    v = jnp.where(core == 0, y, x)
    low = lower_half(SLOT_BLOCK)

    def at_u(d):
        moved = turn(u, d)
        return device(jnp.where(core == 0, moved, x), jnp.where(core == 0, y, moved), z, core)

    def at_v(d):
        moved = turn(v, d)
        return device(jnp.where(core == 0, x, moved), jnp.where(core == 0, moved, y), z, core)

    def at_z(d):
        return device(x, y, turn(z, d), core)

    sibling = device(x, y, z, 1 - core)

    def load(dz, dv):
        j = turn(v, dv) * 4 + turn(z, dz)
        return pltpu.make_async_copy(rows_ref.at[j], data.at[dz, dv], load_sem.at[dz, dv])

    for dz in ORDER:
        for dv in ORDER:
            load(dz, dv).start()

    greet([to(d) for d in range(1, 4) for to in (at_u, at_v, at_z)] + [sibling])

    def spread(buffer, mine, stage, to):
        return [
            remote(buffer.at[mine], buffer.at[mine], p_send.at[stage, d - 1], p_recv.at[stage, d - 1], to(d))
            for d in range(1, 4)
        ]

    def gathered(buffer, mine, stage, to):
        for d in range(1, 4):
            there = buffer.at[turn(mine, -d)]
            remote(there, there, p_send.at[stage, d - 1], p_recv.at[stage, d - 1], to(d)).wait_recv()
        return (buffer[0] + buffer[1]) + (buffer[2] + buffer[3])

    def start(copies):
        for copy in copies:
            copy.start()
        return copies

    def send_a(dz, dv):
        return remote(
            table.at[dz, dv, pl.ds(0, FIRST)],
            az.at[dz - 1, dv],
            az_send.at[dz - 1, dv],
            az_recv.at[dz - 1, dv],
            at_z(dz),
        )

    def send_b(dv, dz):
        return remote(
            table.at[dz, dv, pl.ds(FIRST, HALF - FIRST)],
            bv.at[dv - 1, dz],
            bv_send.at[dv - 1, dz],
            bv_recv.at[dv - 1, dz],
            at_v(dv),
        )

    def second_a(dv):
        return remote(sum_a.at[dv], va.at[dv - 1], va_send.at[dv - 1], va_recv.at[dv - 1], at_v(dv))

    def second_b(dz):
        return remote(sum_b.at[dz], zb.at[dz - 1], zb_send.at[dz - 1], zb_recv.at[dz - 1], at_z(dz))

    def one_table(dz, dv):
        load(dz, dv).wait()
        j = turn(v, dv) * 4 + turn(z, dz)
        slot = lax.broadcasted_iota(jnp.int32, (SLOT_BLOCK, 8 * 128), 0)

        def part(block, parity):
            seg = seg_ref[j, parity : parity + 1, :] - block * SLOT_BLOCK
            hot = jnp.where(slot == seg, 1.0, 0.0).astype(BF)
            found = jnp.dot(
                hot, data[dz, dv, :, parity * 128 : parity * 128 + 256], preferred_element_type=F32
            )
            return found[:, :128], found[:, 128:]

        for block in range(HALF // SLOT_BLOCK):
            at = pl.ds(block * SLOT_BLOCK, SLOT_BLOCK)
            even0, even1 = part(block, 0)
            odd0, odd1 = part(block, 1)
            r0 = pltpu.roll(odd0, 64, 1)
            r1 = pltpu.roll(odd1, 64, 1)
            table[dz, dv, at, 0:128] = (even0 + jnp.where(low, r0, r1)).astype(BF)
            first = even1 + r1
            even0, even1 = part(block + HALF // SLOT_BLOCK, 0)
            odd0, odd1 = part(block + HALF // SLOT_BLOCK, 1)
            r0 = pltpu.roll(even0, 64, 1)
            r1 = pltpu.roll(even1, 64, 1)
            table[dz, dv, at, 128:256] = jnp.where(low, first, r0 + odd0).astype(BF)
            table[dz, dv, at, 256:384] = (jnp.where(low, r0, r1) + odd1).astype(BF)

    def tables(dz):
        def one(turns, carry):
            dv = lax.rem(turns + 1, 4)
            one_table(dz, dv)
            if dz > 0:
                send_a(dz, dv).start()

            @pl.when(dv > 0)
            def _():
                send_b(dv, dz).start()

            return carry

        lax.fori_loop(0, 4, one, 0)

    def add_four(first, second, third, fourth, target, size):
        rows = first.shape[0]

        def one(n, carry):
            at = pl.ds(pl.multiple_of(n * size, size), size)
            total = (first[at].astype(F32) + second[at].astype(F32)) + (
                third[at].astype(F32) + fourth[at].astype(F32)
            )
            target[at] = total.astype(target.dtype)
            return carry

        lax.fori_loop(0, rows // size, one, 0)

    def total_b(dz):
        for dv in range(1, 4):
            send_b(dv, dz).wait_recv()
        mine = table.at[dz, 0, pl.ds(FIRST, HALF - FIRST)]
        add_four(mine, bv.at[0, dz], bv.at[1, dz], bv.at[2, dz], sum_b.at[dz], 64)
        if dz > 0:
            second_b(dz).start()

    def total_a(dv):
        for dz in range(1, 4):
            send_a(dz, dv).wait_recv()
        mine = table.at[0, dv, pl.ds(0, FIRST)]
        add_four(mine, az.at[0, dv], az.at[1, dv], az.at[2, dv], sum_a.at[dv], 64)
        if dv > 0:
            second_a(dv).start()

    def w_copies(source, arrive, stage, to, line, size):
        return [
            remote(
                source.at[pl.ds(turn(line, d) * size, size)],
                arrive.at[d - 1],
                w_send.at[stage, d - 1],
                w_recv.at[stage, d - 1],
                to(d),
            )
            for d in range(1, 4)
        ]

    pu[u] = pg_ref[...]
    p0 = start(spread(pu, u, 0, at_u))
    s3 = start(w_copies(wz_ref, w3_in, 0, at_u, u, 4))
    tables(1)
    tables(2)
    pv[v] = gathered(pu, u, 0, at_u)
    p1 = start(spread(pv, v, 1, at_v))
    for copy in s3:
        copy.wait_recv()
    add_four(wz_ref.at[pl.ds(u * 4, 4)], w3_in.at[0], w3_in.at[1], w3_in.at[2], w4, 1)
    s4 = start(w_copies(w4, w4_in, 1, at_v, v, 1))
    total_b(1)
    tables(3)
    pz[z] = gathered(pv, v, 1, at_v)
    p2 = start(spread(pz, z, 2, at_z))
    total_b(2)
    tables(0)
    total_b(3)
    pc[core] = gathered(pz, z, 2, at_z)
    p3 = remote(pc.at[core], pc.at[core], p_send.at[3, 0], p_recv.at[3, 0], sibling)
    p3.start()
    for copy in s4:
        copy.wait_recv()
    total = w4[v].astype(F32) + w4_in[0, 0].astype(F32)
    wout_ref[...] = total + (w4_in[1, 0].astype(F32) + w4_in[2, 0].astype(F32))
    for dv in ORDER:
        total_a(dv)
    total_b(0)
    remote(pc.at[1 - core], pc.at[1 - core], p_send.at[3, 0], p_recv.at[3, 0], sibling).wait_recv()
    pout_ref[...] = lax.dot_general(
        pc[0] + pc[1],
        reorder(F32),
        NT,
        precision=lax.Precision.HIGHEST,
        preferred_element_type=F32,
    )

    def finish(mine, others, start_row, rows):
        def one(part, carry):
            at = pl.ds(pl.multiple_of(part * 128, 128), 128)
            before = pl.ds(pl.multiple_of(part * 128 + start_row, 128), 128)
            after = pl.ds(pl.multiple_of(part * 128 + start_row + HALF, 128), 128)
            total = mine[at, :].astype(F32) + others[0, at].astype(F32)
            total = total + (others[1, at].astype(F32) + others[2, at].astype(F32))
            r1 = pltpu.roll(total[:, 128:256], 64, 1)
            r2 = pltpu.roll(total[:, 256:], 64, 1)
            out_ref[:128, before] = total[:, :128].T
            out_ref[128:, before] = total[:, 128:256].T[:64]
            out_ref[:128, after] = jnp.where(lower_half(128), r1, r2).T
            out_ref[128:, after] = r2.T[:64]
            return carry

        lax.fori_loop(0, rows // 128, one, 0)

    for d in range(1, 4):
        second_a(d).wait_recv()
    finish(sum_a.at[0], va, 0, FIRST)
    for d in range(1, 4):
        second_b(d).wait_recv()
    finish(sum_b.at[0], zb, FIRST, HALF - FIRST)

    for copy in p0 + p1 + p2 + [p3] + s3 + s4:
        copy.wait_send()
    for d in range(1, 4):
        second_a(d).wait_send()
        second_b(d).wait_send()
        for n in range(4):
            send_a(d, n).wait_send()
            send_b(d, n).wait_send()


def sums(rows, seg, wz, pg):
    any_space = pl.BlockSpec(memory_space=pl.ANY)
    whole = pl.BlockSpec(memory_space=pltpu.VMEM)
    dma = pltpu.SemaphoreType.DMA
    rest = HALF - FIRST
    return pl.pallas_call(
        sums_kernel,
        in_specs=[any_space, whole, whole, whole],
        out_specs=[whole] * 3,
        out_shape=[
            jax.ShapeDtypeStruct((2 * K, H), F32),
            jax.ShapeDtypeStruct((K, F), F32),
            jax.ShapeDtypeStruct((E, UNIQUE_CAP), F32),
        ],
        scratch_shapes=[
            pltpu.VMEM((4, 4) + rows.shape[1:], BF),
            pltpu.VMEM((4, 4, HALF, 2 * E), BF),
            pltpu.VMEM((3, 4, FIRST, 2 * E), BF),
            pltpu.VMEM((3, 4, rest, 2 * E), BF),
            pltpu.VMEM((4, FIRST, 2 * E), BF),
            pltpu.VMEM((4, rest, 2 * E), BF),
            pltpu.VMEM((3, FIRST, 2 * E), BF),
            pltpu.VMEM((3, rest, 2 * E), BF),
            pltpu.VMEM((3, 4, 2 * K, H), BF),
            pltpu.VMEM((4, 2 * K, H), BF),
            pltpu.VMEM((3, 1, 2 * K, H), BF),
            pltpu.VMEM((4, K, F), F32),
            pltpu.VMEM((4, K, F), F32),
            pltpu.VMEM((4, K, F), F32),
            pltpu.VMEM((2, K, F), F32),
            dma((4, 4)),
            dma((3, 4)),
            dma((3, 4)),
            dma((3, 4)),
            dma((3, 4)),
            dma((3,)),
            dma((3,)),
            dma((3,)),
            dma((3,)),
            dma((2, 3)),
            dma((2, 3)),
            dma((4, 3)),
            dma((4, 3)),
        ],
        compiler_params=pltpu.CompilerParams(
            vmem_limit_bytes=VMEM_LIMIT, collective_id=2, has_side_effects=True
        ),
        cost_estimate=pl.CostEstimate(
            flops=16 * 4 * UNIQUE_CAP * 1024 * 256, bytes_accessed=30_000_000, transcendentals=0
        ),
        name="sums",
    )(rows, seg, wz, pg)


def turn_features(a):
    rest = a.shape[1:]
    return a.reshape((-1, 8, 2) + rest).swapaxes(1, 2).reshape(a.shape)


def on_device(pooled, projection, out_weight, cotangent, segments):
    own = turn_features(out_weight.reshape(-1, K, H)).swapaxes(0, 1)
    pg, rows, wz, seg = main(pooled, projection.T, own, segments.T, cotangent)
    weight_grad, pg, row_grad = sums(rows, seg, wz, pg)
    return (weight_grad, pg.T, row_grad.T)


def solution(mesh):
    placed = (
        P(("fsdp", "emb"), None),
        P(),
        P("fsdp", None),
        P(("fsdp", "emb"), None),
        P(None, ("fsdp", "emb")),
    )
    return jax.shard_map(
        on_device,
        mesh=mesh,
        in_specs=placed,
        out_specs=(P(("fsdp", "emb"), None), P(), P(("fsdp", "emb"), None)),
        check_vma=False,
    )
```

```python
import functools

import jax
import jax.numpy as jnp
from jax import lax
from jax.experimental import pallas as pl
from jax.experimental.pallas import tpu as pltpu
from jax.sharding import PartitionSpec as P

F = 256
E = 192
K = 96
H = 128
UNIQUE_CAP = 1024
PAIRS = F // 2
ROWS = 16
SCALE = E ** (-0.5)
BF = jnp.bfloat16
F32 = jnp.float32
VMEM_LIMIT = 60 * 1024 * 1024
NT = (((1,), (1,)), ((), ()))
TN = (((0,), (0,)), ((), ()))


def interleave(even, odd):
    width = even.shape[-1]
    both = jnp.concatenate([even.reshape(16, 8, width), odd.reshape(16, 8, width)], axis=1)
    return both.reshape(F, width)


def reorder(dtype):
    column = lax.broadcasted_iota(jnp.int32, (F, F), 1)
    within = column & 15
    natural = (column - within) + (within & 7) * 2 + (within >> 3)
    return jnp.where(lax.broadcasted_iota(jnp.int32, (F, F), 0) == natural, 1.0, 0.0).astype(dtype)


def lower_half(rows):
    return lax.broadcasted_iota(jnp.int32, (rows, 128), 1) < 64


MESH = pl.DeviceIdType.MESH


def place():
    fsdp = lax.axis_index("fsdp")
    emb = lax.axis_index("emb")
    return fsdp // 4, fsdp % 4, emb // 2, emb % 2


def device(x, y, z, core):
    return (x * 4 + y, z * 2 + core)


def turn(at, d):
    return lax.rem(at + 4 + d, 4)


def greet(devices):
    barrier = pltpu.get_barrier_semaphore()
    for to in devices:
        pl.semaphore_signal(barrier, inc=1, device_id=to, device_id_type=MESH)
    pl.semaphore_wait(barrier, len(devices))


def remote(source, target, send, recv, to):
    return pltpu.make_async_remote_copy(
        src_ref=source,
        dst_ref=target,
        send_sem=send,
        recv_sem=recv,
        device_id=to,
        device_id_type=MESH,
    )


SLOTS = 3
PAD = ROWS + 1
STEPS = 8


def main_kernel(
    x_ref, natural_ref, own_ref, cut_ref, cot_ref,
    pg_ref, rows_ref, wz_ref, seg_ref,
    projt_ref, wide, ready, mixed_all, gram, weight_ref, slope_ref, gg_all, turned, stage, give, other, w2_in,
    u_send, u_recv, v_send, v_recv, s_send, s_recv, g_send, g_recv, first_sem,
    send_sem, recv_sem, own_sem, pair_sem, z_send, z_recv,
):
    step = pl.program_id(0)
    batch = gram.shape[1]
    low = lower_half(PAIRS)
    x, y, z, core = place()
    u = jnp.where(core == 0, x, y)
    v = jnp.where(core == 0, y, x)
    line = u
    half = pl.ds(pl.multiple_of(core * (K // 2), K // 2), K // 2)
    other_half = pl.ds(pl.multiple_of((1 - core) * (K // 2), K // 2), K // 2)
    sibling = device(x, y, z, 1 - core)
    back = step - STEPS
    slot = lax.rem(step + SLOTS - STEPS % SLOTS, SLOTS)

    def at(du, dv, dz):
        moved_u, moved_v = turn(u, du), turn(v, dv)
        return device(
            jnp.where(core == 0, moved_u, moved_v),
            jnp.where(core == 0, moved_v, moved_u),
            turn(z, dz),
            core,
        )

    def block(du, dv):
        moved_u, moved_v = turn(u, du), turn(v, dv)
        return jnp.where(core == 0, moved_u * 4 + moved_v, moved_v * 4 + moved_u)

    def along_u(d):
        return remote(
            own_ref.at[half], weight_ref.at[block(0, 0), half], u_send.at[d - 1], u_recv.at[d - 1], at(d, 0, 0)
        )

    def from_u(d):
        there = weight_ref.at[block(-d, 0), half]
        return remote(there, there, u_send.at[d - 1], u_recv.at[d - 1], at(d, 0, 0))

    def along_v(d, du):
        there = weight_ref.at[block(du, 0), half]
        source = own_ref.at[half] if du == 0 else there
        return remote(source, there, v_send.at[d - 1, du], v_recv.at[d - 1, du], at(0, d, 0))

    def from_v(d, du):
        there = weight_ref.at[block(du, -d), half]
        return remote(there, there, v_send.at[d - 1, du], v_recv.at[d - 1, du], at(0, d, 0))

    def to_sibling(du, dv):
        there = weight_ref.at[block(du, dv), half]
        return remote(there, there, s_send.at[du, dv % 4], s_recv.at[du, dv % 4], sibling)

    def from_sibling(du, dv):
        first = jnp.where(core == 0, turn(x, dv), turn(x, du))
        second = jnp.where(core == 0, turn(y, du), turn(y, dv))
        there = weight_ref.at[first * 4 + second, other_half]
        return remote(there, there, s_send.at[du, dv % 4], s_recv.at[du, dv % 4], sibling)

    def segment_parts(dv, dz):
        to_v, to_z = turn(v, dv), turn(z, dz)
        for along in range(4):
            chip = jnp.where(core == 0, along * 4 + to_v, to_v * 4 + along) * 4 + to_z
            source = cut_ref.at[:, pl.ds(pl.multiple_of(chip * 256, 256), 256)]
            yield along, source, seg_ref.at[v * 4 + z, :, pl.ds(along * 256, 256)]

    def segments_to(dv, dz):
        return [
            remote(source, there, g_send.at[dv, dz, n], g_recv.at[dv, dz, n], at(0, dv, dz))
            for n, source, there in segment_parts(dv, dz)
        ]

    def segments_from(dv, dz):
        found = []
        for n in range(4):
            there = seg_ref.at[turn(v, -dv) * 4 + turn(z, -dz), :, pl.ds(n * 256, 256)]
            found.append(remote(there, there, g_send.at[dv, dz, n], g_recv.at[dv, dz, n], at(0, dv, dz)))
        return found

    def segments_own():
        return [
            pltpu.make_async_copy(source, there, g_send.at[0, 0, n])
            for n, source, there in segment_parts(0, 0)
        ]

    def weight_copy():
        return remote(give, other, pair_sem.at[0], pair_sem.at[1], sibling)

    def weight_z(d):
        there = turn(z, d)
        to = device(x, y, there, core)
        return remote(give.at[pl.ds(there * 16, 16)], w2_in.at[d - 1], z_send.at[d - 1], z_recv.at[d - 1], to)

    def copies(block, where):
        at_x = pl.ds((x * 2 + core) * 128 + block * ROWS, ROWS)
        at_y = pl.ds((y * 2 + core) * 128 + block * ROWS, ROWS)
        found = []
        for d in (2, 1, 3):
            tx = lax.rem(x + d, 4)
            ty = lax.rem(y + d, 4)
            for kind, group, rows, target in (
                (0, tx, at_x, device(tx, y, z, 0)),
                (1, 4 + ty, at_y, device(x, ty, z, 1)),
            ):
                found.append(
                    pltpu.make_async_remote_copy(
                        src_ref=stage.at[where, pl.ds(group * 16, 16)],
                        dst_ref=rows_ref.at[:, rows],
                        send_sem=send_sem.at[where, kind * 3 + d - 1],
                        recv_sem=recv_sem.at[block, d * 2 + core],
                        device_id=target,
                        device_id_type=MESH,
                    )
                )
        group = jnp.where(core == 0, 4 + y, x)
        there = pl.ds((jnp.where(core == 0, y, x) * 2 + core) * 128 + block * ROWS, ROWS)
        found.append(
            pltpu.make_async_remote_copy(
                src_ref=stage.at[where, pl.ds(group * 16, 16)],
                dst_ref=rows_ref.at[:, there],
                send_sem=send_sem.at[where, 6],
                recv_sem=recv_sem.at[block, 0],
                device_id=sibling,
                device_id_type=MESH,
            )
        )
        return found

    def own_copy(block, where):
        group = jnp.where(core == 0, x, 4 + y)
        here = pl.ds((line * 2 + core) * 128 + block * ROWS, ROWS)
        return pltpu.make_async_copy(
            stage.at[where, pl.ds(group * 16, 16)], rows_ref.at[:, here], own_sem.at[where]
        )

    plane = [(dv, dz) for dv in range(4) for dz in range(4) if dv or dz]
    blocks = [(du, dv) for du in range(4) for dv in range(4) if du or dv]
    weight_copy_own = pltpu.make_async_copy(own_ref, weight_ref.at[block(0, 0)], first_sem.at[0])

    def pass_on(arrived):
        for du in arrived:
            for d in range(1, 4):
                from_v(d, du).wait_recv()
                to_sibling(du, 4 - d).start()

    @pl.when(step == 0)
    def _():
        pg_ref[...] = jnp.zeros_like(pg_ref)
        projt_ref[...] = jnp.dot(
            natural_ref[...], reorder(BF), preferred_element_type=F32
        ).astype(BF)
        senders = [at(d, 0, 0) for d in range(1, 4)] + [at(0, dv, dz) for dv, dz in plane] + [sibling]
        for d in range(1, 4):
            moved = turn(u, d)
            senders.append(
                device(jnp.where(core == 0, moved, x), jnp.where(core == 0, y, moved), z, 1 - core)
            )
        greet(senders)
        for d in range(1, 4):
            along_u(d).start()
        for d in range(1, 4):
            along_v(d, 0).start()
        weight_copy_own.start()

    @pl.when(step == 1)
    def _():
        for d in (1, 3, 2):
            from_u(d).wait_recv()
            for dv in range(1, 4):
                along_v(dv, 4 - d).start()
            to_sibling(4 - d, 0).start()

    @pl.when(step == 2)
    def _():
        for copy in segments_own():
            copy.start()
        for dv, dz in plane:
            for copy in segments_to(dv, dz):
                copy.start()

    @pl.when(step == 3)
    def _():
        pass_on((0,))

    @pl.when(step == 6)
    def _():
        pass_on((1, 3))

    def spread(turns, carry):
        for inner in range(8):
            tile = turns * 8 + inner
            wide[pl.ds(pl.multiple_of(tile * ROWS, ROWS), ROWS), :] = x_ref[
                :, pl.ds(pl.multiple_of(tile * 128, 128), 128)
            ].astype(F32)
        return carry

    lax.fori_loop(0, F * E // 1024, spread, 0)

    def matrix(b):
        a0 = wide[pl.ds(b, PAIRS, stride=3 * ROWS), :]
        a1 = wide[pl.ds(b + ROWS, PAIRS, stride=3 * ROWS), :]
        a2 = wide[pl.ds(b + 2 * ROWS, PAIRS, stride=3 * ROWS), :]
        r1 = pltpu.roll(a1, 64, 1)
        r2 = pltpu.roll(a2, 64, 1)
        even = jnp.concatenate([a0, jnp.where(low, a1, 0.0)], axis=1)
        odd = jnp.concatenate([jnp.where(low, r1, r2), jnp.where(low, r2, 0.0)], axis=1)
        return interleave(even, odd).astype(BF)

    @pl.when(step < STEPS)
    def _():
        def samples(turns, carry):
            group = [turns * 4 + inner for inner in range(4)]
            xs = [matrix(b) for b in group]
            mixed = [
                jnp.dot(projt_ref[...], xb, preferred_element_type=F32).astype(BF) for xb in xs
            ]
            grams = [
                lax.dot_general(m, xb, NT, preferred_element_type=F32) * SCALE
                for m, xb in zip(mixed, xs)
            ]
            for b, m, gram_b in zip(group, mixed, grams):
                mixed_all[step * ROWS + b] = m
                turned[pl.ds(b, K, stride=PAD), :] = gram_b[:, :128]
                turned[pl.ds(K * PAD + b, K, stride=PAD), :] = gram_b[:, 128:]
            return carry

        lax.fori_loop(0, ROWS // 4, samples, 0)
        rows = pl.ds(pl.multiple_of(step * ROWS, ROWS), ROWS)

        def pack_gram(turns, carry):
            for inner in range(8):
                k = turns * 8 + inner
                for part in range(2):
                    at = pl.ds((part * K + k) * PAD, ROWS)
                    gram[k, rows, part * 128 : part * 128 + 128] = turned[at, :].astype(BF)
            return carry

        lax.fori_loop(0, K // 8, pack_gram, 0)

    @pl.when(step == STEPS - 1)
    def _():
        pass_on((2,))

    def gram_grads():
        def gram_grad(turns, carry):
            for inner in range(4):
                k = turns * 4 + inner
                gg = lax.dot_general(
                    slope_ref[...], weight_ref[:, k].reshape(F, H), NT, preferred_element_type=F32
                )
                turned[pl.ds(k, batch, stride=K + 1), :] = gg[:, :128]
                turned[pl.ds(batch * (K + 1) + k, batch, stride=K + 1), :] = gg[:, 128:]
            return carry

        lax.fori_loop(0, K // 4, gram_grad, 0)

        def pack_gg(turns, carry):
            for inner in range(4):
                b = turns * 4 + inner
                for part in range(2):
                    gg_all[b, :, part * 128 : part * 128 + 128] = turned[
                        pl.ds((part * batch + b) * (K + 1), K), :
                    ].astype(BF)
            return carry

        lax.fori_loop(0, batch // 4, pack_gg, 0)

    def weight_grads(first):
        def one(turns, carry):
            for inner in range(4):
                k = first + turns * 4 + inner
                wgrad = lax.dot_general(gram[k], slope_ref[...], TN, preferred_element_type=F32)
                for block in range(16):
                    for parity in range(2):
                        at = block * 16 + parity * 8
                        turned[
                            pl.ds(block * 8 * (2 * K + 1) + parity * K + k, 8, stride=2 * K + 1), :
                        ] = wgrad[at : at + 8]
            return carry

        lax.fori_loop(0, K // 8, one, 0)

    @pl.when(step == STEPS)
    def _():
        weight_copy_own.wait()
        for du, dv in blocks:
            from_sibling(du, dv).wait_recv()

        def product(turns, total):
            for inner in range(8):
                k = turns * 8 + inner
                total = total + jnp.dot(
                    gram[k], weight_ref[:, k].reshape(F, H), preferred_element_type=F32
                )
            return total

        preact = lax.fori_loop(0, K // 8, product, jnp.zeros((batch, H), F32))
        sig = jax.nn.sigmoid(preact)
        slope_ref[...] = (
            cot_ref[...].astype(F32) * sig * (1.0 + preact * (1.0 - sig))
        ).astype(BF)
        gram_grads()

    @pl.when(step >= STEPS)
    def _():
        def samples(turns, total):
            group = [turns * 4 + inner for inner in range(4)]
            xs = [matrix(b) for b in group]
            ggs = [gg_all[back * ROWS + b] for b in group]
            mgs = [
                jnp.dot(gg, xb, preferred_element_type=F32).astype(BF) for gg, xb in zip(ggs, xs)
            ]
            for mg, xb in zip(mgs, xs):
                total = total + lax.dot_general(mg, xb, NT, preferred_element_type=F32)
            for b, gg, mg in zip(group, ggs, mgs):
                left = jnp.concatenate([gg, projt_ref[...]], axis=0)
                right = jnp.concatenate([mixed_all[back * ROWS + b], mg], axis=0)
                fg = lax.dot_general(left, right, TN, preferred_element_type=F32) * SCALE
                fg = fg.reshape(16, 2, 8, 256)
                even = fg[:, 0].reshape(PAIRS, 256)
                odd = fg[:, 1].reshape(PAIRS, 256)
                r0 = pltpu.roll(odd[:, :128], 64, 1)
                r1 = pltpu.roll(odd[:, 128:], 64, 1)
                ready[pl.ds(b, PAIRS, stride=3 * PAD), :] = even[:, :128]
                ready[pl.ds(b + PAD, PAIRS, stride=3 * PAD), :] = jnp.where(low, even[:, 128:], r0)
                ready[pl.ds(b + 2 * PAD, PAIRS, stride=3 * PAD), :] = jnp.where(low, r0, r1)
            return total

        pg_ref[...] += lax.fori_loop(0, ROWS // 4, samples, jnp.zeros((K, F), F32)) * SCALE

        @pl.when(back >= SLOTS)
        def _():
            for copy in copies(back - SLOTS, slot):
                copy.wait_send()
            own_copy(back - SLOTS, slot).wait()

        def pack(q, carry):
            for kind in range(2):
                for last in range(4):
                    first, second = q // 4, q % 4
                    if kind == 0:
                        owner = ((first * 4 + second) * 4 + last) * 2
                    else:
                        owner = ((second * 4 + first) * 4 + last) * 2 + 1
                    for tile in range(3):
                        at = pl.ds((owner * 3 + tile) * PAD, ROWS)
                        stage[slot, kind * 64 + q * 4 + last, :, tile * 128 : tile * 128 + 128] = ready[
                            at, :
                        ].astype(BF)
            return carry

        lax.fori_loop(0, 16, pack, 0)
        for copy in copies(back, slot):
            copy.start()
        own_copy(back, slot).start()

    @pl.when(back == 0)
    def _():
        weight_grads(0)

    @pl.when(back == 1)
    def _():
        weight_grads(K // 2)

        def pack_wgrad(chip, carry):
            give[chip] = turned[
                pl.ds((chip * 2 + 1 - core) * (2 * K + 1), 2 * K), :
            ].astype(BF)
            return carry

        lax.fori_loop(0, 64, pack_wgrad, 0)
        weight_copy().start()

    @pl.when(back == 2)
    def _():
        weight_copy().wait_send()
        weight_copy().wait_recv()

        def pair_sum(n, carry):
            to_z, first, second = n // 16, (n // 4) % 4, n % 4
            chip = jnp.where(core == 0, first * 4 + second, second * 4 + first) * 4 + to_z
            mine = turned[pl.ds((chip * 2 + core) * (2 * K + 1), 2 * K), :]
            give[n] = (mine + other[chip].astype(F32)).astype(BF)
            return carry

        lax.fori_loop(0, 64, pair_sum, 0)
        for d in range(1, 4):
            weight_z(d).start()

    @pl.when(back == STEPS - 1)
    def _():
        for du, dv in blocks:
            to_sibling(du, dv).wait_send()
        for dv, dz in plane:
            for copy in segments_from(dv, dz):
                copy.wait_recv()
            for copy in segments_to(dv, dz):
                copy.wait_send()
        for d in range(1, 4):
            along_u(d).wait_send()
            for du in range(4):
                along_v(d, du).wait_send()
        for copy in segments_own():
            copy.wait()
        for ago in range(SLOTS):
            sent, where = back - ago, lax.rem(slot + SLOTS - ago, SLOTS)
            for copy in copies(sent, where):
                copy.wait_send()
            own_copy(sent, where).wait()
        for d in range(1, 4):
            weight_z(d).wait_recv()

        def sum_z(n, carry):
            total = give[z * 16 + n].astype(F32) + w2_in[0, n].astype(F32)
            total = total + (w2_in[1, n].astype(F32) + w2_in[2, n].astype(F32))
            wz_ref[n] = total.astype(BF)
            return carry

        lax.fori_loop(0, 16, sum_z, 0)
        for d in range(1, 4):
            weight_z(d).wait_send()

        def arrived(block, carry):
            def wait(sender, sem):
                at = pl.ds(sender * 128 + block * ROWS, ROWS)
                pltpu.make_async_remote_copy(
                    src_ref=stage.at[0, pl.ds(0, 16)],
                    dst_ref=rows_ref.at[:, at],
                    send_sem=send_sem.at[0, 0],
                    recv_sem=recv_sem.at[block, sem],
                    device_id=sibling,
                    device_id_type=MESH,
                ).wait_recv()

            wait(line * 2 + 1 - core, 0)
            for d in range(1, 4):
                for other in range(2):
                    wait(lax.rem(line + 4 - d, 4) * 2 + other, d * 2 + other)
            return carry

        lax.fori_loop(0, STEPS, arrived, 0)


def main(x, projt, own, cut, cot):
    batch = x.shape[0]
    any_space = pl.BlockSpec(memory_space=pl.ANY)
    dma = pltpu.SemaphoreType.DMA
    return pl.pallas_call(
        main_kernel,
        grid=(2 * STEPS,),
        in_specs=[
            pl.BlockSpec((ROWS, F * E), lambda i: (lax.rem(i, STEPS), 0)),
            pl.BlockSpec((K, F), lambda i: (0, 0)),
            any_space,
            any_space,
            pl.BlockSpec((batch, H), lambda i: (0, 0)),
        ],
        out_specs=[
            pl.BlockSpec((K, F), lambda i: (0, 0)),
            any_space,
            pl.BlockSpec((16, 2 * K, H), lambda i: (0, 0, 0)),
            any_space,
        ],
        out_shape=[
            jax.ShapeDtypeStruct((K, F), F32),
            jax.ShapeDtypeStruct((16, 8 * batch, 2 * E), BF),
            jax.ShapeDtypeStruct((16, 2 * K, H), BF),
            jax.ShapeDtypeStruct((16, 2, 8 * batch), jnp.int32),
        ],
        scratch_shapes=[
            pltpu.VMEM((K, F), BF),
            pltpu.VMEM((F * E // 128 * ROWS, 128), F32),
            pltpu.VMEM((3 * PAIRS * PAD, 128), F32),
            pltpu.VMEM((batch, K, 256), BF),
            pltpu.VMEM((K, batch, F), BF),
            pltpu.VMEM((16,) + own.shape, BF),
            pltpu.VMEM((batch, H), BF),
            pltpu.VMEM((batch, K, F), BF),
            pltpu.VMEM((2 * batch * (K + 1), H), F32),
            pltpu.VMEM((SLOTS, PAIRS, ROWS, 2 * E), BF),
            pltpu.VMEM((64, 2 * K, H), BF),
            pltpu.VMEM((64, 2 * K, H), BF),
            pltpu.VMEM((3, 16, 2 * K, H), BF),
            dma((3,)),
            dma((3,)),
            dma((3, 4)),
            dma((3, 4)),
            dma((4, 4)),
            dma((4, 4)),
            dma((4, 4, 4)),
            dma((4, 4, 4)),
            dma((1,)),
            dma((SLOTS, 7)),
            dma((STEPS, 8)),
            dma((SLOTS,)),
            dma((2,)),
            dma((3,)),
            dma((3,)),
        ],
        compiler_params=pltpu.CompilerParams(
            vmem_limit_bytes=VMEM_LIMIT, collective_id=1, has_side_effects=True
        ),
        cost_estimate=pl.CostEstimate(
            flops=18 * batch * F * E * K, bytes_accessed=60_000_000, transcendentals=batch * H
        ),
        name="main",
    )(x, projt, own, cut, cot)


SLOT_BLOCK = 256
HALF = UNIQUE_CAP // 2
FIRST = 128
ORDER = (1, 2, 3, 0)


def sums_kernel(
    rows_ref, seg_ref, wz_ref, pg_ref,
    wout_ref, pout_ref, out_ref,
    data, table, az, bv, sum_a, sum_b, va, zb, w3_in, w4, w4_in, pu, pv, pz, pc,
    load_sem, az_send, az_recv, bv_send, bv_recv, va_send, va_recv, zb_send, zb_recv,
    w_send, w_recv, p_send, p_recv,
):
    x, y, z, core = place()
    u = jnp.where(core == 0, x, y)
    v = jnp.where(core == 0, y, x)
    low = lower_half(SLOT_BLOCK)

    def at_u(d):
        moved = turn(u, d)
        return device(jnp.where(core == 0, moved, x), jnp.where(core == 0, y, moved), z, core)

    def at_v(d):
        moved = turn(v, d)
        return device(jnp.where(core == 0, x, moved), jnp.where(core == 0, moved, y), z, core)

    def at_z(d):
        return device(x, y, turn(z, d), core)

    sibling = device(x, y, z, 1 - core)

    def load(dz, dv):
        j = turn(v, dv) * 4 + turn(z, dz)
        return pltpu.make_async_copy(rows_ref.at[j], data.at[dz, dv], load_sem.at[dz, dv])

    for dz in ORDER:
        for dv in ORDER:
            load(dz, dv).start()

    greet([to(d) for d in range(1, 4) for to in (at_u, at_v, at_z)] + [sibling])

    def spread(buffer, mine, stage, to):
        return [
            remote(buffer.at[mine], buffer.at[mine], p_send.at[stage, d - 1], p_recv.at[stage, d - 1], to(d))
            for d in range(1, 4)
        ]

    def gathered(buffer, mine, stage, to):
        for d in range(1, 4):
            there = buffer.at[turn(mine, -d)]
            remote(there, there, p_send.at[stage, d - 1], p_recv.at[stage, d - 1], to(d)).wait_recv()
        return (buffer[0] + buffer[1]) + (buffer[2] + buffer[3])

    def start(copies):
        for copy in copies:
            copy.start()
        return copies

    def send_a(dz, dv):
        return remote(
            table.at[dz, dv, pl.ds(0, FIRST)],
            az.at[dz - 1, dv],
            az_send.at[dz - 1, dv],
            az_recv.at[dz - 1, dv],
            at_z(dz),
        )

    def send_b(dv, dz):
        return remote(
            table.at[dz, dv, pl.ds(FIRST, HALF - FIRST)],
            bv.at[dv - 1, dz],
            bv_send.at[dv - 1, dz],
            bv_recv.at[dv - 1, dz],
            at_v(dv),
        )

    def second_a(dv):
        return remote(sum_a.at[dv], va.at[dv - 1], va_send.at[dv - 1], va_recv.at[dv - 1], at_v(dv))

    def second_b(dz):
        return remote(sum_b.at[dz], zb.at[dz - 1], zb_send.at[dz - 1], zb_recv.at[dz - 1], at_z(dz))

    def one_table(dz, dv):
        load(dz, dv).wait()
        j = turn(v, dv) * 4 + turn(z, dz)
        slot = lax.broadcasted_iota(jnp.int32, (SLOT_BLOCK, 8 * 128), 0)

        def part(block, parity):
            seg = seg_ref[j, parity : parity + 1, :] - block * SLOT_BLOCK
            hot = jnp.where(slot == seg, 1.0, 0.0).astype(BF)
            found = jnp.dot(
                hot, data[dz, dv, :, parity * 128 : parity * 128 + 256], preferred_element_type=F32
            )
            return found[:, :128], found[:, 128:]

        for block in range(HALF // SLOT_BLOCK):
            at = pl.ds(block * SLOT_BLOCK, SLOT_BLOCK)
            even0, even1 = part(block, 0)
            odd0, odd1 = part(block, 1)
            r0 = pltpu.roll(odd0, 64, 1)
            r1 = pltpu.roll(odd1, 64, 1)
            table[dz, dv, at, 0:128] = (even0 + jnp.where(low, r0, r1)).astype(BF)
            first = even1 + r1
            even0, even1 = part(block + HALF // SLOT_BLOCK, 0)
            odd0, odd1 = part(block + HALF // SLOT_BLOCK, 1)
            r0 = pltpu.roll(even0, 64, 1)
            r1 = pltpu.roll(even1, 64, 1)
            table[dz, dv, at, 128:256] = jnp.where(low, first, r0 + odd0).astype(BF)
            table[dz, dv, at, 256:384] = (jnp.where(low, r0, r1) + odd1).astype(BF)

    def tables(dz):
        def one(turns, carry):
            dv = lax.rem(turns + 1, 4)
            one_table(dz, dv)
            if dz > 0:
                send_a(dz, dv).start()

            @pl.when(dv > 0)
            def _():
                send_b(dv, dz).start()

            return carry

        lax.fori_loop(0, 4, one, 0)

    def add_four(first, second, third, fourth, target, size):
        rows = first.shape[0]

        def one(n, carry):
            at = pl.ds(pl.multiple_of(n * size, size), size)
            total = (first[at].astype(F32) + second[at].astype(F32)) + (
                third[at].astype(F32) + fourth[at].astype(F32)
            )
            target[at] = total.astype(target.dtype)
            return carry

        lax.fori_loop(0, rows // size, one, 0)

    def total_b(dz):
        for dv in range(1, 4):
            send_b(dv, dz).wait_recv()
        mine = table.at[dz, 0, pl.ds(FIRST, HALF - FIRST)]
        add_four(mine, bv.at[0, dz], bv.at[1, dz], bv.at[2, dz], sum_b.at[dz], 64)
        if dz > 0:
            second_b(dz).start()

    def total_a(dv):
        for dz in range(1, 4):
            send_a(dz, dv).wait_recv()
        mine = table.at[0, dv, pl.ds(0, FIRST)]
        add_four(mine, az.at[0, dv], az.at[1, dv], az.at[2, dv], sum_a.at[dv], 64)
        if dv > 0:
            second_a(dv).start()

    def w_copies(source, arrive, stage, to, line, size):
        return [
            remote(
                source.at[pl.ds(turn(line, d) * size, size)],
                arrive.at[d - 1],
                w_send.at[stage, d - 1],
                w_recv.at[stage, d - 1],
                to(d),
            )
            for d in range(1, 4)
        ]

    pu[u] = pg_ref[...]
    p0 = start(spread(pu, u, 0, at_u))
    s3 = start(w_copies(wz_ref, w3_in, 0, at_u, u, 4))
    tables(1)
    tables(2)
    pv[v] = gathered(pu, u, 0, at_u)
    p1 = start(spread(pv, v, 1, at_v))
    for copy in s3:
        copy.wait_recv()
    add_four(wz_ref.at[pl.ds(u * 4, 4)], w3_in.at[0], w3_in.at[1], w3_in.at[2], w4, 1)
    s4 = start(w_copies(w4, w4_in, 1, at_v, v, 1))
    total_b(1)
    tables(3)
    pz[z] = gathered(pv, v, 1, at_v)
    p2 = start(spread(pz, z, 2, at_z))
    total_b(2)
    tables(0)
    total_b(3)
    pc[core] = gathered(pz, z, 2, at_z)
    p3 = remote(pc.at[core], pc.at[core], p_send.at[3, 0], p_recv.at[3, 0], sibling)
    p3.start()
    for copy in s4:
        copy.wait_recv()
    total = w4[v].astype(F32) + w4_in[0, 0].astype(F32)
    wout_ref[...] = total + (w4_in[1, 0].astype(F32) + w4_in[2, 0].astype(F32))
    for dv in ORDER:
        total_a(dv)
    total_b(0)
    remote(pc.at[1 - core], pc.at[1 - core], p_send.at[3, 0], p_recv.at[3, 0], sibling).wait_recv()
    pout_ref[...] = lax.dot_general(
        pc[0] + pc[1],
        reorder(F32),
        NT,
        precision=lax.Precision.HIGHEST,
        preferred_element_type=F32,
    )

    def finish(mine, others, start_row, rows):
        def one(part, carry):
            at = pl.ds(pl.multiple_of(part * 128, 128), 128)
            before = pl.ds(pl.multiple_of(part * 128 + start_row, 128), 128)
            after = pl.ds(pl.multiple_of(part * 128 + start_row + HALF, 128), 128)
            total = mine[at, :].astype(F32) + others[0, at].astype(F32)
            total = total + (others[1, at].astype(F32) + others[2, at].astype(F32))
            r1 = pltpu.roll(total[:, 128:256], 64, 1)
            r2 = pltpu.roll(total[:, 256:], 64, 1)
            out_ref[:128, before] = total[:, :128].T
            out_ref[128:, before] = total[:, 128:256].T[:64]
            out_ref[:128, after] = jnp.where(lower_half(128), r1, r2).T
            out_ref[128:, after] = r2.T[:64]
            return carry

        lax.fori_loop(0, rows // 128, one, 0)

    for d in range(1, 4):
        second_a(d).wait_recv()
    finish(sum_a.at[0], va, 0, FIRST)
    for d in range(1, 4):
        second_b(d).wait_recv()
    finish(sum_b.at[0], zb, FIRST, HALF - FIRST)

    for copy in p0 + p1 + p2 + [p3] + s3 + s4:
        copy.wait_send()
    for d in range(1, 4):
        second_a(d).wait_send()
        second_b(d).wait_send()
        for n in range(4):
            send_a(d, n).wait_send()
            send_b(d, n).wait_send()


def sums(rows, seg, wz, pg):
    any_space = pl.BlockSpec(memory_space=pl.ANY)
    whole = pl.BlockSpec(memory_space=pltpu.VMEM)
    dma = pltpu.SemaphoreType.DMA
    rest = HALF - FIRST
    return pl.pallas_call(
        sums_kernel,
        in_specs=[any_space, whole, whole, whole],
        out_specs=[whole] * 3,
        out_shape=[
            jax.ShapeDtypeStruct((2 * K, H), F32),
            jax.ShapeDtypeStruct((K, F), F32),
            jax.ShapeDtypeStruct((E, UNIQUE_CAP), F32),
        ],
        scratch_shapes=[
            pltpu.VMEM((4, 4) + rows.shape[1:], BF),
            pltpu.VMEM((4, 4, HALF, 2 * E), BF),
            pltpu.VMEM((3, 4, FIRST, 2 * E), BF),
            pltpu.VMEM((3, 4, rest, 2 * E), BF),
            pltpu.VMEM((4, FIRST, 2 * E), BF),
            pltpu.VMEM((4, rest, 2 * E), BF),
            pltpu.VMEM((3, FIRST, 2 * E), BF),
            pltpu.VMEM((3, rest, 2 * E), BF),
            pltpu.VMEM((3, 4, 2 * K, H), BF),
            pltpu.VMEM((4, 2 * K, H), BF),
            pltpu.VMEM((3, 1, 2 * K, H), BF),
            pltpu.VMEM((4, K, F), F32),
            pltpu.VMEM((4, K, F), F32),
            pltpu.VMEM((4, K, F), F32),
            pltpu.VMEM((2, K, F), F32),
            dma((4, 4)),
            dma((3, 4)),
            dma((3, 4)),
            dma((3, 4)),
            dma((3, 4)),
            dma((3,)),
            dma((3,)),
            dma((3,)),
            dma((3,)),
            dma((2, 3)),
            dma((2, 3)),
            dma((4, 3)),
            dma((4, 3)),
        ],
        compiler_params=pltpu.CompilerParams(
            vmem_limit_bytes=VMEM_LIMIT, collective_id=2, has_side_effects=True
        ),
        cost_estimate=pl.CostEstimate(
            flops=16 * 4 * UNIQUE_CAP * 1024 * 256, bytes_accessed=30_000_000, transcendentals=0
        ),
        name="sums",
    )(rows, seg, wz, pg)


def finish_kernel(w_ref, p_ref, r_ref, wout_ref, pout_ref, rout_ref):
    wout_ref[...] = w_ref[...]
    pout_ref[...] = p_ref[...]
    rout_ref[...] = r_ref[...]


def finish(*results):
    whole = pl.BlockSpec(memory_space=pltpu.VMEM)
    return pl.pallas_call(
        finish_kernel,
        in_specs=[whole] * 3,
        out_specs=[whole] * 3,
        out_shape=[jax.ShapeDtypeStruct(a.shape, a.dtype) for a in results],
        name="finish",
    )(*results)


def turn_features(a):
    rest = a.shape[1:]
    return a.reshape((-1, 8, 2) + rest).swapaxes(1, 2).reshape(a.shape)


def on_device(pooled, projection, out_weight, cotangent, segments):
    own = turn_features(out_weight.reshape(-1, K, H)).swapaxes(0, 1)
    pg, rows, wz, seg = main(pooled, projection.T, own, segments.T, cotangent)
    weight_grad, pg, row_grad = finish(*sums(rows, seg, wz, pg))
    return (weight_grad, pg.T, row_grad.T)


def solution(mesh):
    placed = (
        P(("fsdp", "emb"), None),
        P(),
        P("fsdp", None),
        P(("fsdp", "emb"), None),
        P(None, ("fsdp", "emb")),
    )
    return jax.shard_map(
        on_device,
        mesh=mesh,
        in_specs=placed,
        out_specs=(P(("fsdp", "emb"), None), P(), P(("fsdp", "emb"), None)),
        check_vma=False,
    )
```

```python
import functools

import jax
import jax.numpy as jnp
from jax import lax
from jax.experimental import pallas as pl
from jax.experimental.pallas import tpu as pltpu
from jax.sharding import PartitionSpec as P

F = 256
E = 192
K = 96
H = 128
UNIQUE_CAP = 1024
PAIRS = F // 2
ROWS = 16
SCALE = E ** (-0.5)
BF = jnp.bfloat16
F32 = jnp.float32
VMEM_LIMIT = 60 * 1024 * 1024
NT = (((1,), (1,)), ((), ()))
TN = (((0,), (0,)), ((), ()))


def interleave(even, odd):
    width = even.shape[-1]
    both = jnp.concatenate([even.reshape(16, 8, width), odd.reshape(16, 8, width)], axis=1)
    return both.reshape(F, width)


def reorder(dtype):
    column = lax.broadcasted_iota(jnp.int32, (F, F), 1)
    within = column & 15
    natural = (column - within) + (within & 7) * 2 + (within >> 3)
    return jnp.where(lax.broadcasted_iota(jnp.int32, (F, F), 0) == natural, 1.0, 0.0).astype(dtype)


def lower_half(rows):
    return lax.broadcasted_iota(jnp.int32, (rows, 128), 1) < 64


MESH = pl.DeviceIdType.MESH


def place():
    fsdp = lax.axis_index("fsdp")
    emb = lax.axis_index("emb")
    return fsdp // 4, fsdp % 4, emb // 2, emb % 2


def device(x, y, z, core):
    return (x * 4 + y, z * 2 + core)


def turn(at, d):
    return lax.rem(at + 4 + d, 4)


def greet(devices):
    barrier = pltpu.get_barrier_semaphore()
    for to in devices:
        pl.semaphore_signal(barrier, inc=1, device_id=to, device_id_type=MESH)
    pl.semaphore_wait(barrier, len(devices))


def remote(source, target, send, recv, to):
    return pltpu.make_async_remote_copy(
        src_ref=source,
        dst_ref=target,
        send_sem=send,
        recv_sem=recv,
        device_id=to,
        device_id_type=MESH,
    )


SLOTS = 3
PAD = ROWS + 1
STEPS = 8


def main_kernel(
    x_ref, natural_ref, own_ref, cut_ref, cot_ref,
    pg_ref, rows_ref, wz_ref, seg_ref,
    projt_ref, wide, ready, mixed_all, gram, weight_ref, slope_ref, gg_all, turned, stage, give, other, w2_in,
    u_send, u_recv, v_send, v_recv, s_send, s_recv, g_send, g_recv, first_sem,
    send_sem, recv_sem, own_sem, pair_sem, z_send, z_recv,
):
    step = pl.program_id(0)
    batch = gram.shape[1]
    low = lower_half(PAIRS)
    x, y, z, core = place()
    u = jnp.where(core == 0, x, y)
    v = jnp.where(core == 0, y, x)
    line = u
    half = pl.ds(pl.multiple_of(core * (K // 2), K // 2), K // 2)
    other_half = pl.ds(pl.multiple_of((1 - core) * (K // 2), K // 2), K // 2)
    sibling = device(x, y, z, 1 - core)
    back = step - STEPS
    slot = lax.rem(step + SLOTS - STEPS % SLOTS, SLOTS)

    def at(du, dv, dz):
        moved_u, moved_v = turn(u, du), turn(v, dv)
        return device(
            jnp.where(core == 0, moved_u, moved_v),
            jnp.where(core == 0, moved_v, moved_u),
            turn(z, dz),
            core,
        )

    def block(du, dv):
        moved_u, moved_v = turn(u, du), turn(v, dv)
        return jnp.where(core == 0, moved_u * 4 + moved_v, moved_v * 4 + moved_u)

    def along_u(d):
        return remote(
            own_ref.at[half], weight_ref.at[block(0, 0), half], u_send.at[d - 1], u_recv.at[d - 1], at(d, 0, 0)
        )

    def from_u(d):
        there = weight_ref.at[block(-d, 0), half]
        return remote(there, there, u_send.at[d - 1], u_recv.at[d - 1], at(d, 0, 0))

    def along_v(d, du):
        there = weight_ref.at[block(du, 0), half]
        source = own_ref.at[half] if du == 0 else there
        return remote(source, there, v_send.at[d - 1, du], v_recv.at[d - 1, du], at(0, d, 0))

    def from_v(d, du):
        there = weight_ref.at[block(du, -d), half]
        return remote(there, there, v_send.at[d - 1, du], v_recv.at[d - 1, du], at(0, d, 0))

    def to_sibling(du, dv):
        there = weight_ref.at[block(du, dv), half]
        return remote(there, there, s_send.at[du, dv % 4], s_recv.at[du, dv % 4], sibling)

    def from_sibling(du, dv):
        first = jnp.where(core == 0, turn(x, dv), turn(x, du))
        second = jnp.where(core == 0, turn(y, du), turn(y, dv))
        there = weight_ref.at[first * 4 + second, other_half]
        return remote(there, there, s_send.at[du, dv % 4], s_recv.at[du, dv % 4], sibling)

    def segment_parts(dv, dz):
        to_v, to_z = turn(v, dv), turn(z, dz)
        for along in range(4):
            chip = jnp.where(core == 0, along * 4 + to_v, to_v * 4 + along) * 4 + to_z
            source = cut_ref.at[:, pl.ds(pl.multiple_of(chip * 256, 256), 256)]
            yield along, source, seg_ref.at[v * 4 + z, :, pl.ds(along * 256, 256)]

    def segments_to(dv, dz):
        return [
            remote(source, there, g_send.at[dv, dz, n], g_recv.at[dv, dz, n], at(0, dv, dz))
            for n, source, there in segment_parts(dv, dz)
        ]

    def segments_from(dv, dz):
        found = []
        for n in range(4):
            there = seg_ref.at[turn(v, -dv) * 4 + turn(z, -dz), :, pl.ds(n * 256, 256)]
            found.append(remote(there, there, g_send.at[dv, dz, n], g_recv.at[dv, dz, n], at(0, dv, dz)))
        return found

    def segments_own():
        return [
            pltpu.make_async_copy(source, there, g_send.at[0, 0, n])
            for n, source, there in segment_parts(0, 0)
        ]

    def weight_copy():
        return remote(give, other, pair_sem.at[0], pair_sem.at[1], sibling)

    def weight_z(d):
        there = turn(z, d)
        to = device(x, y, there, core)
        return remote(give.at[pl.ds(there * 16, 16)], w2_in.at[d - 1], z_send.at[d - 1], z_recv.at[d - 1], to)

    def copies(block, where):
        at_x = pl.ds((x * 2 + core) * 128 + block * ROWS, ROWS)
        at_y = pl.ds((y * 2 + core) * 128 + block * ROWS, ROWS)
        found = []
        for d in (2, 1, 3):
            tx = lax.rem(x + d, 4)
            ty = lax.rem(y + d, 4)
            for kind, group, rows, target in (
                (0, tx, at_x, device(tx, y, z, 0)),
                (1, 4 + ty, at_y, device(x, ty, z, 1)),
            ):
                found.append(
                    pltpu.make_async_remote_copy(
                        src_ref=stage.at[where, pl.ds(group * 16, 16)],
                        dst_ref=rows_ref.at[:, rows],
                        send_sem=send_sem.at[where, kind * 3 + d - 1],
                        recv_sem=recv_sem.at[block, d * 2 + core],
                        device_id=target,
                        device_id_type=MESH,
                    )
                )
        group = jnp.where(core == 0, 4 + y, x)
        there = pl.ds((jnp.where(core == 0, y, x) * 2 + core) * 128 + block * ROWS, ROWS)
        found.append(
            pltpu.make_async_remote_copy(
                src_ref=stage.at[where, pl.ds(group * 16, 16)],
                dst_ref=rows_ref.at[:, there],
                send_sem=send_sem.at[where, 6],
                recv_sem=recv_sem.at[block, 0],
                device_id=sibling,
                device_id_type=MESH,
            )
        )
        return found

    def own_copy(block, where):
        group = jnp.where(core == 0, x, 4 + y)
        here = pl.ds((line * 2 + core) * 128 + block * ROWS, ROWS)
        return pltpu.make_async_copy(
            stage.at[where, pl.ds(group * 16, 16)], rows_ref.at[:, here], own_sem.at[where]
        )

    plane = [(dv, dz) for dv in range(4) for dz in range(4) if dv or dz]
    blocks = [(du, dv) for du in range(4) for dv in range(4) if du or dv]
    weight_copy_own = pltpu.make_async_copy(own_ref, weight_ref.at[block(0, 0)], first_sem.at[0])

    def pass_on(arrived):
        for du in arrived:
            for d in range(1, 4):
                from_v(d, du).wait_recv()
                to_sibling(du, 4 - d).start()

    @pl.when(step == 0)
    def _():
        pg_ref[...] = jnp.zeros_like(pg_ref)
        projt_ref[...] = jnp.dot(
            natural_ref[...], reorder(BF), preferred_element_type=F32
        ).astype(BF)
        senders = [at(d, 0, 0) for d in range(1, 4)] + [at(0, dv, dz) for dv, dz in plane] + [sibling]
        for d in range(1, 4):
            moved = turn(u, d)
            senders.append(
                device(jnp.where(core == 0, moved, x), jnp.where(core == 0, y, moved), z, 1 - core)
            )
        greet(senders)
        for d in range(1, 4):
            along_u(d).start()
        for d in range(1, 4):
            along_v(d, 0).start()
        weight_copy_own.start()

    @pl.when(step == 1)
    def _():
        for d in (1, 3, 2):
            from_u(d).wait_recv()
            for dv in range(1, 4):
                along_v(dv, 4 - d).start()
            to_sibling(4 - d, 0).start()

    @pl.when(step == 2)
    def _():
        for copy in segments_own():
            copy.start()
        for dv, dz in plane:
            for copy in segments_to(dv, dz):
                copy.start()

    @pl.when(step == 3)
    def _():
        pass_on((0,))

    @pl.when(step == 6)
    def _():
        pass_on((1, 3))

    def spread(turns, carry):
        for inner in range(8):
            tile = turns * 8 + inner
            wide[pl.ds(pl.multiple_of(tile * ROWS, ROWS), ROWS), :] = x_ref[
                :, pl.ds(pl.multiple_of(tile * 128, 128), 128)
            ].astype(F32)
        return carry

    lax.fori_loop(0, F * E // 1024, spread, 0)

    def matrix(b):
        a0 = wide[pl.ds(b, PAIRS, stride=3 * ROWS), :]
        a1 = wide[pl.ds(b + ROWS, PAIRS, stride=3 * ROWS), :]
        a2 = wide[pl.ds(b + 2 * ROWS, PAIRS, stride=3 * ROWS), :]
        r1 = pltpu.roll(a1, 64, 1)
        r2 = pltpu.roll(a2, 64, 1)
        even = jnp.concatenate([a0, jnp.where(low, a1, 0.0)], axis=1)
        odd = jnp.concatenate([jnp.where(low, r1, r2), jnp.where(low, r2, 0.0)], axis=1)
        return interleave(even, odd).astype(BF)

    @pl.when(step < STEPS)
    def _():
        def samples(turns, carry):
            group = [turns * 4 + inner for inner in range(4)]
            xs = [matrix(b) for b in group]
            mixed = [
                jnp.dot(projt_ref[...], xb, preferred_element_type=F32).astype(BF) for xb in xs
            ]
            grams = [
                lax.dot_general(m, xb, NT, preferred_element_type=F32) * SCALE
                for m, xb in zip(mixed, xs)
            ]
            for b, m, gram_b in zip(group, mixed, grams):
                mixed_all[step * ROWS + b] = m
                turned[pl.ds(b, K, stride=PAD), :] = gram_b[:, :128]
                turned[pl.ds(K * PAD + b, K, stride=PAD), :] = gram_b[:, 128:]
            return carry

        lax.fori_loop(0, ROWS // 4, samples, 0)
        rows = pl.ds(pl.multiple_of(step * ROWS, ROWS), ROWS)

        def pack_gram(turns, carry):
            for inner in range(8):
                k = turns * 8 + inner
                for part in range(2):
                    at = pl.ds((part * K + k) * PAD, ROWS)
                    gram[k, rows, part * 128 : part * 128 + 128] = turned[at, :].astype(BF)
            return carry

        lax.fori_loop(0, K // 8, pack_gram, 0)

    @pl.when(step == STEPS - 1)
    def _():
        pass_on((2,))

    def gram_grads():
        def gram_grad(turns, carry):
            for inner in range(4):
                k = turns * 4 + inner
                gg = lax.dot_general(
                    slope_ref[...], weight_ref[:, k].reshape(F, H), NT, preferred_element_type=F32
                )
                turned[pl.ds(k, batch, stride=K + 1), :] = gg[:, :128]
                turned[pl.ds(batch * (K + 1) + k, batch, stride=K + 1), :] = gg[:, 128:]
            return carry

        lax.fori_loop(0, K // 4, gram_grad, 0)

        def pack_gg(turns, carry):
            for inner in range(4):
                b = turns * 4 + inner
                for part in range(2):
                    gg_all[b, :, part * 128 : part * 128 + 128] = turned[
                        pl.ds((part * batch + b) * (K + 1), K), :
                    ].astype(BF)
            return carry

        lax.fori_loop(0, batch // 4, pack_gg, 0)

    def weight_grads(first):
        def one(turns, carry):
            for inner in range(4):
                k = first + turns * 4 + inner
                wgrad = lax.dot_general(gram[k], slope_ref[...], TN, preferred_element_type=F32)
                for block in range(16):
                    for parity in range(2):
                        at = block * 16 + parity * 8
                        turned[
                            pl.ds(block * 8 * (2 * K + 1) + parity * K + k, 8, stride=2 * K + 1), :
                        ] = wgrad[at : at + 8]
            return carry

        lax.fori_loop(0, K // 8, one, 0)

    @pl.when(step == STEPS)
    def _():
        weight_copy_own.wait()
        for du, dv in blocks:
            from_sibling(du, dv).wait_recv()

        def product(turns, total):
            for inner in range(8):
                k = turns * 8 + inner
                total = total + jnp.dot(
                    gram[k], weight_ref[:, k].reshape(F, H), preferred_element_type=F32
                )
            return total

        preact = lax.fori_loop(0, K // 8, product, jnp.zeros((batch, H), F32))
        sig = jax.nn.sigmoid(preact)
        slope_ref[...] = (
            cot_ref[...].astype(F32) * sig * (1.0 + preact * (1.0 - sig))
        ).astype(BF)
        gram_grads()

    @pl.when(step >= STEPS)
    def _():
        def samples(turns, total):
            group = [turns * 4 + inner for inner in range(4)]
            xs = [matrix(b) for b in group]
            ggs = [gg_all[back * ROWS + b] for b in group]
            mgs = [
                jnp.dot(gg, xb, preferred_element_type=F32).astype(BF) for gg, xb in zip(ggs, xs)
            ]
            for mg, xb in zip(mgs, xs):
                total = total + lax.dot_general(mg, xb, NT, preferred_element_type=F32)
            for b, gg, mg in zip(group, ggs, mgs):
                left = jnp.concatenate([gg, projt_ref[...]], axis=0)
                right = jnp.concatenate([mixed_all[back * ROWS + b], mg], axis=0)
                fg = lax.dot_general(left, right, TN, preferred_element_type=F32) * SCALE
                fg = fg.reshape(16, 2, 8, 256)
                even = fg[:, 0].reshape(PAIRS, 256)
                odd = fg[:, 1].reshape(PAIRS, 256)
                r0 = pltpu.roll(odd[:, :128], 64, 1)
                r1 = pltpu.roll(odd[:, 128:], 64, 1)
                ready[pl.ds(b, PAIRS, stride=3 * PAD), :] = even[:, :128]
                ready[pl.ds(b + PAD, PAIRS, stride=3 * PAD), :] = jnp.where(low, even[:, 128:], r0)
                ready[pl.ds(b + 2 * PAD, PAIRS, stride=3 * PAD), :] = jnp.where(low, r0, r1)
            return total

        pg_ref[...] += lax.fori_loop(0, ROWS // 4, samples, jnp.zeros((K, F), F32)) * SCALE

        @pl.when(back >= SLOTS)
        def _():
            for copy in copies(back - SLOTS, slot):
                copy.wait_send()
            own_copy(back - SLOTS, slot).wait()

        def pack(q, carry):
            for kind in range(2):
                for last in range(4):
                    first, second = q // 4, q % 4
                    if kind == 0:
                        owner = ((first * 4 + second) * 4 + last) * 2
                    else:
                        owner = ((second * 4 + first) * 4 + last) * 2 + 1
                    for tile in range(3):
                        at = pl.ds((owner * 3 + tile) * PAD, ROWS)
                        stage[slot, kind * 64 + q * 4 + last, :, tile * 128 : tile * 128 + 128] = ready[
                            at, :
                        ].astype(BF)
            return carry

        lax.fori_loop(0, 16, pack, 0)
        for copy in copies(back, slot):
            copy.start()
        own_copy(back, slot).start()

    @pl.when(back == 0)
    def _():
        weight_grads(0)

    @pl.when(back == 1)
    def _():
        weight_grads(K // 2)

        def pack_wgrad(chip, carry):
            give[chip] = turned[
                pl.ds((chip * 2 + 1 - core) * (2 * K + 1), 2 * K), :
            ].astype(BF)
            return carry

        lax.fori_loop(0, 64, pack_wgrad, 0)
        weight_copy().start()

    @pl.when(back == 2)
    def _():
        weight_copy().wait_send()
        weight_copy().wait_recv()

        def pair_sum(n, carry):
            to_z, first, second = n // 16, (n // 4) % 4, n % 4
            chip = jnp.where(core == 0, first * 4 + second, second * 4 + first) * 4 + to_z
            mine = turned[pl.ds((chip * 2 + core) * (2 * K + 1), 2 * K), :]
            give[n] = (mine + other[chip].astype(F32)).astype(BF)
            return carry

        lax.fori_loop(0, 64, pair_sum, 0)
        for d in range(1, 4):
            weight_z(d).start()

    @pl.when(back == STEPS - 1)
    def _():
        for du, dv in blocks:
            to_sibling(du, dv).wait_send()
        for dv, dz in plane:
            for copy in segments_from(dv, dz):
                copy.wait_recv()
            for copy in segments_to(dv, dz):
                copy.wait_send()
        for d in range(1, 4):
            along_u(d).wait_send()
            for du in range(4):
                along_v(d, du).wait_send()
        for copy in segments_own():
            copy.wait()
        for ago in range(SLOTS):
            sent, where = back - ago, lax.rem(slot + SLOTS - ago, SLOTS)
            for copy in copies(sent, where):
                copy.wait_send()
            own_copy(sent, where).wait()
        for d in range(1, 4):
            weight_z(d).wait_recv()

        def sum_z(n, carry):
            total = give[z * 16 + n].astype(F32) + w2_in[0, n].astype(F32)
            total = total + (w2_in[1, n].astype(F32) + w2_in[2, n].astype(F32))
            wz_ref[n] = total.astype(BF)
            return carry

        lax.fori_loop(0, 16, sum_z, 0)
        for d in range(1, 4):
            weight_z(d).wait_send()

        def arrived(block, carry):
            def wait(sender, sem):
                at = pl.ds(sender * 128 + block * ROWS, ROWS)
                pltpu.make_async_remote_copy(
                    src_ref=stage.at[0, pl.ds(0, 16)],
                    dst_ref=rows_ref.at[:, at],
                    send_sem=send_sem.at[0, 0],
                    recv_sem=recv_sem.at[block, sem],
                    device_id=sibling,
                    device_id_type=MESH,
                ).wait_recv()

            wait(line * 2 + 1 - core, 0)
            for d in range(1, 4):
                for other in range(2):
                    wait(lax.rem(line + 4 - d, 4) * 2 + other, d * 2 + other)
            return carry

        lax.fori_loop(0, STEPS, arrived, 0)


def main(x, projt, own, cut, cot):
    batch = x.shape[0]
    any_space = pl.BlockSpec(memory_space=pl.ANY)
    dma = pltpu.SemaphoreType.DMA
    return pl.pallas_call(
        main_kernel,
        grid=(2 * STEPS,),
        in_specs=[
            pl.BlockSpec((ROWS, F * E), lambda i: (lax.rem(i, STEPS), 0)),
            pl.BlockSpec((K, F), lambda i: (0, 0)),
            any_space,
            any_space,
            pl.BlockSpec((batch, H), lambda i: (0, 0)),
        ],
        out_specs=[
            pl.BlockSpec((K, F), lambda i: (0, 0)),
            any_space,
            pl.BlockSpec((16, 2 * K, H), lambda i: (0, 0, 0)),
            any_space,
        ],
        out_shape=[
            jax.ShapeDtypeStruct((K, F), F32),
            jax.ShapeDtypeStruct((16, 8 * batch, 2 * E), BF),
            jax.ShapeDtypeStruct((16, 2 * K, H), BF),
            jax.ShapeDtypeStruct((16, 2, 8 * batch), jnp.int32),
        ],
        scratch_shapes=[
            pltpu.VMEM((K, F), BF),
            pltpu.VMEM((F * E // 128 * ROWS, 128), F32),
            pltpu.VMEM((3 * PAIRS * PAD, 128), F32),
            pltpu.VMEM((batch, K, 256), BF),
            pltpu.VMEM((K, batch, F), BF),
            pltpu.VMEM((16,) + own.shape, BF),
            pltpu.VMEM((batch, H), BF),
            pltpu.VMEM((batch, K, F), BF),
            pltpu.VMEM((2 * batch * (K + 1), H), F32),
            pltpu.VMEM((SLOTS, PAIRS, ROWS, 2 * E), BF),
            pltpu.VMEM((64, 2 * K, H), BF),
            pltpu.VMEM((64, 2 * K, H), BF),
            pltpu.VMEM((3, 16, 2 * K, H), BF),
            dma((3,)),
            dma((3,)),
            dma((3, 4)),
            dma((3, 4)),
            dma((4, 4)),
            dma((4, 4)),
            dma((4, 4, 4)),
            dma((4, 4, 4)),
            dma((1,)),
            dma((SLOTS, 7)),
            dma((STEPS, 8)),
            dma((SLOTS,)),
            dma((2,)),
            dma((3,)),
            dma((3,)),
        ],
        compiler_params=pltpu.CompilerParams(
            vmem_limit_bytes=VMEM_LIMIT, collective_id=1, has_side_effects=True
        ),
        cost_estimate=pl.CostEstimate(
            flops=18 * batch * F * E * K, bytes_accessed=60_000_000, transcendentals=batch * H
        ),
        name="main",
    )(x, projt, own, cut, cot)


SLOT_BLOCK = 256
HALF = UNIQUE_CAP // 2
FIRST = 128
ORDER = (1, 2, 3, 0)


def sums_kernel(
    rows_ref, seg_ref, wz_ref, pg_ref,
    wout_ref, pout_ref, out_ref,
    data, table, az, bv, sum_a, sum_b, va, zb, w3_in, w4, w4_in, pu, pv, pz, pc,
    load_sem, az_send, az_recv, bv_send, bv_recv, va_send, va_recv, zb_send, zb_recv,
    w_send, w_recv, p_send, p_recv,
):
    x, y, z, core = place()
    u = jnp.where(core == 0, x, y)
    v = jnp.where(core == 0, y, x)
    low = lower_half(SLOT_BLOCK)

    def at_u(d):
        moved = turn(u, d)
        return device(jnp.where(core == 0, moved, x), jnp.where(core == 0, y, moved), z, core)

    def at_v(d):
        moved = turn(v, d)
        return device(jnp.where(core == 0, x, moved), jnp.where(core == 0, moved, y), z, core)

    def at_z(d):
        return device(x, y, turn(z, d), core)

    sibling = device(x, y, z, 1 - core)

    def load(dz, dv):
        j = turn(v, dv) * 4 + turn(z, dz)
        return pltpu.make_async_copy(rows_ref.at[j], data.at[dz, dv], load_sem.at[dz, dv])

    for dz in ORDER:
        for dv in ORDER:
            load(dz, dv).start()

    greet([to(d) for d in range(1, 4) for to in (at_u, at_v, at_z)] + [sibling])

    def spread(buffer, mine, stage, to):
        return [
            remote(buffer.at[mine], buffer.at[mine], p_send.at[stage, d - 1], p_recv.at[stage, d - 1], to(d))
            for d in range(1, 4)
        ]

    def gathered(buffer, mine, stage, to):
        for d in range(1, 4):
            there = buffer.at[turn(mine, -d)]
            remote(there, there, p_send.at[stage, d - 1], p_recv.at[stage, d - 1], to(d)).wait_recv()
        return (buffer[0] + buffer[1]) + (buffer[2] + buffer[3])

    def start(copies):
        for copy in copies:
            copy.start()
        return copies

    def send_a(dz, dv):
        return remote(
            table.at[dz, dv, pl.ds(0, FIRST)],
            az.at[dz - 1, dv],
            az_send.at[dz - 1, dv],
            az_recv.at[dz - 1, dv],
            at_z(dz),
        )

    def send_b(dv, dz):
        return remote(
            table.at[dz, dv, pl.ds(FIRST, HALF - FIRST)],
            bv.at[dv - 1, dz],
            bv_send.at[dv - 1, dz],
            bv_recv.at[dv - 1, dz],
            at_v(dv),
        )

    def second_a(dv):
        return remote(sum_a.at[dv], va.at[dv - 1], va_send.at[dv - 1], va_recv.at[dv - 1], at_v(dv))

    def second_b(dz):
        return remote(sum_b.at[dz], zb.at[dz - 1], zb_send.at[dz - 1], zb_recv.at[dz - 1], at_z(dz))

    def one_table(dz, dv):
        load(dz, dv).wait()
        j = turn(v, dv) * 4 + turn(z, dz)
        slot = lax.broadcasted_iota(jnp.int32, (SLOT_BLOCK, 8 * 128), 0)

        def part(block, parity):
            seg = seg_ref[j, parity : parity + 1, :] - block * SLOT_BLOCK
            hot = jnp.where(slot == seg, 1.0, 0.0).astype(BF)
            found = jnp.dot(
                hot, data[dz, dv, :, parity * 128 : parity * 128 + 256], preferred_element_type=F32
            )
            return found[:, :128], found[:, 128:]

        for block in range(HALF // SLOT_BLOCK):
            at = pl.ds(block * SLOT_BLOCK, SLOT_BLOCK)
            even0, even1 = part(block, 0)
            odd0, odd1 = part(block, 1)
            r0 = pltpu.roll(odd0, 64, 1)
            r1 = pltpu.roll(odd1, 64, 1)
            table[dz, dv, at, 0:128] = (even0 + jnp.where(low, r0, r1)).astype(BF)
            first = even1 + r1
            even0, even1 = part(block + HALF // SLOT_BLOCK, 0)
            odd0, odd1 = part(block + HALF // SLOT_BLOCK, 1)
            r0 = pltpu.roll(even0, 64, 1)
            r1 = pltpu.roll(even1, 64, 1)
            table[dz, dv, at, 128:256] = jnp.where(low, first, r0 + odd0).astype(BF)
            table[dz, dv, at, 256:384] = (jnp.where(low, r0, r1) + odd1).astype(BF)

    def tables(dz):
        def one(turns, carry):
            dv = lax.rem(turns + 1, 4)
            one_table(dz, dv)
            if dz > 0:
                send_a(dz, dv).start()

            @pl.when(dv > 0)
            def _():
                send_b(dv, dz).start()

            return carry

        lax.fori_loop(0, 4, one, 0)

    def add_four(first, second, third, fourth, target, size):
        rows = first.shape[0]

        def one(n, carry):
            at = pl.ds(pl.multiple_of(n * size, size), size)
            total = (first[at].astype(F32) + second[at].astype(F32)) + (
                third[at].astype(F32) + fourth[at].astype(F32)
            )
            target[at] = total.astype(target.dtype)
            return carry

        lax.fori_loop(0, rows // size, one, 0)

    def total_b(dz):
        for dv in range(1, 4):
            send_b(dv, dz).wait_recv()
        mine = table.at[dz, 0, pl.ds(FIRST, HALF - FIRST)]
        add_four(mine, bv.at[0, dz], bv.at[1, dz], bv.at[2, dz], sum_b.at[dz], 64)
        if dz > 0:
            second_b(dz).start()

    def total_a(dv):
        for dz in range(1, 4):
            send_a(dz, dv).wait_recv()
        mine = table.at[0, dv, pl.ds(0, FIRST)]
        add_four(mine, az.at[0, dv], az.at[1, dv], az.at[2, dv], sum_a.at[dv], 64)
        if dv > 0:
            second_a(dv).start()

    def w_copies(source, arrive, stage, to, line, size):
        return [
            remote(
                source.at[pl.ds(turn(line, d) * size, size)],
                arrive.at[d - 1],
                w_send.at[stage, d - 1],
                w_recv.at[stage, d - 1],
                to(d),
            )
            for d in range(1, 4)
        ]

    pu[u] = pg_ref[...]
    p0 = start(spread(pu, u, 0, at_u))
    s3 = start(w_copies(wz_ref, w3_in, 0, at_u, u, 4))
    tables(1)
    tables(2)
    total_b(1)
    pv[v] = gathered(pu, u, 0, at_u)
    p1 = start(spread(pv, v, 1, at_v))
    for copy in s3:
        copy.wait_recv()
    add_four(wz_ref.at[pl.ds(u * 4, 4)], w3_in.at[0], w3_in.at[1], w3_in.at[2], w4, 1)
    s4 = start(w_copies(w4, w4_in, 1, at_v, v, 1))
    tables(3)
    total_b(2)
    pz[z] = gathered(pv, v, 1, at_v)
    p2 = start(spread(pz, z, 2, at_z))
    tables(0)
    total_b(3)
    for dv in ORDER:
        total_a(dv)
    pc[core] = gathered(pz, z, 2, at_z)
    p3 = remote(pc.at[core], pc.at[core], p_send.at[3, 0], p_recv.at[3, 0], sibling)
    p3.start()
    for copy in s4:
        copy.wait_recv()
    total = w4[v].astype(F32) + w4_in[0, 0].astype(F32)
    wout_ref[...] = total + (w4_in[1, 0].astype(F32) + w4_in[2, 0].astype(F32))
    total_b(0)
    remote(pc.at[1 - core], pc.at[1 - core], p_send.at[3, 0], p_recv.at[3, 0], sibling).wait_recv()
    pout_ref[...] = lax.dot_general(
        pc[0] + pc[1],
        reorder(F32),
        NT,
        precision=lax.Precision.HIGHEST,
        preferred_element_type=F32,
    )

    def finish(mine, others, start_row, rows):
        def one(part, carry):
            at = pl.ds(pl.multiple_of(part * 128, 128), 128)
            before = pl.ds(pl.multiple_of(part * 128 + start_row, 128), 128)
            after = pl.ds(pl.multiple_of(part * 128 + start_row + HALF, 128), 128)
            total = mine[at, :].astype(F32) + others[0, at].astype(F32)
            total = total + (others[1, at].astype(F32) + others[2, at].astype(F32))
            r1 = pltpu.roll(total[:, 128:256], 64, 1)
            r2 = pltpu.roll(total[:, 256:], 64, 1)
            out_ref[:128, before] = total[:, :128].T
            out_ref[128:, before] = total[:, 128:256].T[:64]
            out_ref[:128, after] = jnp.where(lower_half(128), r1, r2).T
            out_ref[128:, after] = r2.T[:64]
            return carry

        lax.fori_loop(0, rows // 128, one, 0)

    for d in range(1, 4):
        second_a(d).wait_recv()
    finish(sum_a.at[0], va, 0, FIRST)
    for d in range(1, 4):
        second_b(d).wait_recv()
    finish(sum_b.at[0], zb, FIRST, HALF - FIRST)

    for copy in p0 + p1 + p2 + [p3] + s3 + s4:
        copy.wait_send()
    for d in range(1, 4):
        second_a(d).wait_send()
        second_b(d).wait_send()
        for n in range(4):
            send_a(d, n).wait_send()
            send_b(d, n).wait_send()


def sums(rows, seg, wz, pg):
    any_space = pl.BlockSpec(memory_space=pl.ANY)
    whole = pl.BlockSpec(memory_space=pltpu.VMEM)
    dma = pltpu.SemaphoreType.DMA
    rest = HALF - FIRST
    return pl.pallas_call(
        sums_kernel,
        in_specs=[any_space, whole, whole, whole],
        out_specs=[whole] * 3,
        out_shape=[
            jax.ShapeDtypeStruct((2 * K, H), F32),
            jax.ShapeDtypeStruct((K, F), F32),
            jax.ShapeDtypeStruct((E, UNIQUE_CAP), F32),
        ],
        scratch_shapes=[
            pltpu.VMEM((4, 4) + rows.shape[1:], BF),
            pltpu.VMEM((4, 4, HALF, 2 * E), BF),
            pltpu.VMEM((3, 4, FIRST, 2 * E), BF),
            pltpu.VMEM((3, 4, rest, 2 * E), BF),
            pltpu.VMEM((4, FIRST, 2 * E), BF),
            pltpu.VMEM((4, rest, 2 * E), BF),
            pltpu.VMEM((3, FIRST, 2 * E), BF),
            pltpu.VMEM((3, rest, 2 * E), BF),
            pltpu.VMEM((3, 4, 2 * K, H), BF),
            pltpu.VMEM((4, 2 * K, H), BF),
            pltpu.VMEM((3, 1, 2 * K, H), BF),
            pltpu.VMEM((4, K, F), F32),
            pltpu.VMEM((4, K, F), F32),
            pltpu.VMEM((4, K, F), F32),
            pltpu.VMEM((2, K, F), F32),
            dma((4, 4)),
            dma((3, 4)),
            dma((3, 4)),
            dma((3, 4)),
            dma((3, 4)),
            dma((3,)),
            dma((3,)),
            dma((3,)),
            dma((3,)),
            dma((2, 3)),
            dma((2, 3)),
            dma((4, 3)),
            dma((4, 3)),
        ],
        compiler_params=pltpu.CompilerParams(
            vmem_limit_bytes=VMEM_LIMIT, collective_id=2, has_side_effects=True
        ),
        cost_estimate=pl.CostEstimate(
            flops=16 * 4 * UNIQUE_CAP * 1024 * 256, bytes_accessed=30_000_000, transcendentals=0
        ),
        name="sums",
    )(rows, seg, wz, pg)


def finish_kernel(w_ref, p_ref, r_ref, wout_ref, pout_ref, rout_ref):
    wout_ref[...] = w_ref[...]
    pout_ref[...] = p_ref[...]
    rout_ref[...] = r_ref[...]


def finish(*results):
    whole = pl.BlockSpec(memory_space=pltpu.VMEM)
    return pl.pallas_call(
        finish_kernel,
        in_specs=[whole] * 3,
        out_specs=[whole] * 3,
        out_shape=[jax.ShapeDtypeStruct(a.shape, a.dtype) for a in results],
        name="finish",
    )(*results)


def turn_features(a):
    rest = a.shape[1:]
    return a.reshape((-1, 8, 2) + rest).swapaxes(1, 2).reshape(a.shape)


def on_device(pooled, projection, out_weight, cotangent, segments):
    own = turn_features(out_weight.reshape(-1, K, H)).swapaxes(0, 1)
    pg, rows, wz, seg = main(pooled, projection.T, own, segments.T, cotangent)
    weight_grad, pg, row_grad = finish(*sums(rows, seg, wz, pg))
    return (weight_grad, pg.T, row_grad.T)


def solution(mesh):
    placed = (
        P(("fsdp", "emb"), None),
        P(),
        P("fsdp", None),
        P(("fsdp", "emb"), None),
        P(None, ("fsdp", "emb")),
    )
    return jax.shard_map(
        on_device,
        mesh=mesh,
        in_specs=placed,
        out_specs=(P(("fsdp", "emb"), None), P(), P(("fsdp", "emb"), None)),
        check_vma=False,
    )
```
